32 devices in a mesh: head: 2 (over x), inner: 4 (over y, core), outer: 4 (over z).
Axes of the slice: x: 2, y: 2, z: 4, core: 2. Of those that a mesh axis runs over, the one named last changes fastest.
Arguments:
- query: bfloat16 [2048, 4096], P(('outer', 'inner', 'head')), may hold values from -80 to 80
- key: bfloat16 [2048, 1024], P(('outer', 'inner', 'head')), may hold values from -6 to 6
- value: bfloat16 [2048, 1024], P(('outer', 'inner', 'head')), may hold values from -6 to 6
- doc_lengths: int32 [24], replicated, may hold values from 1 to 512, 2048 in all
- resid: bfloat16 [2048, 4096], P('outer', 'inner'), may hold values from -20 to 20
- norm_gain: float32 [4096], P('inner'), may hold values from 0.1 to 1.9
- w_out: bfloat16 [4096, 4096], P('head', ('inner', 'outer')), may hold values from -0.09375 to 0.09375
- w_gate_up: bfloat16 [2, 4096, 7168], P(None, ('inner', 'outer'), 'head'), may hold values from -0.09375 to 0.09375
- w_down: bfloat16 [7168, 4096], P('head', ('inner', 'outer')), may hold values from -0.0625 to 0.0625
Outputs:
- context: bfloat16 [2048, 4096], P(('outer', 'inner'), 'head')
- layer_out: bfloat16 [2048, 4096], P(('outer', 'head'), 'inner')
The draws below stay inside these ranges and needn't reach their ends.
Inputs may be any that keep to these rules, and one draw needn't show every extreme that they name: `doc_lengths`: the 24 lengths sum to 2048, and the longest is exactly 512.
All inputs are finite; a program needn't handle non-finite values.
Results may differ from the reference program's by a relative error of at most 0.03.
Values may be sent and summed in bfloat16 or wider, within the bound.
No kernel may reach another device: no remote copies, remote signals or barrier semaphores. Data moves between devices by JAX's collectives and lax.ppermute only.
A program may use at most 128 MiB of HBM per device.

```python
import math
import jax
import jax.numpy as jnp
import numpy as np
from jax import lax

D = 4096
QUERY_HEADS = 32
KEY_VALUE_HEADS = 8
HEAD_WIDTH = 128
FF = 7168
SEQUENCE_BLOCK = 128
DOCS = 24
WINDOW_LENGTH = 2048
DOC_MOST = 512
N_HEAD = 2
N_INNER = 4


def shared_keys(key):
    return jnp.clip(jax.random.normal(key, (WINDOW_LENGTH, KEY_VALUE_HEADS * HEAD_WIDTH), jnp.float32), -4.0, 4.0)


def draw_key(key, part):
    base_offset = shared_keys(key)
    return base_offset.astype(jnp.bfloat16)


def draw_query(key, part):
    key = jax.random.fold_in(key, 1)
    own_rows = jnp.clip(jax.random.normal(key, (WINDOW_LENGTH, QUERY_HEADS * HEAD_WIDTH), jnp.float32), -4.0, 4.0)
    return own_rows.astype(jnp.bfloat16)


def draw_resid(key, part):
    key = jax.random.fold_in(key, 3)
    noise_key, column_key, row_key = jax.random.split(key, 3)
    column_place = jnp.arange(D, dtype=jnp.float32)[None, :] / (D - 1)
    rough = jax.random.uniform(column_key, (1, D), jnp.float32, -0.5, 0.5)
    row_scale = jnp.exp(jax.random.uniform(row_key, (WINDOW_LENGTH, 1), jnp.float32, -1.6, 0.7))
    column_scale = jnp.exp(1.1 * (column_place - 1.0) + rough)
    field = jnp.clip(jax.random.normal(noise_key, (WINDOW_LENGTH, D), jnp.float32), -4.0, 4.0)
    return (field * column_scale * row_scale).astype(jnp.bfloat16)


def levels(stream_key, extent, cuts, low, top_value):
    level, own = 1.0, jax.random.fold_in(stream_key, 6)
    for position, shards_of in cuts:
        heights = jnp.exp(jax.random.uniform(jax.random.fold_in(own, position), (shards_of,), jnp.float32, low / len(cuts), top_value / len(cuts)))
        level = level * jnp.repeat(heights, extent[position] // shards_of).reshape([-1 if axis == position else 1 for axis in range(len(extent))])
    return level


def profile(number_of, total, limit, lean):
    weights = [(1 << 20) // math.isqrt(grade ** lean) + 1 for grade in range(2, number_of + 1)]
    surplus, counts = total - limit - (number_of - 1), [1] * (number_of - 1)
    while surplus > 0:
        free = [i for i in range(number_of - 1) if counts[i] < limit]
        mass, left = sum([weights[i] for i in free]), surplus
        for i in free:
            extra = min(limit - counts[i], max(1, left * weights[i] // mass), surplus)
            counts[i] = counts[i] + extra
            surplus = surplus - extra
    return np.array([limit] + counts)


def uneven(own_key, number_of, total, reach, lean):
    if number_of == 2:
        one = jax.random.randint(own_key, (), max(1, total - reach), min(reach, total - 1) + 1)
        return jnp.stack([one, total - one])
    tallies = jnp.asarray(profile(number_of, total, reach, lean), jnp.int32)
    pairs = (number_of - 1) // 2
    source_of, sink = tallies[1:1 + 2 * pairs:2], tallies[2:2 + 2 * pairs:2]
    room = jnp.minimum(source_of - 1, reach - sink)
    passed = jax.random.randint(jax.random.fold_in(own_key, 1), (pairs,), 0, 1 << 20) % (room + 1)
    tallies = tallies.at[1:1 + 2 * pairs:2].set(source_of - passed).at[2:2 + 2 * pairs:2].set(sink + passed)
    return tallies[jax.random.permutation(jax.random.fold_in(own_key, 2), number_of)]


def gaussian(own_key, extent, scale, most, cuts=(), kind=jnp.bfloat16):
    array = scale * jax.random.normal(own_key, extent, jnp.float32)
    if cuts:
        array = array * levels(own_key, extent, cuts, -0.22, 0.18)
    return jnp.clip(array, -most, most).astype(kind)


def setup_inputs(seed: int = 0) -> dict:
    streams_of = jax.random.split(jax.random.key(seed), 10)
    return {
        "query": draw_query(jax.random.fold_in(streams_of[9], 71), 0),
        "key": draw_key(jax.random.fold_in(streams_of[9], 71), 0),
        "value": gaussian(streams_of[2], (WINDOW_LENGTH, KEY_VALUE_HEADS * HEAD_WIDTH), 1.0, 6.0, ((0, 32),)),
        "doc_lengths": uneven(streams_of[3], DOCS, WINDOW_LENGTH, DOC_MOST, 2).astype(jnp.int32),
        "resid": draw_resid(jax.random.fold_in(streams_of[9], 71), 0),
        "norm_gain": jnp.clip(1.0 + 0.18 * jax.random.normal(streams_of[5], (D,), jnp.float32), 0.1, 1.9),
        "w_out": gaussian(streams_of[6], (QUERY_HEADS * HEAD_WIDTH, D), (QUERY_HEADS * HEAD_WIDTH) ** -0.5, 0.09375, ((0, 2), (1, 16))),
        "w_gate_up": gaussian(streams_of[7], (2, D, FF), D ** -0.5, 0.09375, ((1, 16), (2, 2))),
        "w_down": gaussian(streams_of[8], (FF, D), FF ** -0.5, 0.0625, ((0, 2), (1, 16))),
    }


def segment_ids(positions, doc_lengths):
    bounds = jnp.cumsum(doc_lengths).astype(jnp.int32)
    return lax.optimization_barrier(jnp.sum((bounds[None, :] <= positions[:, None]).astype(jnp.int32), axis=1)).astype(jnp.int32)

def rounded_back(values):
    return lax.optimization_barrier(values.astype(jnp.bfloat16)).astype(jnp.float32)

def reference(query, key, value, doc_lengths, resid, norm_gain, w_out, w_gate_up, w_down):
    group_width = QUERY_HEADS // KEY_VALUE_HEADS
    score_scale = HEAD_WIDTH ** (-0.5)
    positions = jnp.arange(WINDOW_LENGTH, dtype=jnp.int32)
    all_segments = segment_ids(positions, doc_lengths)
    expanded_keys = key.astype(jnp.float32).reshape(WINDOW_LENGTH, KEY_VALUE_HEADS, HEAD_WIDTH)
    expanded_values = value.astype(jnp.float32).reshape(WINDOW_LENGTH, KEY_VALUE_HEADS, HEAD_WIDTH)

    def query_block(block_index):
        anchor = (block_index * SEQUENCE_BLOCK).astype(jnp.int32)
        query_matrix = lax.dynamic_slice_in_dim(query, anchor, SEQUENCE_BLOCK, 0).astype(jnp.float32)
        query_matrix = query_matrix.reshape(SEQUENCE_BLOCK, KEY_VALUE_HEADS, group_width, HEAD_WIDTH)
        scores = jnp.einsum('qkgd,nkd->kgqn', query_matrix, expanded_keys) * score_scale
        query_place = anchor + jnp.arange(SEQUENCE_BLOCK, dtype=jnp.int32)
        query_segment = lax.dynamic_slice_in_dim(all_segments, anchor, SEQUENCE_BLOCK, 0)
        allowed = (positions[None, :] <= query_place[:, None]) & (all_segments[None, :] == query_segment[:, None])
        masked = jnp.where(allowed, scores, -1e+30)
        row_max = lax.optimization_barrier(jnp.max(masked, axis=-1, keepdims=True))
        exp_scores = jnp.where(allowed, jnp.exp(masked - row_max), 0.0)
        totals = lax.optimization_barrier(jnp.sum(exp_scores, axis=-1))
        summed = jnp.einsum('kgqn,nkd->kgqd', rounded_back(exp_scores), expanded_values)
        result = summed / totals[..., None]
        return jnp.transpose(result, (2, 0, 1, 3)).reshape(SEQUENCE_BLOCK, QUERY_HEADS * HEAD_WIDTH).astype(jnp.bfloat16)
    context = lax.map(query_block, jnp.arange(WINDOW_LENGTH // SEQUENCE_BLOCK, dtype=jnp.int32)).reshape(WINDOW_LENGTH, QUERY_HEADS * HEAD_WIDTH)
    head_cols = QUERY_HEADS * HEAD_WIDTH // N_HEAD
    projected = jnp.zeros((WINDOW_LENGTH, D), jnp.float32)
    for head_group in range(N_HEAD):
        lower = head_group * head_cols
        product = jnp.dot(context[:, lower:lower + head_cols], w_out[lower:lower + head_cols, :], preferred_element_type=jnp.float32)
        projected = projected + rounded_back(product)
    hidden_state = (resid.astype(jnp.float32) + projected).astype(jnp.bfloat16)
    state_wide = lax.optimization_barrier(hidden_state).astype(jnp.float32)
    mean_square = lax.optimization_barrier(jnp.mean(state_wide * state_wide, axis=1, keepdims=True))
    normed = (state_wide * lax.rsqrt(mean_square + 1e-05) * norm_gain[None, :]).astype(jnp.bfloat16)
    feature_cols = D // N_INNER
    gate_sum = jnp.zeros((WINDOW_LENGTH, FF), jnp.float32)
    up_sum = jnp.zeros((WINDOW_LENGTH, FF), jnp.float32)
    for inner_block in range(N_INNER):
        lower = inner_block * feature_cols
        normed_part = normed[:, lower:lower + feature_cols]
        gate_sum = gate_sum + rounded_back(jnp.dot(normed_part, w_gate_up[0, lower:lower + feature_cols, :], preferred_element_type=jnp.float32))
        up_sum = up_sum + rounded_back(jnp.dot(normed_part, w_gate_up[1, lower:lower + feature_cols, :], preferred_element_type=jnp.float32))
    activated = (jax.nn.silu(gate_sum) * up_sum).astype(jnp.bfloat16)
    hidden_cols = FF // N_HEAD
    down_sum = jnp.zeros((WINDOW_LENGTH, D), jnp.float32)
    for head_group in range(N_HEAD):
        lower = head_group * hidden_cols
        product = jnp.dot(activated[:, lower:lower + hidden_cols], w_down[lower:lower + hidden_cols, :], preferred_element_type=jnp.float32)
        down_sum = down_sum + rounded_back(product)
    layer_out = (state_wide + down_sum).astype(jnp.bfloat16)
    return (context, layer_out)
```

```python
import functools

import jax
import jax.numpy as jnp
from jax import lax
from jax.experimental import pallas as pl
from jax.experimental.pallas import tpu as pltpu
from jax.sharding import PartitionSpec as P

D = 4096
QUERY_HEADS = 32
KEY_VALUE_HEADS = 8
HEAD_WIDTH = 128
GROUP = QUERY_HEADS // KEY_VALUE_HEADS
WINDOW_PER_DOC = 4
QUERY_TILE = 128


def swap(array, axis, distance):
    count = lax.axis_size(axis)
    return lax.ppermute(array, axis, [(s, s ^ distance) for s in range(count)])


def attention_kernel(halo_rows, reach, starts_ref, queries_ref, own_ref, halo_ref, out_ref, keys, values):
    tile = pl.program_id(0)
    rows = queries_ref.shape[0]
    span = reach + rows

    @pl.when(tile == 0)
    def _():
        keys[:halo_rows, :] = halo_ref[:, :HEAD_WIDTH]
        values[:halo_rows, :] = halo_ref[:, HEAD_WIDTH:]
        keys[halo_rows:, :] = own_ref[:, :HEAD_WIDTH]
        values[halo_rows:, :] = own_ref[:, HEAD_WIDTH:]

    first = pl.multiple_of(tile * rows + (halo_rows - reach), rows)
    near_keys = keys[pl.ds(first, span), :]
    near_values = values[pl.ds(first, span), :]
    key_place = lax.broadcasted_iota(jnp.int32, (rows, span), 1)
    query_place = lax.broadcasted_iota(jnp.int32, (rows, span), 0) + reach
    start = starts_ref[...] - (first - halo_rows)
    allowed = (key_place <= query_place) & (key_place >= start)
    for g in range(GROUP):
        cols = slice(g * HEAD_WIDTH, (g + 1) * HEAD_WIDTH)
        scores = lax.dot_general(
            queries_ref[:, cols], near_keys, (((1,), (1,)), ((), ())), preferred_element_type=jnp.float32
        ) * (HEAD_WIDTH ** (-0.5))
        masked = jnp.where(allowed, scores, -1e30)
        row_max = jnp.max(masked, axis=1, keepdims=True)
        weights = jnp.exp(masked - row_max)
        totals = jnp.sum(weights, axis=1, keepdims=True)
        summed = jnp.dot(weights.astype(jnp.bfloat16), near_values, preferred_element_type=jnp.float32)
        out_ref[:, cols] = (summed / totals).astype(jnp.bfloat16)


def attention(packed, halo, starts, reach):
    rows = packed.shape[0]
    halo_rows = halo.shape[0]
    q_cols = GROUP * HEAD_WIDTH
    kv_cols = 2 * HEAD_WIDTH
    return pl.pallas_call(
        functools.partial(attention_kernel, halo_rows, reach),
        grid=(rows // QUERY_TILE,),
        in_specs=[
            pl.BlockSpec((QUERY_TILE, 1), lambda t: (t, 0)),
            pl.BlockSpec((QUERY_TILE, q_cols), lambda t: (t, 0)),
            pl.BlockSpec((rows, kv_cols), lambda t: (0, q_cols // kv_cols)),
            pl.BlockSpec((halo_rows, kv_cols), lambda t: (0, 0)),
        ],
        out_specs=pl.BlockSpec((QUERY_TILE, q_cols), lambda t: (t, 0)),
        out_shape=jax.ShapeDtypeStruct((rows, q_cols), jnp.bfloat16),
        scratch_shapes=[
            pltpu.VMEM((halo_rows + rows, HEAD_WIDTH), jnp.bfloat16),
            pltpu.VMEM((halo_rows + rows, HEAD_WIDTH), jnp.bfloat16),
        ],
        compiler_params=pltpu.CompilerParams(vmem_limit_bytes=32 * 1024 * 1024),
        cost_estimate=pl.CostEstimate(
            flops=4 * rows * (reach + QUERY_TILE) * q_cols,
            bytes_accessed=rows * 4 * q_cols,
            transcendentals=rows * (reach + QUERY_TILE) * GROUP,
        ),
    )(starts, packed, packed, halo)


def earlier_planes(kv, hops):
    count = lax.axis_size("outer")
    moved = [lax.ppermute(kv, "outer", [(s, s + d) for s in range(count - d)]) for d in range(hops, 0, -1)]
    return jnp.concatenate(moved, axis=0)


def document_starts(bounds, first, rows):
    place = first + jnp.arange(rows, dtype=jnp.int32)
    starts = jnp.max(jnp.where(bounds[None, :] <= place[:, None], bounds[None, :], 0), axis=1) - first
    return starts[:, None].astype(jnp.int32)


def per_device(query, key, value, doc_lengths, resid, norm_gain, w_out, w_gate_up, w_down):
    inner_count = lax.axis_size("inner")
    outer_count = lax.axis_size("outer")
    head_count = lax.axis_size("head")
    outer, inner, head = lax.axis_index("outer"), lax.axis_index("inner"), lax.axis_index("head")
    rows = query.shape[0]
    plane_rows = rows * inner_count * head_count
    reach = plane_rows * outer_count // WINDOW_PER_DOC
    feature_rows = w_gate_up.shape[1]
    hidden_cols = w_gate_up.shape[2] // outer_count

    weights_out = lax.all_gather(w_out, "outer", axis=1, tiled=True)
    bounds = jnp.cumsum(doc_lengths)
    hops = reach // plane_rows
    token_rows = plane_rows // inner_count
    packing = (head_count, KEY_VALUE_HEADS // head_count)
    groups = jnp.concatenate(
        [
            query.reshape(rows, *packing, GROUP * HEAD_WIDTH),
            key.reshape(rows, *packing, HEAD_WIDTH),
            value.reshape(rows, *packing, HEAD_WIDTH),
        ],
        axis=3,
    )
    q_cols = GROUP * HEAD_WIDTH
    if packing[1] == inner_count:
        groups = jnp.transpose(groups, (2, 1, 0, 3)).reshape(inner_count * head_count, rows, -1)
        packed = lax.all_to_all(groups, ("inner", "head"), split_axis=0, concat_axis=0, tiled=True)
        packed = packed.reshape(plane_rows, -1)
        halo = earlier_planes(packed[:, q_cols:], hops)
        starts = document_starts(bounds, outer * plane_rows, plane_rows)
        own_context = attention(packed, halo, starts, reach)
        across = swap(own_context, "inner", 2)
        parts = [own_context, swap(own_context, "inner", 1), across, swap(across, "inner", 1)]
        plane_context = jnp.zeros((plane_rows, inner_count * q_cols), jnp.bfloat16)
        for d, part in enumerate(parts):
            plane_context = lax.dynamic_update_slice(plane_context, part, (0, (inner ^ d) * q_cols))
        context = lax.dynamic_slice_in_dim(plane_context, inner * token_rows, token_rows, 0)
    else:
        groups = jnp.transpose(groups[:, :, 0], (1, 0, 2))
        packed = lax.all_to_all(groups, "head", split_axis=0, concat_axis=0, tiled=True).reshape(token_rows, -1)
        plane_kv = lax.all_gather(packed[:, q_cols:], "inner", axis=0, tiled=True)
        every_kv = jnp.concatenate([earlier_planes(plane_kv, hops), plane_kv], axis=0)
        halo = lax.dynamic_slice_in_dim(every_kv, inner * token_rows, reach, 0)
        starts = document_starts(bounds, outer * plane_rows + inner * token_rows, token_rows)
        context = attention(packed, halo, starts, reach)
        plane_context = lax.all_gather(context, "inner", axis=0, tiled=True)

    half = plane_rows // head_count
    partial_proj = jnp.dot(plane_context, weights_out, preferred_element_type=jnp.float32).astype(jnp.bfloat16)
    projected = lax.dynamic_slice_in_dim(partial_proj, head * half, half, 0).astype(jnp.float32)
    for e in range(1, head_count):
        sent = lax.dynamic_slice_in_dim(partial_proj, (head ^ e) * half, half, 0)
        projected = projected + swap(sent, "head", e).astype(jnp.float32)
    own_resid = lax.dynamic_slice_in_dim(resid, head * half, half, 0)
    hidden_part = (own_resid.astype(jnp.float32) + projected).astype(jnp.bfloat16)
    hidden_state = lax.all_to_all(hidden_part, "inner", split_axis=0, concat_axis=1, tiled=True)
    gain = lax.all_gather(norm_gain, "inner", axis=0, tiled=True)
    state_wide = hidden_state.astype(jnp.float32)
    mean_square = jnp.mean(state_wide * state_wide, axis=1, keepdims=True)
    normed = (state_wide * lax.rsqrt(mean_square + 1e-05) * gain[None, :]).astype(jnp.bfloat16)

    tokens = []
    for d in range(outer_count):
        block = swap(normed, "outer", d) if d else normed
        tokens += [block] + [swap(block, "head", e) for e in range(1, head_count)]
    tokens = jnp.concatenate(tokens, axis=0)

    gate_up_weights = jnp.zeros((2, D, hidden_cols), jnp.bfloat16)
    down_weights = jnp.zeros((hidden_cols, D), jnp.bfloat16)
    for d in range(outer_count):
        piece = lax.dynamic_slice_in_dim(w_gate_up, (outer ^ d) * hidden_cols, hidden_cols, 2)
        piece = swap(piece, "outer", d) if d else piece
        across = swap(piece, "inner", 2)
        for e, part in enumerate([piece, swap(piece, "inner", 1), across, swap(across, "inner", 1)]):
            at = ((inner ^ e) * outer_count + (outer ^ d)) * feature_rows
            gate_up_weights = lax.dynamic_update_slice(gate_up_weights, part, (0, at, 0))
    for d in range(outer_count):
        piece = lax.dynamic_slice_in_dim(w_down, (outer ^ d) * hidden_cols, hidden_cols, 0)
        piece = swap(piece, "outer", d) if d else piece
        across = swap(piece, "inner", 2)
        for e, part in enumerate([piece, swap(piece, "inner", 1), across, swap(across, "inner", 1)]):
            at = ((inner ^ e) * outer_count + (outer ^ d)) * feature_rows
            down_weights = lax.dynamic_update_slice(down_weights, part, (0, at))

    gate_up = jnp.einsum("td,kdf->ktf", tokens, gate_up_weights, preferred_element_type=jnp.float32)
    activated = (jax.nn.silu(gate_up[0]) * gate_up[1]).astype(jnp.bfloat16)
    down = jnp.dot(activated, down_weights, preferred_element_type=jnp.float32).astype(jnp.bfloat16)
    down = down.reshape(outer_count, head_count, -1, D)
    paired = down[:, 0].astype(jnp.float32)
    for e in range(1, head_count):
        paired = paired + swap(down[:, e], "head", e).astype(jnp.float32)
    down_sum = paired[0]
    for d in range(1, outer_count):
        down_sum = down_sum + swap(paired[d].astype(jnp.bfloat16), "outer", d).astype(jnp.float32)
    layer_rows = (state_wide + down_sum).astype(jnp.bfloat16)
    layer_out = lax.all_to_all(layer_rows, "inner", split_axis=1, concat_axis=0, tiled=True)
    return (context, layer_out)


def solution(mesh):
    placed = (
        P(("outer", "inner", "head"), None),
        P(("outer", "inner", "head"), None),
        P(("outer", "inner", "head"), None),
        P(),
        P("outer", "inner"),
        P("inner"),
        P("head", ("inner", "outer")),
        P(None, ("inner", "outer"), "head"),
        P("head", ("inner", "outer")),
    )
    return jax.shard_map(
        per_device,
        mesh=mesh,
        in_specs=placed,
        out_specs=(P(("outer", "inner"), "head"), P(("outer", "head"), "inner")),
        check_vma=False,
    )
```

```python
import functools

import jax
import jax.numpy as jnp
from jax import lax
from jax.experimental import pallas as pl
from jax.experimental.pallas import tpu as pltpu
from jax.sharding import PartitionSpec as P

D = 4096
QUERY_HEADS = 32
KEY_VALUE_HEADS = 8
HEAD_WIDTH = 128
GROUP = QUERY_HEADS // KEY_VALUE_HEADS
WINDOW_PER_DOC = 4
QUERY_TILE = 128
PARTS = 2


def swap(array, axis, distance):
    count = lax.axis_size(axis)
    return lax.ppermute(array, axis, [(s, s ^ distance) for s in range(count)])


def attention_kernel(halo_rows, reach, starts_ref, queries_ref, own_ref, halo_ref, out_ref, keys, values):
    tile = pl.program_id(0)
    rows = queries_ref.shape[0]
    span = reach + rows

    @pl.when(tile == 0)
    def _():
        keys[:halo_rows, :] = halo_ref[:, :HEAD_WIDTH]
        values[:halo_rows, :] = halo_ref[:, HEAD_WIDTH:]
        keys[halo_rows:, :] = own_ref[:, :HEAD_WIDTH]
        values[halo_rows:, :] = own_ref[:, HEAD_WIDTH:]

    first = pl.multiple_of(tile * rows + (halo_rows - reach), rows)
    near_keys = keys[pl.ds(first, span), :]
    near_values = values[pl.ds(first, span), :]
    key_place = lax.broadcasted_iota(jnp.int32, (rows, span), 1)
    query_place = lax.broadcasted_iota(jnp.int32, (rows, span), 0) + reach
    start = starts_ref[...] - (first - halo_rows)
    allowed = (key_place <= query_place) & (key_place >= start)
    for g in range(GROUP):
        cols = slice(g * HEAD_WIDTH, (g + 1) * HEAD_WIDTH)
        scores = lax.dot_general(
            queries_ref[:, cols], near_keys, (((1,), (1,)), ((), ())), preferred_element_type=jnp.float32
        ) * (HEAD_WIDTH ** (-0.5))
        masked = jnp.where(allowed, scores, -1e30)
        row_max = jnp.max(masked, axis=1, keepdims=True)
        weights = jnp.exp(masked - row_max)
        totals = jnp.sum(weights, axis=1, keepdims=True)
        summed = jnp.dot(weights.astype(jnp.bfloat16), near_values, preferred_element_type=jnp.float32)
        out_ref[:, cols] = (summed / totals).astype(jnp.bfloat16)


def attention(packed, halo, starts, reach):
    rows = packed.shape[0]
    halo_rows = halo.shape[0]
    q_cols = GROUP * HEAD_WIDTH
    kv_cols = 2 * HEAD_WIDTH
    return pl.pallas_call(
        functools.partial(attention_kernel, halo_rows, reach),
        grid=(rows // QUERY_TILE,),
        in_specs=[
            pl.BlockSpec((QUERY_TILE, 1), lambda t: (t, 0)),
            pl.BlockSpec((QUERY_TILE, q_cols), lambda t: (t, 0)),
            pl.BlockSpec((rows, kv_cols), lambda t: (0, q_cols // kv_cols)),
            pl.BlockSpec((halo_rows, kv_cols), lambda t: (0, 0)),
        ],
        out_specs=pl.BlockSpec((QUERY_TILE, q_cols), lambda t: (t, 0)),
        out_shape=jax.ShapeDtypeStruct((rows, q_cols), jnp.bfloat16),
        scratch_shapes=[
            pltpu.VMEM((halo_rows + rows, HEAD_WIDTH), jnp.bfloat16),
            pltpu.VMEM((halo_rows + rows, HEAD_WIDTH), jnp.bfloat16),
        ],
        compiler_params=pltpu.CompilerParams(vmem_limit_bytes=32 * 1024 * 1024),
        cost_estimate=pl.CostEstimate(
            flops=4 * rows * (reach + QUERY_TILE) * q_cols,
            bytes_accessed=rows * 4 * q_cols,
            transcendentals=rows * (reach + QUERY_TILE) * GROUP,
        ),
    )(starts, packed, packed, halo)


def blocks_over_inner(block):
    across = swap(block, "inner", 2)
    return [block, swap(block, "inner", 1), across, swap(across, "inner", 1)]


def earlier_planes(kv, hops):
    count = lax.axis_size("outer")
    moved = [lax.ppermute(kv, "outer", [(s, s + d) for s in range(count - d)]) for d in range(hops, 0, -1)]
    return jnp.concatenate(moved, axis=0)


def document_starts(bounds, first, rows):
    place = first + jnp.arange(rows, dtype=jnp.int32)
    starts = jnp.max(jnp.where(bounds[None, :] <= place[:, None], bounds[None, :], 0), axis=1) - first
    return starts[:, None].astype(jnp.int32)


def per_device(query, key, value, doc_lengths, resid, norm_gain, w_out, w_gate_up, w_down):
    inner_count = lax.axis_size("inner")
    outer_count = lax.axis_size("outer")
    head_count = lax.axis_size("head")
    outer, inner, head = lax.axis_index("outer"), lax.axis_index("inner"), lax.axis_index("head")
    rows = query.shape[0]
    plane_rows = rows * inner_count * head_count
    reach = plane_rows * outer_count // WINDOW_PER_DOC
    feature_rows = w_gate_up.shape[1]
    hidden_cols = w_gate_up.shape[2] // outer_count

    weights_out = lax.all_gather(w_out, "outer", axis=1, tiled=True)
    bounds = jnp.cumsum(doc_lengths)
    hops = reach // plane_rows
    token_rows = plane_rows // inner_count
    packing = (head_count, KEY_VALUE_HEADS // head_count)
    groups = jnp.concatenate(
        [
            query.reshape(rows, *packing, GROUP * HEAD_WIDTH),
            key.reshape(rows, *packing, HEAD_WIDTH),
            value.reshape(rows, *packing, HEAD_WIDTH),
        ],
        axis=3,
    )
    q_cols = GROUP * HEAD_WIDTH
    if packing[1] == inner_count:
        groups = jnp.transpose(groups, (2, 1, 0, 3)).reshape(inner_count * head_count, rows, -1)
        packed = lax.all_to_all(groups, ("inner", "head"), split_axis=0, concat_axis=0, tiled=True)
        packed = packed.reshape(plane_rows, -1)
        halo = earlier_planes(packed[:, q_cols:], hops)
        starts = document_starts(bounds, outer * plane_rows, plane_rows)
        own_context = attention(packed, halo, starts, reach)
        parts = blocks_over_inner(own_context)
        plane_context = jnp.zeros((plane_rows, inner_count * q_cols), jnp.bfloat16)
        for d, part in enumerate(parts):
            plane_context = lax.dynamic_update_slice(plane_context, part, (0, (inner ^ d) * q_cols))
        context = lax.dynamic_slice_in_dim(plane_context, inner * token_rows, token_rows, 0)
    else:
        groups = jnp.transpose(groups[:, :, 0], (1, 0, 2))
        packed = lax.all_to_all(groups, "head", split_axis=0, concat_axis=0, tiled=True).reshape(token_rows, -1)
        plane_kv = lax.all_gather(packed[:, q_cols:], "inner", axis=0, tiled=True)
        every_kv = jnp.concatenate([earlier_planes(plane_kv, hops), plane_kv], axis=0)
        halo = lax.dynamic_slice_in_dim(every_kv, inner * token_rows, reach, 0)
        starts = document_starts(bounds, outer * plane_rows + inner * token_rows, token_rows)
        context = attention(packed, halo, starts, reach)
        plane_context = lax.all_gather(context, "inner", axis=0, tiled=True)

    half = plane_rows // head_count
    partial_proj = jnp.dot(plane_context, weights_out, preferred_element_type=jnp.float32).astype(jnp.bfloat16)
    projected = lax.dynamic_slice_in_dim(partial_proj, head * half, half, 0).astype(jnp.float32)
    for e in range(1, head_count):
        sent = lax.dynamic_slice_in_dim(partial_proj, (head ^ e) * half, half, 0)
        projected = projected + swap(sent, "head", e).astype(jnp.float32)
    own_resid = lax.dynamic_slice_in_dim(resid, head * half, half, 0)
    hidden_part = (own_resid.astype(jnp.float32) + projected).astype(jnp.bfloat16)

    own_rows = half // inner_count
    state = []
    for a in range(inner_count):
        block = lax.dynamic_slice_in_dim(hidden_part, (inner ^ a) * own_rows, own_rows, 0)
        state.append(swap(block, "inner", a) if a else block)
    state = jnp.concatenate(state, axis=1).astype(jnp.float32)
    mean_square = jnp.mean(state * state, axis=1, keepdims=True)
    normed = (state * lax.rsqrt(mean_square + 1e-05)).astype(jnp.bfloat16)
    part_rows = feature_rows // PARTS
    normed = normed.reshape(own_rows, inner_count, outer_count, PARTS, part_rows)
    normed = jnp.transpose(normed, (0, 3, 1, 2, 4)).reshape(own_rows, D)
    tokens = []
    for d in range(outer_count):
        block = swap(normed, "outer", d) if d else normed
        tokens += [block] + [swap(block, "head", e) for e in range(1, head_count)]
    tokens = jnp.concatenate(tokens, axis=0)

    own_gain = lax.dynamic_slice_in_dim(norm_gain, outer * feature_rows, feature_rows, 0)
    streams = []
    latest = context
    for part in range(PARTS):
        rows_of = slice(part * part_rows, (part + 1) * part_rows)
        for which in range(2):
            piece = (w_gate_up[which, rows_of].astype(jnp.float32) * own_gain[rows_of, None]).astype(jnp.bfloat16)
            piece = jnp.transpose(piece.reshape(part_rows, outer_count, hidden_cols), (1, 0, 2))
            piece = lax.optimization_barrier((piece, latest))[0]
            latest = lax.all_to_all(piece, "outer", split_axis=0, concat_axis=0, tiled=True)
            streams.append(blocks_over_inner(latest.reshape(outer_count * part_rows, hidden_cols)))
    down_streams = []
    for part in range(PARTS):
        piece = w_down[:, part * part_rows : (part + 1) * part_rows].reshape(outer_count, hidden_cols, part_rows)
        piece = lax.optimization_barrier((piece, latest))[0]
        latest = lax.all_to_all(piece, "outer", split_axis=0, concat_axis=0, tiled=True)
        columns = jnp.transpose(latest, (1, 0, 2)).reshape(hidden_cols, outer_count * part_rows)
        down_streams.append(blocks_over_inner(columns))

    depth = outer_count * part_rows
    gate, up = 0.0, 0.0
    for part in range(PARTS):
        for a in range(inner_count):
            at = (part * inner_count + a) * depth
            near = tokens[:, at : at + depth]
            gate = gate + jnp.dot(near, streams[2 * part][a], preferred_element_type=jnp.float32)
            up = up + jnp.dot(near, streams[2 * part + 1][a], preferred_element_type=jnp.float32)
    activated = (jax.nn.silu(gate) * up).astype(jnp.bfloat16)

    down_sums = []
    for part in range(PARTS):
        down = [jnp.dot(activated, block, preferred_element_type=jnp.float32) for block in down_streams[part]]
        down = jnp.concatenate(down, axis=1).astype(jnp.bfloat16)
        down = down.reshape(outer_count, head_count, own_rows, D // PARTS)
        paired = down[:, 0].astype(jnp.float32)
        for e in range(1, head_count):
            paired = paired + swap(down[:, e], "head", e).astype(jnp.float32)
        down_sum = paired[0]
        for d in range(1, outer_count):
            down_sum = down_sum + swap(paired[d].astype(jnp.bfloat16), "outer", d).astype(jnp.float32)
        down_sums.append(down_sum.reshape(own_rows, inner_count, outer_count, 1, part_rows))
    down_sum = jnp.concatenate(down_sums, axis=3).reshape(own_rows, D)
    layer_rows = (state + down_sum).astype(jnp.bfloat16)
    layer_out = jnp.zeros((half, D // inner_count), jnp.bfloat16)
    for a in range(inner_count):
        block = layer_rows[:, a * (D // inner_count) : (a + 1) * (D // inner_count)]
        block = swap(block, "inner", a) if a else block
        layer_out = lax.dynamic_update_slice(layer_out, block, ((inner ^ a) * own_rows, 0))
    return (context, layer_out)


def solution(mesh):
    placed = (
        P(("outer", "inner", "head"), None),
        P(("outer", "inner", "head"), None),
        P(("outer", "inner", "head"), None),
        P(),
        P("outer", "inner"),
        P("inner"),
        P("head", ("inner", "outer")),
        P(None, ("inner", "outer"), "head"),
        P("head", ("inner", "outer")),
    )
    return jax.shard_map(
        per_device,
        mesh=mesh,
        in_specs=placed,
        out_specs=(P(("outer", "inner"), "head"), P(("outer", "head"), "inner")),
        check_vma=False,
    )
```

```python
import functools

import jax
import jax.numpy as jnp
from jax import lax
from jax.experimental import pallas as pl
from jax.experimental.pallas import tpu as pltpu
from jax.sharding import PartitionSpec as P

D = 4096
QUERY_HEADS = 32
KEY_VALUE_HEADS = 8
HEAD_WIDTH = 128
GROUP = QUERY_HEADS // KEY_VALUE_HEADS
Q_COLS = GROUP * HEAD_WIDTH
KV_COLS = 2 * HEAD_WIDTH
WINDOW_PER_DOC = 4
QUERY_TILE = 128
ROW_TILE = 256
VMEM_LIMIT = 48 * 1024 * 1024
ANY = pl.BlockSpec(memory_space=pl.ANY)
VMEM = pl.BlockSpec(memory_space=pltpu.VMEM)
SMEM = pl.BlockSpec(memory_space=pltpu.SMEM)


def swap(array, axis, distance):
    if distance == 0:
        return array
    count = lax.axis_size(axis)
    return lax.ppermute(array, axis, [(s, s ^ distance) for s in range(count)])


def after(array, earlier):
    return lax.optimization_barrier((array, earlier))[0]


def blocks_over_inner(block):
    across = swap(block, "inner", 2)
    return [block, swap(block, "inner", 1), across, swap(across, "inner", 1)]


def earlier_planes(kv, hops):
    count = lax.axis_size("outer")
    moved = [lax.ppermute(kv, "outer", [(s, s + d) for s in range(count - d)]) for d in range(hops, 0, -1)]
    return jnp.concatenate(moved, axis=0)


def document_starts(bounds, first, rows):
    place = first + jnp.arange(rows, dtype=jnp.int32)
    starts = jnp.max(jnp.where(bounds[None, :] <= place[:, None], bounds[None, :], 0), axis=1) - first
    return starts[:, None].astype(jnp.int32)


def row_tiles(rows):
    step = ROW_TILE if rows % ROW_TILE == 0 else rows
    return [slice(at, at + step) for at in range(0, rows, step)]


def attention_kernel(halo_rows, reach, starts_ref, queries_ref, own_ref, halo_ref, out_ref, keys, values):
    tile = pl.program_id(0)
    rows = queries_ref.shape[0]
    span = reach + rows

    @pl.when(tile == 0)
    def _():
        keys[:halo_rows, :] = halo_ref[:, :HEAD_WIDTH]
        values[:halo_rows, :] = halo_ref[:, HEAD_WIDTH:]
        keys[halo_rows:, :] = own_ref[:, :HEAD_WIDTH]
        values[halo_rows:, :] = own_ref[:, HEAD_WIDTH:]

    first = pl.multiple_of(tile * rows + (halo_rows - reach), rows)
    near_keys = keys[pl.ds(first, span), :]
    near_values = values[pl.ds(first, span), :]
    key_place = lax.broadcasted_iota(jnp.int32, (rows, span), 1)
    query_place = lax.broadcasted_iota(jnp.int32, (rows, span), 0) + reach
    start = starts_ref[...] - (first - halo_rows)
    allowed = (key_place <= query_place) & (key_place >= start)
    for g in range(GROUP):
        cols = slice(g * HEAD_WIDTH, (g + 1) * HEAD_WIDTH)
        scores = lax.dot_general(
            queries_ref[:, cols], near_keys, (((1,), (1,)), ((), ())), preferred_element_type=jnp.float32
        ) * (HEAD_WIDTH ** (-0.5))
        masked = jnp.where(allowed, scores, -1e30)
        row_max = jnp.max(masked, axis=1, keepdims=True)
        weights = jnp.exp(masked - row_max)
        totals = jnp.sum(weights, axis=1, keepdims=True)
        summed = jnp.dot(weights.astype(jnp.bfloat16), near_values, preferred_element_type=jnp.float32)
        out_ref[:, cols] = (summed / totals).astype(jnp.bfloat16)


def attention(packed, halo, halo_at, starts, reach):
    rows = packed.shape[0]
    halo_rows = halo.shape[0]
    return pl.pallas_call(
        functools.partial(attention_kernel, halo_rows, reach),
        grid=(rows // QUERY_TILE,),
        in_specs=[
            pl.BlockSpec((QUERY_TILE, 1), lambda t: (t, 0)),
            pl.BlockSpec((QUERY_TILE, Q_COLS), lambda t: (t, 0)),
            pl.BlockSpec((rows, KV_COLS), lambda t: (0, Q_COLS // KV_COLS)),
            pl.BlockSpec((halo_rows, KV_COLS), lambda t: (0, halo_at)),
        ],
        out_specs=pl.BlockSpec((QUERY_TILE, Q_COLS), lambda t: (t, 0)),
        out_shape=jax.ShapeDtypeStruct((rows, Q_COLS), jnp.bfloat16),
        scratch_shapes=[
            pltpu.VMEM((halo_rows + rows, HEAD_WIDTH), jnp.bfloat16),
            pltpu.VMEM((halo_rows + rows, HEAD_WIDTH), jnp.bfloat16),
        ],
        compiler_params=pltpu.CompilerParams(vmem_limit_bytes=VMEM_LIMIT),
        cost_estimate=pl.CostEstimate(
            flops=4 * rows * (reach + QUERY_TILE) * Q_COLS,
            bytes_accessed=rows * 4 * Q_COLS,
            transcendentals=rows * (reach + QUERY_TILE) * GROUP,
        ),
        name="attention",
    )(starts, packed, packed, halo)


def gain_kernel(gain_ref, weights_ref, gate_ref, up_ref):
    for which, out_ref in enumerate((gate_ref, up_ref)):
        out_ref[0] = (weights_ref[which].astype(jnp.float32) * gain_ref[...]).astype(jnp.bfloat16)


def scaled_gate_up(w_gate_up, gain, outer_count):
    _, rows, width = w_gate_up.shape
    cols = width // outer_count
    if cols % HEAD_WIDTH:
        wide = (w_gate_up.astype(jnp.float32) * gain[None]).astype(jnp.bfloat16)
        return jnp.transpose(wide.reshape(2, rows, outer_count, cols), (0, 2, 1, 3))
    return pl.pallas_call(
        gain_kernel,
        grid=(outer_count,),
        in_specs=[
            pl.BlockSpec((rows, 1), lambda p: (0, 0)),
            pl.BlockSpec((2, rows, cols), lambda p: (0, 0, p)),
        ],
        out_specs=[pl.BlockSpec((1, rows, cols), lambda p: (p, 0, 0))] * 2,
        out_shape=[jax.ShapeDtypeStruct((outer_count, rows, cols), jnp.bfloat16)] * 2,
        compiler_params=pltpu.CompilerParams(vmem_limit_bytes=VMEM_LIMIT),
        cost_estimate=pl.CostEstimate(flops=2 * rows * width, bytes_accessed=8 * rows * width, transcendentals=0),
        name="take_gain",
    )(gain, w_gate_up)


def projection_kernel(block_count, place_ref, *refs):
    blocks, weights_ref = refs[:block_count], refs[block_count]
    kept_ref, sent_ref = refs[block_count + 1 : block_count + 3]
    inner, head = place_ref[0], place_ref[1]
    half, depth = kept_ref.shape[0], blocks[0].shape[1]
    for e in range(sent_ref.shape[0] + 1):
        rows = pl.ds(pl.multiple_of((head ^ e) * half, half), half)
        total = jnp.zeros(kept_ref.shape, jnp.float32)
        for a, block in enumerate(blocks):
            at = pl.ds(pl.multiple_of((inner ^ a) * depth, depth), depth) if block_count > 1 else slice(None)
            total = total + jnp.dot(block[rows, :], weights_ref[at, :], preferred_element_type=jnp.float32)
        if e == 0:
            kept_ref[...] = total.astype(jnp.bfloat16)
        else:
            sent_ref[e - 1] = total.astype(jnp.bfloat16)
    if block_count > 1:
        context_ref = refs[block_count + 3]
        tokens = context_ref.shape[0]
        own = pl.ds(pl.multiple_of(inner * tokens, tokens), tokens)
        for a, block in enumerate(blocks):
            context_ref[:, pl.ds(pl.multiple_of((inner ^ a) * depth, depth), depth)] = block[own, :]


def projection(blocks, weights, place, head_count, inner_count):
    rows, depth = blocks[0].shape
    half, width = rows // head_count, weights.shape[1]
    outs = [(half, width), (head_count - 1, half, width)]
    if len(blocks) > 1:
        outs.append((rows // inner_count, len(blocks) * depth))
    return pl.pallas_call(
        functools.partial(projection_kernel, len(blocks)),
        in_specs=[SMEM] + [VMEM] * (len(blocks) + 1),
        out_specs=[VMEM] * len(outs),
        out_shape=[jax.ShapeDtypeStruct(shape, jnp.bfloat16) for shape in outs],
        compiler_params=pltpu.CompilerParams(vmem_limit_bytes=VMEM_LIMIT),
        cost_estimate=pl.CostEstimate(
            flops=2 * rows * weights.size, bytes_accessed=2 * (weights.size + rows * 2 * width), transcendentals=0
        ),
        name="projection",
    )(place, *blocks, weights)


def gate_up_kernel(token_count, block_count, *refs):
    tokens = refs[:token_count]
    weights = refs[token_count : token_count + 2 * block_count]
    out_ref, held, near, gate, up, token_sems, weight_sems = refs[token_count + 2 * block_count :]
    piece = held.shape[0] // token_count
    token_copies = [
        pltpu.make_async_copy(ref, held.at[pl.ds(j * piece, piece)], token_sems.at[j]) for j, ref in enumerate(tokens)
    ]
    weight_copies = [pltpu.make_async_copy(ref, near.at[j], weight_sems.at[j]) for j, ref in enumerate(weights)]
    for copy in token_copies + weight_copies:
        copy.start()
    for copy in token_copies:
        copy.wait()
    depth = near.shape[1]
    for a in range(block_count):
        for which, total in enumerate((gate, up)):
            weight_copies[2 * a + which].wait()
            for rows in row_tiles(held.shape[0]):
                product = jnp.dot(
                    held[rows, a * depth : (a + 1) * depth], near[2 * a + which], preferred_element_type=jnp.float32
                )
                total[rows, :] = product if a == 0 else total[rows, :] + product
    for rows in row_tiles(held.shape[0]):
        out_ref[rows, :] = (gate[rows, :] / (1.0 + jnp.exp(-gate[rows, :])) * up[rows, :]).astype(jnp.bfloat16)


def gate_up(tokens, gates, ups):
    if len(tokens) > 8:
        tokens = [jnp.concatenate(tokens, axis=0)]
    rows = sum(piece.shape[0] for piece in tokens)
    depth, cols = gates[0].shape
    weights = [block for pair in zip(gates, ups) for block in pair]
    return pl.pallas_call(
        functools.partial(gate_up_kernel, len(tokens), len(gates)),
        in_specs=[ANY] * (len(tokens) + len(weights)),
        out_specs=VMEM,
        out_shape=jax.ShapeDtypeStruct((rows, cols), jnp.bfloat16),
        scratch_shapes=[
            pltpu.VMEM((rows, depth * len(gates)), jnp.bfloat16),
            pltpu.VMEM((len(weights), depth, cols), jnp.bfloat16),
            pltpu.VMEM((rows, cols), jnp.float32),
            pltpu.VMEM((rows, cols), jnp.float32),
            pltpu.SemaphoreType.DMA((len(tokens),)),
            pltpu.SemaphoreType.DMA((len(weights),)),
        ],
        compiler_params=pltpu.CompilerParams(vmem_limit_bytes=VMEM_LIMIT),
        cost_estimate=pl.CostEstimate(
            flops=4 * rows * depth * len(gates) * cols,
            bytes_accessed=2 * (rows * depth * len(gates) + len(weights) * depth * cols),
            transcendentals=rows * cols,
        ),
        name="gate_up",
    )(*tokens, *weights)


def down_kernel(activated_ref, weights_ref, kept_ref, sent_ref):
    sources, _, cols = weights_ref.shape
    kept_rows = kept_ref.shape[0]
    for s in range(sources):
        at = slice(s * cols, (s + 1) * cols)
        for e in range(sent_ref.shape[0] + 1):
            rows = slice(e * kept_rows, (e + 1) * kept_rows)
            product = jnp.dot(activated_ref[rows, :], weights_ref[s], preferred_element_type=jnp.float32)
            if e == 0:
                kept_ref[:, at] = product.astype(jnp.bfloat16)
            else:
                sent_ref[e - 1, :, at] = product.astype(jnp.bfloat16)


def down_product(activated, weights, head_count):
    rows = activated.shape[0] // head_count
    sources, depth, cols = weights.shape
    return pl.pallas_call(
        down_kernel,
        in_specs=[VMEM, VMEM],
        out_specs=[VMEM, VMEM],
        out_shape=[
            jax.ShapeDtypeStruct((rows, sources * cols), jnp.bfloat16),
            jax.ShapeDtypeStruct((head_count - 1, rows, sources * cols), jnp.bfloat16),
        ],
        compiler_params=pltpu.CompilerParams(vmem_limit_bytes=VMEM_LIMIT),
        cost_estimate=pl.CostEstimate(
            flops=2 * activated.size * sources * cols,
            bytes_accessed=2 * (activated.size + weights.size + head_count * rows * sources * cols),
            transcendentals=0,
        ),
        name="down",
    )(activated, weights)


def per_device(query, key, value, doc_lengths, resid, norm_gain, w_out, w_gate_up, w_down):
    inner_count = lax.axis_size("inner")
    outer_count = lax.axis_size("outer")
    head_count = lax.axis_size("head")
    outer, inner, head = lax.axis_index("outer"), lax.axis_index("inner"), lax.axis_index("head")
    rows = query.shape[0]
    plane_rows = rows * inner_count * head_count
    reach = plane_rows * outer_count // WINDOW_PER_DOC
    feature_rows = w_gate_up.shape[1]
    hidden_cols = w_gate_up.shape[2] // outer_count
    bounds = jnp.cumsum(doc_lengths)
    hops = reach // plane_rows
    token_rows = plane_rows // inner_count
    half = plane_rows // head_count
    packing = (rows, head_count, KEY_VALUE_HEADS // head_count, -1)

    weights_out = lax.all_gather(w_out, "outer", axis=1, tiled=True)
    own_gain = lax.dynamic_slice_in_dim(norm_gain, outer * feature_rows, feature_rows, 0)
    w_gate, w_up = scaled_gate_up(w_gate_up, own_gain[:, None], outer_count)
    if packing[2] == inner_count and hops == 1:
        earlier = [lax.ppermute(part, "outer", [(s, s + 1) for s in range(outer_count - 1)]) for part in (key, value)]
        groups = jnp.concatenate([part.reshape(packing) for part in (query, key, value, *earlier)], axis=3)
        groups = jnp.transpose(groups, (2, 1, 0, 3)).reshape(inner_count * head_count, rows, -1)
        packed = lax.all_to_all(groups, ("inner", "head"), split_axis=0, concat_axis=0, tiled=True)
        packed = packed.reshape(plane_rows, -1)
        starts = document_starts(bounds, outer * plane_rows, plane_rows)
        own_context = attention(packed, packed, Q_COLS // KV_COLS + 1, starts, reach)
        blocks = blocks_over_inner(own_context)
    else:
        groups = jnp.concatenate([part.reshape(packing) for part in (query, key, value)], axis=3)
        groups = jnp.transpose(groups[:, :, 0], (1, 0, 2))
        packed = lax.all_to_all(groups, "head", split_axis=0, concat_axis=0, tiled=True).reshape(token_rows, -1)
        plane_kv = lax.all_gather(packed[:, Q_COLS:], "inner", axis=0, tiled=True)
        every_kv = jnp.concatenate([earlier_planes(plane_kv, hops), plane_kv], axis=0)
        halo = lax.dynamic_slice_in_dim(every_kv, inner * token_rows, reach, 0)
        starts = document_starts(bounds, outer * plane_rows + inner * token_rows, token_rows)
        own_context = attention(packed, halo, 0, starts, reach)
        blocks = [lax.all_gather(own_context, "inner", axis=0, tiled=True)]

    spread = functools.partial(lax.all_to_all, axis_name="outer", split_axis=0, concat_axis=0, tiled=True)
    gate_here = spread(after(w_gate, packed))
    up_here = spread(after(w_up, gate_here))
    down_here = spread(after(w_down.reshape(outer_count, hidden_cols, feature_rows), up_here))
    gates = blocks_over_inner(gate_here.reshape(-1, hidden_cols))
    ups = blocks_over_inner(up_here.reshape(-1, hidden_cols))
    downs = blocks_over_inner(down_here)

    place = jnp.stack([inner, head]).astype(jnp.int32)
    kept, sent, *whole = projection(blocks, weights_out, place, head_count, inner_count)
    context = whole[0] if whole else own_context
    projected = kept.astype(jnp.float32)
    for e in range(1, head_count):
        projected = projected + swap(sent[e - 1], "head", e).astype(jnp.float32)
    own_resid = lax.dynamic_slice_in_dim(resid, head * half, half, 0)
    hidden_part = (own_resid.astype(jnp.float32) + projected).astype(jnp.bfloat16)

    own_rows = half // inner_count
    state = []
    for a in range(inner_count):
        block = lax.dynamic_slice_in_dim(hidden_part, (inner ^ a) * own_rows, own_rows, 0)
        state.append(swap(block, "inner", a).astype(jnp.float32))
    squares = sum([jnp.sum(block * block, axis=1, keepdims=True) for block in state])
    inverse = lax.rsqrt(squares / D + 1e-05)
    normed = jnp.concatenate([block * inverse for block in state], axis=1).astype(jnp.bfloat16)
    along_outer = [swap(normed, "outer", d) for d in range(outer_count)]
    tokens = [swap(block, "head", e) for e in range(head_count) for block in along_outer]

    activated = gate_up(tokens, gates, ups)
    layer_out = jnp.zeros((half, D // inner_count), jnp.bfloat16)
    for a in range(inner_count):
        kept, sent = down_product(activated, downs[a], head_count)
        paired = kept.astype(jnp.float32)
        for e in range(1, head_count):
            paired = paired + swap(sent[e - 1], "head", e).astype(jnp.float32)
        paired = paired.reshape(outer_count, own_rows, -1)
        total = state[a] + paired[0]
        for d in range(1, outer_count):
            total = total + swap(paired[d].astype(jnp.bfloat16), "outer", d).astype(jnp.float32)
        block = swap(total.astype(jnp.bfloat16), "inner", a)
        layer_out = lax.dynamic_update_slice(layer_out, block, ((inner ^ a) * own_rows, 0))
    return (context, layer_out)


def solution(mesh):
    placed = (
        P(("outer", "inner", "head"), None),
        P(("outer", "inner", "head"), None),
        P(("outer", "inner", "head"), None),
        P(),
        P("outer", "inner"),
        P("inner"),
        P("head", ("inner", "outer")),
        P(None, ("inner", "outer"), "head"),
        P("head", ("inner", "outer")),
    )
    return jax.shard_map(
        per_device,
        mesh=mesh,
        in_specs=placed,
        out_specs=(P(("outer", "inner"), "head"), P(("outer", "head"), "inner")),
        check_vma=False,
    )
```

```python
import functools

import jax
import jax.numpy as jnp
from jax import lax
from jax.experimental import pallas as pl
from jax.experimental.pallas import tpu as pltpu
from jax.sharding import PartitionSpec as P

D = 4096
QUERY_HEADS = 32
KEY_VALUE_HEADS = 8
HEAD_WIDTH = 128
GROUP = QUERY_HEADS // KEY_VALUE_HEADS
Q_COLS = GROUP * HEAD_WIDTH
KV_COLS = 2 * HEAD_WIDTH
WINDOW_PER_DOC = 4
QUERY_TILE = 128
ROW_TILE = 256
VMEM_LIMIT = 48 * 1024 * 1024
ANY = pl.BlockSpec(memory_space=pl.ANY)
VMEM = pl.BlockSpec(memory_space=pltpu.VMEM)
SMEM = pl.BlockSpec(memory_space=pltpu.SMEM)


def swap(array, axis, distance):
    if distance == 0:
        return array
    count = lax.axis_size(axis)
    return lax.ppermute(array, axis, [(s, s ^ distance) for s in range(count)])


def after(array, earlier):
    return lax.optimization_barrier((array, earlier))[0]


def blocks_over_inner(block):
    across = swap(block, "inner", 2)
    return [block, swap(block, "inner", 1), across, swap(across, "inner", 1)]


def earlier_planes(kv, hops):
    count = lax.axis_size("outer")
    moved = [lax.ppermute(kv, "outer", [(s, s + d) for s in range(count - d)]) for d in range(hops, 0, -1)]
    return jnp.concatenate(moved, axis=0)


def document_starts(bounds, first, rows):
    place = first + jnp.arange(rows, dtype=jnp.int32)
    starts = jnp.max(jnp.where(bounds[None, :] <= place[:, None], bounds[None, :], 0), axis=1) - first
    return starts[:, None].astype(jnp.int32)


def row_tiles(rows):
    step = ROW_TILE if rows % ROW_TILE == 0 else rows
    return [slice(at, at + step) for at in range(0, rows, step)]


def attention_kernel(halo_rows, reach, starts_ref, queries_ref, own_ref, halo_ref, out_ref, keys, values):
    tile = pl.program_id(0)
    rows = queries_ref.shape[0]
    span = reach + rows

    @pl.when(tile == 0)
    def _():
        keys[:halo_rows, :] = halo_ref[:, :HEAD_WIDTH]
        values[:halo_rows, :] = halo_ref[:, HEAD_WIDTH:]
        keys[halo_rows:, :] = own_ref[:, :HEAD_WIDTH]
        values[halo_rows:, :] = own_ref[:, HEAD_WIDTH:]

    first = pl.multiple_of(tile * rows + (halo_rows - reach), rows)
    near_keys = keys[pl.ds(first, span), :]
    near_values = values[pl.ds(first, span), :]
    key_place = lax.broadcasted_iota(jnp.int32, (rows, span), 1)
    query_place = lax.broadcasted_iota(jnp.int32, (rows, span), 0) + reach
    start = starts_ref[...] - (first - halo_rows)
    allowed = (key_place <= query_place) & (key_place >= start)
    for g in range(GROUP):
        cols = slice(g * HEAD_WIDTH, (g + 1) * HEAD_WIDTH)
        scores = lax.dot_general(
            queries_ref[:, cols], near_keys, (((1,), (1,)), ((), ())), preferred_element_type=jnp.float32
        ) * (HEAD_WIDTH ** (-0.5))
        masked = jnp.where(allowed, scores, -1e30)
        row_max = jnp.max(masked, axis=1, keepdims=True)
        weights = jnp.exp(masked - row_max)
        totals = jnp.sum(weights, axis=1, keepdims=True)
        summed = jnp.dot(weights.astype(jnp.bfloat16), near_values, preferred_element_type=jnp.float32)
        out_ref[:, cols] = (summed / totals).astype(jnp.bfloat16)


def attention(packed, halo, halo_at, starts, reach):
    rows = packed.shape[0]
    halo_rows = halo.shape[0]
    return pl.pallas_call(
        functools.partial(attention_kernel, halo_rows, reach),
        grid=(rows // QUERY_TILE,),
        in_specs=[
            pl.BlockSpec((QUERY_TILE, 1), lambda t: (t, 0)),
            pl.BlockSpec((QUERY_TILE, Q_COLS), lambda t: (t, 0)),
            pl.BlockSpec((rows, KV_COLS), lambda t: (0, Q_COLS // KV_COLS)),
            pl.BlockSpec((halo_rows, KV_COLS), lambda t: (0, halo_at)),
        ],
        out_specs=pl.BlockSpec((QUERY_TILE, Q_COLS), lambda t: (t, 0)),
        out_shape=jax.ShapeDtypeStruct((rows, Q_COLS), jnp.bfloat16),
        scratch_shapes=[
            pltpu.VMEM((halo_rows + rows, HEAD_WIDTH), jnp.bfloat16),
            pltpu.VMEM((halo_rows + rows, HEAD_WIDTH), jnp.bfloat16),
        ],
        compiler_params=pltpu.CompilerParams(vmem_limit_bytes=VMEM_LIMIT),
        cost_estimate=pl.CostEstimate(
            flops=4 * rows * (reach + QUERY_TILE) * Q_COLS,
            bytes_accessed=rows * 4 * Q_COLS,
            transcendentals=rows * (reach + QUERY_TILE) * GROUP,
        ),
        name="attention",
    )(starts, packed, packed, halo)


def gain_kernel(gain_ref, weights_ref, gate_ref, up_ref):
    for which, out_ref in enumerate((gate_ref, up_ref)):
        out_ref[0] = (weights_ref[which].astype(jnp.float32) * gain_ref[...]).astype(jnp.bfloat16)


def scaled_gate_up(w_gate_up, gain, outer_count):
    _, rows, width = w_gate_up.shape
    cols = width // outer_count
    if cols % HEAD_WIDTH:
        wide = (w_gate_up.astype(jnp.float32) * gain[None]).astype(jnp.bfloat16)
        return jnp.transpose(wide.reshape(2, rows, outer_count, cols), (0, 2, 1, 3))
    return pl.pallas_call(
        gain_kernel,
        grid=(outer_count,),
        in_specs=[
            pl.BlockSpec((rows, 1), lambda p: (0, 0)),
            pl.BlockSpec((2, rows, cols), lambda p: (0, 0, p)),
        ],
        out_specs=[pl.BlockSpec((1, rows, cols), lambda p: (p, 0, 0))] * 2,
        out_shape=[jax.ShapeDtypeStruct((outer_count, rows, cols), jnp.bfloat16)] * 2,
        compiler_params=pltpu.CompilerParams(vmem_limit_bytes=VMEM_LIMIT),
        cost_estimate=pl.CostEstimate(flops=2 * rows * width, bytes_accessed=8 * rows * width, transcendentals=0),
        name="take_gain",
    )(gain, w_gate_up)


def projection_kernel(block_count, place_ref, *refs):
    blocks, weights_ref = refs[:block_count], refs[block_count]
    kept_ref, sent_ref = refs[block_count + 1 : block_count + 3]
    inner, head = place_ref[0], place_ref[1]
    half, depth = kept_ref.shape[0], blocks[0].shape[1]
    for e in range(sent_ref.shape[0] + 1):
        rows = pl.ds(pl.multiple_of((head ^ e) * half, half), half)
        total = jnp.zeros(kept_ref.shape, jnp.float32)
        for a, block in enumerate(blocks):
            at = pl.ds(pl.multiple_of((inner ^ a) * depth, depth), depth) if block_count > 1 else slice(None)
            total = total + jnp.dot(block[rows, :], weights_ref[at, :], preferred_element_type=jnp.float32)
        if e == 0:
            kept_ref[...] = total.astype(jnp.bfloat16)
        else:
            sent_ref[e - 1] = total.astype(jnp.bfloat16)
    if block_count > 1:
        context_ref = refs[block_count + 3]
        tokens = context_ref.shape[0]
        own = pl.ds(pl.multiple_of(inner * tokens, tokens), tokens)
        for a, block in enumerate(blocks):
            context_ref[:, pl.ds(pl.multiple_of((inner ^ a) * depth, depth), depth)] = block[own, :]


def projection(blocks, weights, place, head_count, inner_count):
    rows, depth = blocks[0].shape
    half, width = rows // head_count, weights.shape[1]
    outs = [(half, width), (head_count - 1, half, width)]
    if len(blocks) > 1:
        outs.append((rows // inner_count, len(blocks) * depth))
    return pl.pallas_call(
        functools.partial(projection_kernel, len(blocks)),
        in_specs=[SMEM] + [VMEM] * (len(blocks) + 1),
        out_specs=[VMEM] * len(outs),
        out_shape=[jax.ShapeDtypeStruct(shape, jnp.bfloat16) for shape in outs],
        compiler_params=pltpu.CompilerParams(vmem_limit_bytes=VMEM_LIMIT),
        cost_estimate=pl.CostEstimate(
            flops=2 * rows * weights.size, bytes_accessed=2 * (weights.size + rows * 2 * width), transcendentals=0
        ),
        name="projection",
    )(place, *blocks, weights)


def gate_up_kernel(block_count, *refs):
    tokens = refs[0]
    weights = refs[1 : 1 + 2 * block_count]
    out_ref, held, near, gate, up, token_sems, weight_sems = refs[1 + 2 * block_count :]
    depth = near.shape[1]
    copies = []
    for a in range(block_count):
        cols = slice(a * depth, (a + 1) * depth)
        copies.append(pltpu.make_async_copy(tokens.at[:, cols], held.at[:, cols], token_sems.at[a]))
        for j in (2 * a, 2 * a + 1):
            copies.append(pltpu.make_async_copy(weights[j], near.at[j], weight_sems.at[j]))
    for copy in copies:
        copy.start()
    for a in range(block_count):
        copies[3 * a].wait()
        for which, total in enumerate((gate, up)):
            copies[3 * a + 1 + which].wait()
            for rows in row_tiles(held.shape[0]):
                product = jnp.dot(
                    held[rows, a * depth : (a + 1) * depth], near[2 * a + which], preferred_element_type=jnp.float32
                )
                total[rows, :] = product if a == 0 else total[rows, :] + product
    for rows in row_tiles(held.shape[0]):
        out_ref[rows, :] = (gate[rows, :] / (1.0 + jnp.exp(-gate[rows, :])) * up[rows, :]).astype(jnp.bfloat16)


def gate_up(tokens, gates, ups):
    rows = tokens.shape[0]
    depth, cols = gates[0].shape
    weights = [block for pair in zip(gates, ups) for block in pair]
    return pl.pallas_call(
        functools.partial(gate_up_kernel, len(gates)),
        in_specs=[ANY] * (1 + len(weights)),
        out_specs=VMEM,
        out_shape=jax.ShapeDtypeStruct((rows, cols), jnp.bfloat16),
        scratch_shapes=[
            pltpu.VMEM((rows, depth * len(gates)), jnp.bfloat16),
            pltpu.VMEM((len(weights), depth, cols), jnp.bfloat16),
            pltpu.VMEM((rows, cols), jnp.float32),
            pltpu.VMEM((rows, cols), jnp.float32),
            pltpu.SemaphoreType.DMA((len(gates),)),
            pltpu.SemaphoreType.DMA((len(weights),)),
        ],
        compiler_params=pltpu.CompilerParams(vmem_limit_bytes=VMEM_LIMIT),
        cost_estimate=pl.CostEstimate(
            flops=4 * rows * depth * len(gates) * cols,
            bytes_accessed=2 * (rows * depth * len(gates) + len(weights) * depth * cols),
            transcendentals=rows * cols,
        ),
        name="gate_up",
    )(tokens, *weights)


def down_kernel(place_ref, activated_ref, weights_ref, kept_ref, sent_ref):
    sources, _, cols = weights_ref.shape
    head_count = sent_ref.shape[0] + 1
    head = place_ref[1]
    piece = kept_ref.shape[0] // sources
    for e in range(head_count):
        rows = []
        for o in range(sources):
            first = pl.multiple_of((o * head_count + (head ^ e)) * piece, piece)
            rows.append(activated_ref[pl.ds(first, piece), :])
        rows = jnp.concatenate(rows, axis=0)
        for s in range(sources):
            at = slice(s * cols, (s + 1) * cols)
            product = jnp.dot(rows, weights_ref[s], preferred_element_type=jnp.float32)
            if e == 0:
                kept_ref[:, at] = product.astype(jnp.bfloat16)
            else:
                sent_ref[e - 1, :, at] = product.astype(jnp.bfloat16)


def down_product(activated, weights, place, head_count):
    rows = activated.shape[0] // head_count
    sources, depth, cols = weights.shape
    return pl.pallas_call(
        down_kernel,
        in_specs=[SMEM, VMEM, VMEM],
        out_specs=[VMEM, VMEM],
        out_shape=[
            jax.ShapeDtypeStruct((rows, sources * cols), jnp.bfloat16),
            jax.ShapeDtypeStruct((head_count - 1, rows, sources * cols), jnp.bfloat16),
        ],
        compiler_params=pltpu.CompilerParams(vmem_limit_bytes=VMEM_LIMIT),
        cost_estimate=pl.CostEstimate(
            flops=2 * activated.size * sources * cols,
            bytes_accessed=2 * (activated.size + weights.size + head_count * rows * sources * cols),
            transcendentals=0,
        ),
        name="down",
    )(place, activated, weights)


def per_device(query, key, value, doc_lengths, resid, norm_gain, w_out, w_gate_up, w_down):
    inner_count = lax.axis_size("inner")
    outer_count = lax.axis_size("outer")
    head_count = lax.axis_size("head")
    outer, inner, head = lax.axis_index("outer"), lax.axis_index("inner"), lax.axis_index("head")
    rows = query.shape[0]
    plane_rows = rows * inner_count * head_count
    reach = plane_rows * outer_count // WINDOW_PER_DOC
    feature_rows = w_gate_up.shape[1]
    hidden_cols = w_gate_up.shape[2] // outer_count
    bounds = jnp.cumsum(doc_lengths)
    hops = reach // plane_rows
    token_rows = plane_rows // inner_count
    half = plane_rows // head_count
    packing = (rows, head_count, KEY_VALUE_HEADS // head_count, -1)

    weights_out = lax.all_gather(w_out, "outer", axis=1, tiled=True)
    own_gain = lax.dynamic_slice_in_dim(norm_gain, outer * feature_rows, feature_rows, 0)
    w_gate, w_up = scaled_gate_up(w_gate_up, own_gain[:, None], outer_count)
    if packing[2] == inner_count and hops == 1:
        earlier = [lax.ppermute(part, "outer", [(s, s + 1) for s in range(outer_count - 1)]) for part in (key, value)]
        groups = jnp.concatenate([part.reshape(packing) for part in (query, key, value, *earlier)], axis=3)
        groups = jnp.transpose(groups, (2, 1, 0, 3)).reshape(inner_count * head_count, rows, -1)
        packed = lax.all_to_all(groups, ("inner", "head"), split_axis=0, concat_axis=0, tiled=True)
        packed = packed.reshape(plane_rows, -1)
        starts = document_starts(bounds, outer * plane_rows, plane_rows)
        own_context = attention(packed, packed, Q_COLS // KV_COLS + 1, starts, reach)
        blocks = blocks_over_inner(own_context)
    else:
        groups = jnp.concatenate([part.reshape(packing) for part in (query, key, value)], axis=3)
        groups = jnp.transpose(groups[:, :, 0], (1, 0, 2))
        packed = lax.all_to_all(groups, "head", split_axis=0, concat_axis=0, tiled=True).reshape(token_rows, -1)
        plane_kv = lax.all_gather(packed[:, Q_COLS:], "inner", axis=0, tiled=True)
        every_kv = jnp.concatenate([earlier_planes(plane_kv, hops), plane_kv], axis=0)
        halo = lax.dynamic_slice_in_dim(every_kv, inner * token_rows, reach, 0)
        starts = document_starts(bounds, outer * plane_rows + inner * token_rows, token_rows)
        own_context = attention(packed, halo, 0, starts, reach)
        blocks = [lax.all_gather(own_context, "inner", axis=0, tiled=True)]

    place = jnp.stack([inner, head]).astype(jnp.int32)
    kept, sent, *whole = projection(blocks, weights_out, place, head_count, inner_count)
    context = whole[0] if whole else own_context
    projected = kept.astype(jnp.float32)
    for e in range(1, head_count):
        projected = projected + swap(sent[e - 1], "head", e).astype(jnp.float32)
    own_resid = lax.dynamic_slice_in_dim(resid, head * half, half, 0)
    hidden_part = (own_resid.astype(jnp.float32) + projected).astype(jnp.bfloat16)

    own_rows = half // inner_count
    state = []
    for a in range(inner_count):
        block = lax.dynamic_slice_in_dim(hidden_part, (inner ^ a) * own_rows, own_rows, 0)
        state.append(swap(block, "inner", a).astype(jnp.float32))
    squares = sum([jnp.sum(block * block, axis=1, keepdims=True) for block in state])
    inverse = lax.rsqrt(squares / D + 1e-05)
    normed = jnp.concatenate([block * inverse for block in state], axis=1).astype(jnp.bfloat16)
    tokens = lax.all_gather(normed, ("outer", "head"), axis=0, tiled=True)

    spread = functools.partial(lax.all_to_all, axis_name="outer", split_axis=0, concat_axis=0, tiled=True)
    gate_here = spread(after(w_gate, kept))
    up_here = spread(after(w_up, hidden_part))
    down_here = spread(after(w_down.reshape(outer_count, hidden_cols, feature_rows), tokens))
    gates = blocks_over_inner(after(gate_here, normed).reshape(-1, hidden_cols))
    ups = blocks_over_inner(after(up_here, normed).reshape(-1, hidden_cols))
    downs = blocks_over_inner(down_here)

    activated = gate_up(tokens, gates, ups)
    layer_out = jnp.zeros((half, D // inner_count), jnp.bfloat16)
    for a in range(inner_count):
        kept, sent = down_product(activated, downs[a], place, head_count)
        paired = kept.astype(jnp.float32)
        for e in range(1, head_count):
            paired = paired + swap(sent[e - 1], "head", e).astype(jnp.float32)
        paired = paired.reshape(outer_count, own_rows, -1)
        total = state[a] + lax.dynamic_index_in_dim(paired, outer, 0, False)
        for d in range(1, outer_count):
            sent = lax.dynamic_index_in_dim(paired, outer ^ d, 0, False).astype(jnp.bfloat16)
            total = total + swap(sent, "outer", d).astype(jnp.float32)
        block = swap(total.astype(jnp.bfloat16), "inner", a)
        layer_out = lax.dynamic_update_slice(layer_out, block, ((inner ^ a) * own_rows, 0))
    return (context, layer_out)


def solution(mesh):
    placed = (
        P(("outer", "inner", "head"), None),
        P(("outer", "inner", "head"), None),
        P(("outer", "inner", "head"), None),
        P(),
        P("outer", "inner"),
        P("inner"),
        P("head", ("inner", "outer")),
        P(None, ("inner", "outer"), "head"),
        P("head", ("inner", "outer")),
    )
    return jax.shard_map(
        per_device,
        mesh=mesh,
        in_specs=placed,
        out_specs=(P(("outer", "inner"), "head"), P(("outer", "head"), "inner")),
        check_vma=False,
    )
```

```python
import functools

import jax
import jax.numpy as jnp
from jax import lax
from jax.experimental import pallas as pl
from jax.experimental.pallas import tpu as pltpu
from jax.sharding import PartitionSpec as P

D = 4096
QUERY_HEADS = 32
KEY_VALUE_HEADS = 8
HEAD_WIDTH = 128
GROUP = QUERY_HEADS // KEY_VALUE_HEADS
Q_COLS = GROUP * HEAD_WIDTH
KV_COLS = 2 * HEAD_WIDTH
WINDOW_PER_DOC = 4
QUERY_TILE = 128
ROW_TILE = 256
PARTS = 2
VMEM_LIMIT = 48 * 1024 * 1024
ANY = pl.BlockSpec(memory_space=pl.ANY)
VMEM = pl.BlockSpec(memory_space=pltpu.VMEM)
SMEM = pl.BlockSpec(memory_space=pltpu.SMEM)


def swap(array, axis, distance):
    if distance == 0:
        return array
    count = lax.axis_size(axis)
    return lax.ppermute(array, axis, [(s, s ^ distance) for s in range(count)])


def after(array, earlier):
    return lax.optimization_barrier((array, earlier))[0]


def blocks_over_inner(block):
    across = swap(block, "inner", 2)
    return [block, swap(block, "inner", 1), across, swap(across, "inner", 1)]


def earlier_planes(kv, hops):
    count = lax.axis_size("outer")
    moved = [lax.ppermute(kv, "outer", [(s, s + d) for s in range(count - d)]) for d in range(hops, 0, -1)]
    return jnp.concatenate(moved, axis=0)


def document_starts(bounds, first, rows):
    place = first + jnp.arange(rows, dtype=jnp.int32)
    starts = jnp.max(jnp.where(bounds[None, :] <= place[:, None], bounds[None, :], 0), axis=1) - first
    return starts[:, None].astype(jnp.int32)


def row_tiles(rows):
    step = ROW_TILE if rows % ROW_TILE == 0 else rows
    return [slice(at, at + step) for at in range(0, rows, step)]


def attention_kernel(halo_rows, reach, starts_ref, queries_ref, own_ref, halo_ref, out_ref, keys, values):
    tile = pl.program_id(0)
    rows = queries_ref.shape[0]
    span = reach + rows

    @pl.when(tile == 0)
    def _():
        keys[:halo_rows, :] = halo_ref[:, :HEAD_WIDTH]
        values[:halo_rows, :] = halo_ref[:, HEAD_WIDTH:]
        keys[halo_rows:, :] = own_ref[:, :HEAD_WIDTH]
        values[halo_rows:, :] = own_ref[:, HEAD_WIDTH:]

    first = pl.multiple_of(tile * rows + (halo_rows - reach), rows)
    near_keys = keys[pl.ds(first, span), :]
    near_values = values[pl.ds(first, span), :]
    key_place = lax.broadcasted_iota(jnp.int32, (rows, span), 1)
    query_place = lax.broadcasted_iota(jnp.int32, (rows, span), 0) + reach
    start = starts_ref[...] - (first - halo_rows)
    allowed = (key_place <= query_place) & (key_place >= start)
    for g in range(GROUP):
        cols = slice(g * HEAD_WIDTH, (g + 1) * HEAD_WIDTH)
        scores = lax.dot_general(
            queries_ref[:, cols], near_keys, (((1,), (1,)), ((), ())), preferred_element_type=jnp.float32
        ) * (HEAD_WIDTH ** (-0.5))
        masked = jnp.where(allowed, scores, -1e30)
        row_max = jnp.max(masked, axis=1, keepdims=True)
        weights = jnp.exp(masked - row_max)
        totals = jnp.sum(weights, axis=1, keepdims=True)
        summed = jnp.dot(weights.astype(jnp.bfloat16), near_values, preferred_element_type=jnp.float32)
        out_ref[:, cols] = (summed / totals).astype(jnp.bfloat16)


def attention(packed, halo, halo_at, starts, reach):
    rows = packed.shape[0]
    halo_rows = halo.shape[0]
    return pl.pallas_call(
        functools.partial(attention_kernel, halo_rows, reach),
        grid=(rows // QUERY_TILE,),
        in_specs=[
            pl.BlockSpec((QUERY_TILE, 1), lambda t: (t, 0)),
            pl.BlockSpec((QUERY_TILE, Q_COLS), lambda t: (t, 0)),
            pl.BlockSpec((rows, KV_COLS), lambda t: (0, Q_COLS // KV_COLS)),
            pl.BlockSpec((halo_rows, KV_COLS), lambda t: (0, halo_at)),
        ],
        out_specs=pl.BlockSpec((QUERY_TILE, Q_COLS), lambda t: (t, 0)),
        out_shape=jax.ShapeDtypeStruct((rows, Q_COLS), jnp.bfloat16),
        scratch_shapes=[
            pltpu.VMEM((halo_rows + rows, HEAD_WIDTH), jnp.bfloat16),
            pltpu.VMEM((halo_rows + rows, HEAD_WIDTH), jnp.bfloat16),
        ],
        compiler_params=pltpu.CompilerParams(vmem_limit_bytes=VMEM_LIMIT),
        cost_estimate=pl.CostEstimate(
            flops=4 * rows * (reach + QUERY_TILE) * Q_COLS,
            bytes_accessed=rows * 4 * Q_COLS,
            transcendentals=rows * (reach + QUERY_TILE) * GROUP,
        ),
        name="attention",
    )(starts, packed, packed, halo)


def cut_kernel(gain_ref, gate_up_ref, down_ref, *out_refs):
    rows, cols = out_refs[0].shape[1], out_refs[-1].shape[2]
    for part in range(PARTS):
        at = slice(part * rows, (part + 1) * rows)
        for which in range(2):
            scaled = gate_up_ref[which, at].astype(jnp.float32) * gain_ref[at]
            out_refs[2 * part + which][0] = scaled.astype(jnp.bfloat16)
        out_refs[2 * PARTS + part][0] = down_ref[:, part * cols : (part + 1) * cols]


def cut_weights(w_gate_up, w_down, gain, outer_count):
    _, features, width = w_gate_up.shape
    cols = width // outer_count
    rows = features // PARTS
    if cols % HEAD_WIDTH:
        wide = (w_gate_up.astype(jnp.float32) * gain[None]).astype(jnp.bfloat16)
        wide = jnp.transpose(wide.reshape(2, PARTS, rows, outer_count, cols), (1, 0, 3, 2, 4))
        tall = jnp.transpose(w_down.reshape(outer_count, cols, PARTS, rows), (2, 0, 1, 3))
        return [wide[part, which] for part in range(PARTS) for which in range(2)] + [tall[part] for part in range(PARTS)]
    return pl.pallas_call(
        cut_kernel,
        grid=(outer_count,),
        in_specs=[
            pl.BlockSpec((features, 1), lambda p: (0, 0)),
            pl.BlockSpec((2, features, cols), lambda p: (0, 0, p)),
            pl.BlockSpec((cols, features), lambda p: (p, 0)),
        ],
        out_specs=[pl.BlockSpec((1, rows, cols), lambda p: (p, 0, 0))] * (2 * PARTS)
        + [pl.BlockSpec((1, cols, rows), lambda p: (p, 0, 0))] * PARTS,
        out_shape=[jax.ShapeDtypeStruct((outer_count, rows, cols), jnp.bfloat16)] * (2 * PARTS)
        + [jax.ShapeDtypeStruct((outer_count, cols, rows), jnp.bfloat16)] * PARTS,
        compiler_params=pltpu.CompilerParams(vmem_limit_bytes=VMEM_LIMIT),
        cost_estimate=pl.CostEstimate(flops=2 * features * width, bytes_accessed=12 * features * width, transcendentals=0),
        name="cut_weights",
    )(gain, w_gate_up, w_down)


def projection_kernel(block_count, place_ref, *refs):
    blocks, weights_ref = refs[:block_count], refs[block_count]
    kept_ref, sent_ref = refs[block_count + 1 : block_count + 3]
    inner, head = place_ref[0], place_ref[1]
    half, depth = kept_ref.shape[0], blocks[0].shape[1]
    for e in range(sent_ref.shape[0] + 1):
        rows = pl.ds(pl.multiple_of((head ^ e) * half, half), half)
        total = jnp.zeros(kept_ref.shape, jnp.float32)
        for a, block in enumerate(blocks):
            at = pl.ds(pl.multiple_of((inner ^ a) * depth, depth), depth) if block_count > 1 else slice(None)
            total = total + jnp.dot(block[rows, :], weights_ref[at, :], preferred_element_type=jnp.float32)
        if e == 0:
            kept_ref[...] = total.astype(jnp.bfloat16)
        else:
            sent_ref[e - 1] = total.astype(jnp.bfloat16)
    if block_count > 1:
        context_ref = refs[block_count + 3]
        tokens = context_ref.shape[0]
        own = pl.ds(pl.multiple_of(inner * tokens, tokens), tokens)
        for a, block in enumerate(blocks):
            context_ref[:, pl.ds(pl.multiple_of((inner ^ a) * depth, depth), depth)] = block[own, :]


def projection(blocks, weights, place, head_count, inner_count):
    rows, depth = blocks[0].shape
    half, width = rows // head_count, weights.shape[1]
    outs = [(half, width), (head_count - 1, half, width)]
    if len(blocks) > 1:
        outs.append((rows // inner_count, len(blocks) * depth))
    return pl.pallas_call(
        functools.partial(projection_kernel, len(blocks)),
        in_specs=[SMEM] + [VMEM] * (len(blocks) + 1),
        out_specs=[VMEM] * len(outs),
        out_shape=[jax.ShapeDtypeStruct(shape, jnp.bfloat16) for shape in outs],
        compiler_params=pltpu.CompilerParams(vmem_limit_bytes=VMEM_LIMIT),
        cost_estimate=pl.CostEstimate(
            flops=2 * rows * weights.size, bytes_accessed=2 * (weights.size + rows * 2 * width), transcendentals=0
        ),
        name="projection",
    )(place, *blocks, weights)


def gate_up_kernel(block_count, tokens, *refs):
    weights = refs[: 2 * PARTS * block_count]
    out_ref, held, near, sums, token_sems, weight_sems = refs[2 * PARTS * block_count :]
    rows, depth = weights[0].shape[0], weights[0].shape[0] * PARTS
    copies = []
    for a in range(block_count):
        cols = slice(a * depth, (a + 1) * depth)
        copies.append([pltpu.make_async_copy(tokens.at[:, cols], held.at[:, cols], token_sems.at[a])])
        for j in range(2 * PARTS * a, 2 * PARTS * (a + 1)):
            part, which = (j // 2) % PARTS, j % 2
            target = near.at[which, pl.ds(a * depth + part * rows, rows)]
            copies[a].append(pltpu.make_async_copy(weights[j], target, weight_sems.at[j]))
    for group in copies:
        for copy in group:
            copy.start()
    for a, group in enumerate(copies):
        for copy in group:
            copy.wait()
        at = slice(a * depth, (a + 1) * depth)
        for which in range(2):
            for tile in row_tiles(held.shape[0]):
                product = jnp.dot(held[tile, at], near[which, at], preferred_element_type=jnp.float32)
                total = product if a == 0 else sums[which, tile, :] + product
                if a < block_count - 1:
                    sums[which, tile, :] = total
                else:
                    out_ref[which, tile, :] = total.astype(jnp.bfloat16)


def gate_up(tokens, blocks):
    rows = tokens.shape[0]
    weights = [stream for block in blocks for stream in block]
    depth, cols = weights[0].shape
    depth = depth * PARTS * len(blocks)
    return pl.pallas_call(
        functools.partial(gate_up_kernel, len(blocks)),
        in_specs=[ANY] * (1 + len(weights)),
        out_specs=VMEM,
        out_shape=jax.ShapeDtypeStruct((2, rows, cols), jnp.bfloat16),
        scratch_shapes=[
            pltpu.VMEM((rows, depth), jnp.bfloat16),
            pltpu.VMEM((2, depth, cols), jnp.bfloat16),
            pltpu.VMEM((2, rows, cols), jnp.float32),
            pltpu.SemaphoreType.DMA((len(blocks),)),
            pltpu.SemaphoreType.DMA((len(weights),)),
        ],
        compiler_params=pltpu.CompilerParams(vmem_limit_bytes=VMEM_LIMIT),
        cost_estimate=pl.CostEstimate(
            flops=4 * rows * depth * cols,
            bytes_accessed=2 * (rows * depth + 2 * depth * cols + 2 * rows * cols),
            transcendentals=0,
        ),
        name="gate_up",
    )(tokens, *weights)


def activation_kernel(here_ref, there_ref, out_ref):
    gate = here_ref[0].astype(jnp.float32) + there_ref[0].astype(jnp.float32)
    up = here_ref[1].astype(jnp.float32) + there_ref[1].astype(jnp.float32)
    out_ref[...] = (gate / (1.0 + jnp.exp(-gate)) * up).astype(jnp.bfloat16)


def activation(here, there):
    _, rows, cols = here.shape
    step = min(rows, ROW_TILE)
    return pl.pallas_call(
        activation_kernel,
        grid=(rows // step,),
        in_specs=[pl.BlockSpec((2, step, cols), lambda t: (0, t, 0))] * 2,
        out_specs=pl.BlockSpec((step, cols), lambda t: (t, 0)),
        out_shape=jax.ShapeDtypeStruct((rows, cols), jnp.bfloat16),
        compiler_params=pltpu.CompilerParams(vmem_limit_bytes=VMEM_LIMIT),
        cost_estimate=pl.CostEstimate(flops=8 * rows * cols, bytes_accessed=10 * rows * cols, transcendentals=rows * cols),
        name="activation",
    )(here, there)


def down_kernel(place_ref, activated_ref, weights_ref, kept_ref, sent_ref):
    sources, _, cols = weights_ref.shape
    head_count = sent_ref.shape[0] + 1
    head = place_ref[1]
    piece = kept_ref.shape[0] // sources
    if cols % HEAD_WIDTH:
        blocks = [weights_ref[s] for s in range(sources)]
    else:
        blocks = [jnp.concatenate([weights_ref[s] for s in range(sources)], axis=1)]
    for e in range(head_count):
        rows = []
        for o in range(sources):
            first = pl.multiple_of((o * head_count + (head ^ e)) * piece, piece)
            rows.append(activated_ref[pl.ds(first, piece), :])
        rows = jnp.concatenate(rows, axis=0)
        for s, block in enumerate(blocks):
            at = slice(s * block.shape[1], (s + 1) * block.shape[1])
            product = jnp.dot(rows, block, preferred_element_type=jnp.float32)
            if e == 0:
                kept_ref[:, at] = product.astype(jnp.bfloat16)
            else:
                sent_ref[e - 1, :, at] = product.astype(jnp.bfloat16)


def down_product(activated, weights, place, head_count):
    rows = activated.shape[0] // head_count
    sources, depth, cols = weights.shape
    return pl.pallas_call(
        down_kernel,
        in_specs=[SMEM, VMEM, VMEM],
        out_specs=[VMEM, VMEM],
        out_shape=[
            jax.ShapeDtypeStruct((rows, sources * cols), jnp.bfloat16),
            jax.ShapeDtypeStruct((head_count - 1, rows, sources * cols), jnp.bfloat16),
        ],
        compiler_params=pltpu.CompilerParams(vmem_limit_bytes=VMEM_LIMIT),
        cost_estimate=pl.CostEstimate(
            flops=2 * activated.size * sources * cols,
            bytes_accessed=2 * (activated.size + weights.size + head_count * rows * sources * cols),
            transcendentals=0,
        ),
        name="down",
    )(place, activated, weights)


def per_device(query, key, value, doc_lengths, resid, norm_gain, w_out, w_gate_up, w_down):
    inner_count = lax.axis_size("inner")
    outer_count = lax.axis_size("outer")
    head_count = lax.axis_size("head")
    outer, inner, head = lax.axis_index("outer"), lax.axis_index("inner"), lax.axis_index("head")
    rows = query.shape[0]
    plane_rows = rows * inner_count * head_count
    reach = plane_rows * outer_count // WINDOW_PER_DOC
    feature_rows = w_gate_up.shape[1]
    hidden_cols = w_gate_up.shape[2] // outer_count
    bounds = jnp.cumsum(doc_lengths)
    hops = reach // plane_rows
    token_rows = plane_rows // inner_count
    half = plane_rows // head_count
    packing = (rows, head_count, KEY_VALUE_HEADS // head_count, -1)

    weights_out = lax.all_gather(w_out, "outer", axis=1, tiled=True)
    if packing[2] == inner_count and hops == 1:
        earlier = [lax.ppermute(part, "outer", [(s, s + 1) for s in range(outer_count - 1)]) for part in (key, value)]
        groups = jnp.concatenate([part.reshape(packing) for part in (query, key, value, *earlier)], axis=3)
        groups = jnp.transpose(groups, (2, 1, 0, 3)).reshape(inner_count * head_count, rows, -1)
        packed = lax.all_to_all(groups, ("inner", "head"), split_axis=0, concat_axis=0, tiled=True)
        packed = packed.reshape(plane_rows, -1)
        starts = document_starts(bounds, outer * plane_rows, plane_rows)
        own_context = attention(packed, packed, Q_COLS // KV_COLS + 1, starts, reach)
        blocks = blocks_over_inner(own_context)
    else:
        groups = jnp.concatenate([part.reshape(packing) for part in (query, key, value)], axis=3)
        groups = jnp.transpose(groups[:, :, 0], (1, 0, 2))
        packed = lax.all_to_all(groups, "head", split_axis=0, concat_axis=0, tiled=True).reshape(token_rows, -1)
        plane_kv = lax.all_gather(packed[:, Q_COLS:], "inner", axis=0, tiled=True)
        every_kv = jnp.concatenate([earlier_planes(plane_kv, hops), plane_kv], axis=0)
        halo = lax.dynamic_slice_in_dim(every_kv, inner * token_rows, reach, 0)
        starts = document_starts(bounds, outer * plane_rows + inner * token_rows, token_rows)
        own_context = attention(packed, halo, 0, starts, reach)
        blocks = [lax.all_gather(own_context, "inner", axis=0, tiled=True)]

    spread = functools.partial(lax.all_to_all, axis_name="outer", split_axis=0, concat_axis=0, tiled=True)
    over_y = functools.partial(swap, axis="inner", distance=2)
    fence = lambda *arrays: lax.optimization_barrier(arrays)
    own_gain = lax.dynamic_slice_in_dim(norm_gain, outer * feature_rows, feature_rows, 0)
    cut = cut_weights(w_gate_up, w_down, own_gain[:, None], outer_count)

    place = jnp.stack([inner, head]).astype(jnp.int32)
    first = spread(after(cut[0], weights_out))
    kept, sent, *whole = projection(blocks, weights_out, place, head_count, inner_count)
    context = whole[0] if whole else own_context
    projected = kept.astype(jnp.float32)
    for e in range(1, head_count):
        projected = projected + swap(sent[e - 1], "head", e).astype(jnp.float32)
    projected, first = fence(projected, first)
    own_resid = lax.dynamic_slice_in_dim(resid, head * half, half, 0)
    hidden_part = (own_resid.astype(jnp.float32) + projected).astype(jnp.bfloat16)

    second = spread(after(cut[1], first))
    upper = inner // 2
    own_rows = half // 2
    mine = lax.dynamic_slice_in_dim(hidden_part, upper * own_rows, own_rows, 0)
    others = lax.dynamic_slice_in_dim(hidden_part, (1 - upper) * own_rows, own_rows, 0)
    state = [mine.astype(jnp.float32), over_y(others).astype(jnp.float32)]
    squares = sum([jnp.sum(block * block, axis=1) for block in state])
    squares = squares + swap(squares, "inner", 1)
    inverse = lax.rsqrt(squares / D + 1e-05)[:, None]
    part_rows = feature_rows // PARTS
    normed = jnp.stack([block * inverse for block in state], axis=1).astype(jnp.bfloat16)
    normed = normed.reshape(own_rows, 2, outer_count, PARTS, part_rows)
    normed = jnp.transpose(normed, (0, 1, 3, 2, 4)).reshape(own_rows, 2 * feature_rows * outer_count)
    normed, first, second = fence(normed, first, second)
    tokens = lax.all_gather(normed, ("outer", "head"), axis=0, tiled=True)

    third, first_y, second_y = fence(spread(after(cut[2], normed)), over_y(first), over_y(second))
    fourth, third_y = fence(spread(after(cut[3], third)), over_y(third))
    fifth, fourth_y = fence(spread(after(cut[4], fourth)), over_y(fourth))
    sixth, fifth_y = fence(spread(after(cut[5], fifth)), over_y(fifth))
    here = [first, second, third, fourth]
    there = [first_y, second_y, third_y, fourth_y]
    flat = [[stream.reshape(-1, hidden_cols) for stream in streams] for streams in (here, there)]
    sums = gate_up(tokens, flat)
    activated = activation(sums, swap(sums, "inner", 1))

    downs = [[fifth, sixth], [fifth_y, over_y(sixth)]]
    pieces = [[None] * PARTS, [None] * PARTS]
    for part in range(PARTS):
        for a in range(2):
            kept, sent = down_product(activated, downs[a][part], place, head_count)
            paired = kept.astype(jnp.float32)
            for e in range(1, head_count):
                paired = paired + swap(sent[e - 1], "head", e).astype(jnp.float32)
            paired = paired.reshape(outer_count, own_rows, -1)
            total = lax.dynamic_index_in_dim(paired, outer, 0, False)
            for d in range(1, outer_count):
                sent = lax.dynamic_index_in_dim(paired, outer ^ d, 0, False).astype(jnp.bfloat16)
                total = total + swap(sent, "outer", d).astype(jnp.float32)
            near = state[a].reshape(own_rows, outer_count, PARTS, part_rows)[:, :, part]
            total = (near.reshape(own_rows, -1) + total).astype(jnp.bfloat16)
            pieces[a][part] = (over_y(total) if a else total).reshape(own_rows, outer_count, 1, part_rows)
    halves = [jnp.concatenate(parts, axis=2).reshape(own_rows, -1) for parts in pieces]
    layer_out = jnp.zeros((half, halves[0].shape[1]), jnp.bfloat16)
    layer_out = lax.dynamic_update_slice(layer_out, halves[0], (upper * own_rows, 0))
    layer_out = lax.dynamic_update_slice(layer_out, halves[1], ((1 - upper) * own_rows, 0))
    return (context, layer_out)


def solution(mesh):
    placed = (
        P(("outer", "inner", "head"), None),
        P(("outer", "inner", "head"), None),
        P(("outer", "inner", "head"), None),
        P(),
        P("outer", "inner"),
        P("inner"),
        P("head", ("inner", "outer")),
        P(None, ("inner", "outer"), "head"),
        P("head", ("inner", "outer")),
    )
    return jax.shard_map(
        per_device,
        mesh=mesh,
        in_specs=placed,
        out_specs=(P(("outer", "inner"), "head"), P(("outer", "head"), "inner")),
        check_vma=False,
    )
```

```python
import functools

import jax
import jax.numpy as jnp
from jax import lax
from jax.experimental import pallas as pl
from jax.experimental.pallas import tpu as pltpu
from jax.sharding import PartitionSpec as P

D = 4096
QUERY_HEADS = 32
KEY_VALUE_HEADS = 8
HEAD_WIDTH = 128
GROUP = QUERY_HEADS // KEY_VALUE_HEADS
Q_COLS = GROUP * HEAD_WIDTH
KV_COLS = 2 * HEAD_WIDTH
WINDOW_PER_DOC = 4
QUERY_TILE = 128
ROW_TILE = 256
PARTS = 2
VMEM_LIMIT = 48 * 1024 * 1024
ANY = pl.BlockSpec(memory_space=pl.ANY)
VMEM = pl.BlockSpec(memory_space=pltpu.VMEM)
SMEM = pl.BlockSpec(memory_space=pltpu.SMEM)


def swap(array, axis, distance, only=None):
    if distance == 0:
        return array
    members = range(lax.axis_size(axis)) if only is None else only
    return lax.ppermute(array, axis, [(s, s ^ distance) for s in members])


def after(array, earlier):
    return lax.optimization_barrier((array, earlier))[0]


def blocks_over_inner(block):
    across = swap(block, "inner", 2)
    return [block, swap(block, "inner", 1), across, swap(across, "inner", 1)]


def earlier_planes(kv, hops):
    count = lax.axis_size("outer")
    moved = [lax.ppermute(kv, "outer", [(s, s + d) for s in range(count - d)]) for d in range(hops, 0, -1)]
    return jnp.concatenate(moved, axis=0)


def document_starts(bounds, first, rows):
    place = first + jnp.arange(rows, dtype=jnp.int32)
    starts = jnp.max(jnp.where(bounds[None, :] <= place[:, None], bounds[None, :], 0), axis=1) - first
    return starts[:, None].astype(jnp.int32)


def row_tiles(rows):
    step = ROW_TILE if rows % ROW_TILE == 0 else rows
    return [slice(at, at + step) for at in range(0, rows, step)]


def attention_kernel(halo_rows, reach, starts_ref, queries_ref, own_ref, halo_ref, out_ref, keys, values):
    tile = pl.program_id(0)
    rows = queries_ref.shape[0]
    span = reach + rows

    @pl.when(tile == 0)
    def _():
        keys[:halo_rows, :] = halo_ref[:, :HEAD_WIDTH]
        values[:halo_rows, :] = halo_ref[:, HEAD_WIDTH:]
        keys[halo_rows:, :] = own_ref[:, :HEAD_WIDTH]
        values[halo_rows:, :] = own_ref[:, HEAD_WIDTH:]

    first = pl.multiple_of(tile * rows + (halo_rows - reach), rows)
    near_keys = keys[pl.ds(first, span), :]
    near_values = values[pl.ds(first, span), :]
    key_place = lax.broadcasted_iota(jnp.int32, (rows, span), 1)
    query_place = lax.broadcasted_iota(jnp.int32, (rows, span), 0) + reach
    start = starts_ref[...] - (first - halo_rows)
    allowed = (key_place <= query_place) & (key_place >= start)
    for g in range(GROUP):
        cols = slice(g * HEAD_WIDTH, (g + 1) * HEAD_WIDTH)
        scores = lax.dot_general(
            queries_ref[:, cols], near_keys, (((1,), (1,)), ((), ())), preferred_element_type=jnp.float32
        ) * (HEAD_WIDTH ** (-0.5))
        masked = jnp.where(allowed, scores, -1e30)
        row_max = jnp.max(masked, axis=1, keepdims=True)
        weights = jnp.exp(masked - row_max)
        totals = jnp.sum(weights, axis=1, keepdims=True)
        summed = jnp.dot(weights.astype(jnp.bfloat16), near_values, preferred_element_type=jnp.float32)
        out_ref[:, cols] = (summed / totals).astype(jnp.bfloat16)


def attention(packed, halo, halo_at, starts, reach):
    rows = packed.shape[0]
    halo_rows = halo.shape[0]
    return pl.pallas_call(
        functools.partial(attention_kernel, halo_rows, reach),
        grid=(rows // QUERY_TILE,),
        in_specs=[
            pl.BlockSpec((QUERY_TILE, 1), lambda t: (t, 0)),
            pl.BlockSpec((QUERY_TILE, Q_COLS), lambda t: (t, 0)),
            pl.BlockSpec((rows, KV_COLS), lambda t: (0, Q_COLS // KV_COLS)),
            pl.BlockSpec((halo_rows, KV_COLS), lambda t: (0, halo_at)),
        ],
        out_specs=pl.BlockSpec((QUERY_TILE, Q_COLS), lambda t: (t, 0)),
        out_shape=jax.ShapeDtypeStruct((rows, Q_COLS), jnp.bfloat16),
        scratch_shapes=[
            pltpu.VMEM((halo_rows + rows, HEAD_WIDTH), jnp.bfloat16),
            pltpu.VMEM((halo_rows + rows, HEAD_WIDTH), jnp.bfloat16),
        ],
        compiler_params=pltpu.CompilerParams(vmem_limit_bytes=VMEM_LIMIT),
        cost_estimate=pl.CostEstimate(
            flops=4 * rows * (reach + QUERY_TILE) * Q_COLS,
            bytes_accessed=rows * 4 * Q_COLS,
            transcendentals=rows * (reach + QUERY_TILE) * GROUP,
        ),
        name="attention",
    )(starts, packed, packed, halo)


def gain_kernel(gain_ref, weights_ref, out_ref):
    for which in range(2):
        out_ref[0, which] = (weights_ref[which].astype(jnp.float32) * gain_ref[...]).astype(jnp.bfloat16)


def take_gain(w_gate_up, gain, outer_count):
    _, rows, width = w_gate_up.shape
    cols = width // outer_count
    if cols % HEAD_WIDTH:
        wide = (w_gate_up.astype(jnp.float32) * gain[None]).astype(jnp.bfloat16)
        return jnp.transpose(wide.reshape(2, rows, outer_count, cols), (2, 0, 1, 3))
    return pl.pallas_call(
        gain_kernel,
        grid=(outer_count,),
        in_specs=[
            pl.BlockSpec((rows, 1), lambda p: (0, 0)),
            pl.BlockSpec((2, rows, cols), lambda p: (0, 0, p)),
        ],
        out_specs=pl.BlockSpec((1, 2, rows, cols), lambda p: (p, 0, 0, 0)),
        out_shape=jax.ShapeDtypeStruct((outer_count, 2, rows, cols), jnp.bfloat16),
        compiler_params=pltpu.CompilerParams(vmem_limit_bytes=VMEM_LIMIT),
        cost_estimate=pl.CostEstimate(flops=2 * rows * width, bytes_accessed=8 * rows * width, transcendentals=0),
        name="take_gain",
    )(gain, w_gate_up)


def projection_kernel(block_count, place_ref, *refs):
    blocks, weights_ref = refs[:block_count], refs[block_count]
    kept_ref, sent_ref = refs[block_count + 1 : block_count + 3]
    inner, head = place_ref[0], place_ref[1]
    half, depth = kept_ref.shape[0], blocks[0].shape[1]
    for e in range(sent_ref.shape[0] + 1):
        rows = pl.ds(pl.multiple_of((head ^ e) * half, half), half)
        total = jnp.zeros(kept_ref.shape, jnp.float32)
        for a, block in enumerate(blocks):
            at = pl.ds(pl.multiple_of((inner ^ a) * depth, depth), depth) if block_count > 1 else slice(None)
            total = total + jnp.dot(block[rows, :], weights_ref[at, :], preferred_element_type=jnp.float32)
        if e == 0:
            kept_ref[...] = total.astype(jnp.bfloat16)
        else:
            sent_ref[e - 1] = total.astype(jnp.bfloat16)
    if block_count > 1:
        context_ref = refs[block_count + 3]
        tokens = context_ref.shape[0]
        own = pl.ds(pl.multiple_of(inner * tokens, tokens), tokens)
        for a, block in enumerate(blocks):
            context_ref[:, pl.ds(pl.multiple_of((inner ^ a) * depth, depth), depth)] = block[own, :]


def projection(blocks, weights, place, head_count, inner_count):
    rows, depth = blocks[0].shape
    half, width = rows // head_count, weights.shape[1]
    outs = [(half, width), (head_count - 1, half, width)]
    if len(blocks) > 1:
        outs.append((rows // inner_count, len(blocks) * depth))
    return pl.pallas_call(
        functools.partial(projection_kernel, len(blocks)),
        in_specs=[SMEM] + [VMEM] * (len(blocks) + 1),
        out_specs=[VMEM] * len(outs),
        out_shape=[jax.ShapeDtypeStruct(shape, jnp.bfloat16) for shape in outs],
        compiler_params=pltpu.CompilerParams(vmem_limit_bytes=VMEM_LIMIT),
        cost_estimate=pl.CostEstimate(
            flops=2 * rows * weights.size, bytes_accessed=2 * (weights.size + rows * 2 * width), transcendentals=0
        ),
        name="projection",
    )(place, *blocks, weights)


def gate_up_kernel(place_ref, tokens, cut, far, cut_y, far_y, out_ref, held, near, sums, token_sems, weight_sems):
    outer = place_ref[2]
    sources, _, rows, _ = cut.shape
    depth = sources * rows
    copies = []
    for a, far_ref in enumerate((far, far_y)):
        cols = slice(a * depth, (a + 1) * depth)
        copies.append([pltpu.make_async_copy(tokens.at[:, cols], held.at[:, cols], token_sems.at[a])])
        for which in range(2):
            for d in range(sources):
                own = cut.at[outer, which] if a == 0 else cut_y.at[which]
                first = pl.multiple_of(a * depth + (outer ^ d) * rows, rows)
                target = near.at[which, pl.ds(first, rows)]
                source = far_ref.at[d - 1, which] if d else own
                copies[a].append(pltpu.make_async_copy(source, target, weight_sems.at[a, which, d]))
    for group in copies:
        for copy in group:
            copy.start()
    for a, group in enumerate(copies):
        for copy in group:
            copy.wait()
        at = slice(a * depth, (a + 1) * depth)
        for which in range(2):
            for tile in row_tiles(held.shape[0]):
                product = jnp.dot(held[tile, at], near[which, at], preferred_element_type=jnp.float32)
                if a == 0:
                    sums[which, tile, :] = product
                else:
                    out_ref[which, tile, :] = (sums[which, tile, :] + product).astype(jnp.bfloat16)


def gate_up(place, tokens, cut, far, cut_y, far_y):
    rows, depth = tokens.shape
    sources, _, _, cols = cut.shape
    return pl.pallas_call(
        gate_up_kernel,
        in_specs=[SMEM] + [ANY] * 5,
        out_specs=VMEM,
        out_shape=jax.ShapeDtypeStruct((2, rows, cols), jnp.bfloat16),
        scratch_shapes=[
            pltpu.VMEM((rows, depth), jnp.bfloat16),
            pltpu.VMEM((2, depth, cols), jnp.bfloat16),
            pltpu.VMEM((2, rows, cols), jnp.float32),
            pltpu.SemaphoreType.DMA((2,)),
            pltpu.SemaphoreType.DMA((2, 2, sources)),
        ],
        compiler_params=pltpu.CompilerParams(vmem_limit_bytes=VMEM_LIMIT),
        cost_estimate=pl.CostEstimate(
            flops=4 * rows * depth * cols,
            bytes_accessed=2 * (rows * depth + 2 * depth * cols + 2 * rows * cols),
            transcendentals=0,
        ),
        name="gate_up",
    )(place, tokens, cut, far, cut_y, far_y)


def activation_kernel(here_ref, there_ref, out_ref):
    gate = here_ref[0].astype(jnp.float32) + there_ref[0].astype(jnp.float32)
    up = here_ref[1].astype(jnp.float32) + there_ref[1].astype(jnp.float32)
    out_ref[...] = (gate / (1.0 + jnp.exp(-gate)) * up).astype(jnp.bfloat16)


def activation(here, there):
    _, rows, cols = here.shape
    step = min(rows, ROW_TILE)
    return pl.pallas_call(
        activation_kernel,
        grid=(rows // step,),
        in_specs=[pl.BlockSpec((2, step, cols), lambda t: (0, t, 0))] * 2,
        out_specs=pl.BlockSpec((step, cols), lambda t: (t, 0)),
        out_shape=jax.ShapeDtypeStruct((rows, cols), jnp.bfloat16),
        compiler_params=pltpu.CompilerParams(vmem_limit_bytes=VMEM_LIMIT),
        cost_estimate=pl.CostEstimate(flops=8 * rows * cols, bytes_accessed=10 * rows * cols, transcendentals=rows * cols),
        name="activation",
    )(here, there)


def down_kernel(part, place_ref, activated_ref, weights, kept_ref, sent_ref, near, sems):
    sources = weights.shape[0]
    cols = weights.shape[2]
    head, outer = place_ref[1], place_ref[2]
    count = near.shape[0]
    copies = [
        pltpu.make_async_copy(weights.at[outer ^ (part * count + s)], near.at[s], sems.at[s]) for s in range(count)
    ]
    for copy in copies:
        copy.start()
    head_count = sent_ref.shape[0] + 1
    piece = kept_ref.shape[0] // sources
    for e in range(head_count):
        rows = []
        for o in range(sources):
            first = pl.multiple_of((o * head_count + (head ^ e)) * piece, piece)
            rows.append(activated_ref[pl.ds(first, piece), :])
        rows = jnp.concatenate(rows, axis=0)
        for s in range(count):
            if e == 0:
                copies[s].wait()
            at = slice(s * cols, (s + 1) * cols)
            product = jnp.dot(rows, near[s], preferred_element_type=jnp.float32)
            if e == 0:
                kept_ref[:, at] = product.astype(jnp.bfloat16)
            else:
                sent_ref[e - 1, :, at] = product.astype(jnp.bfloat16)


def down_product(place, activated, weights, part, head_count):
    rows = activated.shape[0] // head_count
    sources, depth, cols = weights.shape
    count = sources // PARTS
    return pl.pallas_call(
        functools.partial(down_kernel, part),
        in_specs=[SMEM, VMEM, ANY],
        out_specs=[VMEM, VMEM],
        out_shape=[
            jax.ShapeDtypeStruct((rows, count * cols), jnp.bfloat16),
            jax.ShapeDtypeStruct((head_count - 1, rows, count * cols), jnp.bfloat16),
        ],
        scratch_shapes=[pltpu.VMEM((count, depth, cols), jnp.bfloat16), pltpu.SemaphoreType.DMA((count,))],
        compiler_params=pltpu.CompilerParams(vmem_limit_bytes=VMEM_LIMIT),
        cost_estimate=pl.CostEstimate(
            flops=2 * activated.size * count * cols,
            bytes_accessed=2 * (activated.size + weights.size // PARTS + head_count * rows * count * cols),
            transcendentals=0,
        ),
        name="down",
    )(place, activated, weights)


def per_device(query, key, value, doc_lengths, resid, norm_gain, w_out, w_gate_up, w_down):
    inner_count = lax.axis_size("inner")
    outer_count = lax.axis_size("outer")
    head_count = lax.axis_size("head")
    outer, inner, head = lax.axis_index("outer"), lax.axis_index("inner"), lax.axis_index("head")
    rows = query.shape[0]
    plane_rows = rows * inner_count * head_count
    reach = plane_rows * outer_count // WINDOW_PER_DOC
    feature_rows = w_gate_up.shape[1]
    hidden_cols = w_gate_up.shape[2] // outer_count
    bounds = jnp.cumsum(doc_lengths)
    hops = reach // plane_rows
    token_rows = plane_rows // inner_count
    half = plane_rows // head_count
    packing = (rows, head_count, KEY_VALUE_HEADS // head_count, -1)

    weights_out = lax.all_gather(w_out, "outer", axis=1, tiled=True)
    fence = lambda *arrays: lax.optimization_barrier(arrays)
    own_gain = lax.dynamic_slice_in_dim(norm_gain, outer * feature_rows, feature_rows, 0)
    cut = take_gain(w_gate_up, own_gain[:, None], outer_count)
    if packing[2] == inner_count and hops == 1:
        earlier = [lax.ppermute(part, "outer", [(s, s + 1) for s in range(outer_count - 1)]) for part in (key, value)]
        groups = jnp.concatenate([part.reshape(packing) for part in (query, key, value, *earlier)], axis=3)
        groups = jnp.transpose(groups, (2, 1, 0, 3)).reshape(inner_count * head_count, rows, -1)
        packed = lax.all_to_all(groups, ("inner", "head"), split_axis=0, concat_axis=0, tiled=True)
        packed, cut = fence(packed.reshape(plane_rows, -1), cut)
        starts = document_starts(bounds, outer * plane_rows, plane_rows)
        own_context = attention(packed, packed, Q_COLS // KV_COLS + 1, starts, reach)
        blocks = blocks_over_inner(own_context)
    else:
        groups = jnp.concatenate([part.reshape(packing) for part in (query, key, value)], axis=3)
        groups = jnp.transpose(groups[:, :, 0], (1, 0, 2))
        packed = lax.all_to_all(groups, "head", split_axis=0, concat_axis=0, tiled=True).reshape(token_rows, -1)
        plane_kv = lax.all_gather(packed[:, Q_COLS:], "inner", axis=0, tiled=True)
        every_kv = jnp.concatenate([earlier_planes(plane_kv, hops), plane_kv], axis=0)
        halo = lax.dynamic_slice_in_dim(every_kv, inner * token_rows, reach, 0)
        starts = document_starts(bounds, outer * plane_rows + inner * token_rows, token_rows)
        own_context = attention(packed, halo, 0, starts, reach)
        blocks = [lax.all_gather(own_context, "inner", axis=0, tiled=True)]

    over_y = functools.partial(swap, axis="inner", distance=2)
    piece_for = lambda array, d: lax.dynamic_index_in_dim(array, outer ^ d, 0, False)
    down_cut = w_down.reshape(outer_count, hidden_cols, feature_rows)
    ends, middle = (0, outer_count - 1), (1, 2)
    split_last = outer_count == 4
    early = []
    if split_last:
        early = [swap(piece_for(array, 3), "outer", 3, middle) for array in (cut, down_cut)]
    cut_y = over_y(after(piece_for(cut, 0), blocks[-1]))
    weights_out, cut_y, *early = fence(weights_out, cut_y, *early)

    def send(array):
        moved = [swap(piece_for(array, d), "outer", d) for d in range(1, outer_count - split_last)]
        return moved + ([swap(piece_for(array, 3), "outer", 3, ends)] if split_last else [])

    def received(pieces, met):
        return pieces[:-1] + [pieces[-1] + met] if split_last else pieces

    place = jnp.stack([inner, head, outer]).astype(jnp.int32)
    gates = send(after(cut[:, 0], weights_out))
    kept, sent, *whole = projection(blocks, weights_out, place, head_count, inner_count)
    context = whole[0] if whole else own_context
    projected = kept.astype(jnp.float32)
    for e in range(1, head_count):
        projected = projected + swap(sent[e - 1], "head", e).astype(jnp.float32)
    projected, *gates = fence(projected, *gates)
    own_resid = lax.dynamic_slice_in_dim(resid, head * half, half, 0)
    hidden_part = (own_resid.astype(jnp.float32) + projected).astype(jnp.bfloat16)

    ups = send(after(cut[:, 1], gates[0]))
    upper = inner // 2
    own_rows = half // 2
    mine = lax.dynamic_slice_in_dim(hidden_part, upper * own_rows, own_rows, 0)
    others = lax.dynamic_slice_in_dim(hidden_part, (1 - upper) * own_rows, own_rows, 0)
    state = [mine.astype(jnp.float32), over_y(others).astype(jnp.float32)]
    squares = sum([jnp.sum(block * block, axis=1) for block in state])
    squares = squares + swap(squares, "inner", 1)
    inverse = lax.rsqrt(squares / D + 1e-05)[:, None]
    normed = jnp.concatenate([block * inverse for block in state], axis=1).astype(jnp.bfloat16)
    normed, *ups = fence(normed, *ups)
    tokens = lax.all_gather(normed, ("outer", "head"), axis=0, tiled=True)

    gates = received(gates, early[0][0] if early else None)
    ups = received(ups, early[0][1] if early else None)
    far = jnp.stack([jnp.stack(pair) for pair in zip(gates, ups)])
    far_y, *downs = fence(over_y(far), *send(after(down_cut, normed)))
    downs = jnp.stack([piece_for(down_cut, 0)] + received(downs, early[1] if early else None))
    sums = gate_up(place, tokens, cut, far, cut_y, far_y)
    activated = activation(sums, swap(sums, "inner", 1))

    downs = [downs, over_y(downs)]
    layer_out = jnp.zeros((half, outer_count * feature_rows), jnp.bfloat16)
    for a in range(2):
        for part in range(PARTS):
            kept, sent = down_product(place, activated, downs[a], part, head_count)
            if a == 0:
                downs[1] = after(downs[1], kept)
            paired = kept.astype(jnp.float32)
            for e in range(1, head_count):
                paired = paired + swap(sent[e - 1], "head", e).astype(jnp.float32)
            paired = paired.reshape(outer_count, own_rows, -1)
            total = piece_for(paired, 0)
            for d in range(1, outer_count):
                total = total + swap(piece_for(paired, d).astype(jnp.bfloat16), "outer", d).astype(jnp.float32)
            width = total.shape[1]
            total = (state[a][:, part * width : (part + 1) * width] + total).astype(jnp.bfloat16)
            first_row = ((1 - upper) if a else upper) * own_rows
            layer_out = lax.dynamic_update_slice(layer_out, over_y(total) if a else total, (first_row, part * width))
    return (context, layer_out)


def solution(mesh):
    placed = (
        P(("outer", "inner", "head"), None),
        P(("outer", "inner", "head"), None),
        P(("outer", "inner", "head"), None),
        P(),
        P("outer", "inner"),
        P("inner"),
        P("head", ("inner", "outer")),
        P(None, ("inner", "outer"), "head"),
        P("head", ("inner", "outer")),
    )
    return jax.shard_map(
        per_device,
        mesh=mesh,
        in_specs=placed,
        out_specs=(P(("outer", "inner"), "head"), P(("outer", "head"), "inner")),
        check_vma=False,
    )
```

```python
import functools

import jax
import jax.numpy as jnp
from jax import lax
from jax.experimental import pallas as pl
from jax.experimental.pallas import tpu as pltpu
from jax.sharding import PartitionSpec as P

D = 4096
QUERY_HEADS = 32
KEY_VALUE_HEADS = 8
HEAD_WIDTH = 128
GROUP = QUERY_HEADS // KEY_VALUE_HEADS
Q_COLS = GROUP * HEAD_WIDTH
KV_COLS = 2 * HEAD_WIDTH
WINDOW_PER_DOC = 4
QUERY_TILE = 128
ROW_TILE = 256
PARTS = 2
VMEM_LIMIT = 48 * 1024 * 1024
ANY = pl.BlockSpec(memory_space=pl.ANY)
VMEM = pl.BlockSpec(memory_space=pltpu.VMEM)
SMEM = pl.BlockSpec(memory_space=pltpu.SMEM)


def swap(array, axis, distance):
    if distance == 0:
        return array
    count = lax.axis_size(axis)
    return lax.ppermute(array, axis, [(s, s ^ distance) for s in range(count)])


def after(array, earlier):
    return lax.optimization_barrier((array, earlier))[0]


def blocks_over_inner(block):
    across = swap(block, "inner", 2)
    return [block, swap(block, "inner", 1), across, swap(across, "inner", 1)]


def earlier_planes(kv, hops):
    count = lax.axis_size("outer")
    moved = [lax.ppermute(kv, "outer", [(s, s + d) for s in range(count - d)]) for d in range(hops, 0, -1)]
    return jnp.concatenate(moved, axis=0)


def document_starts(bounds, first, rows):
    place = first + jnp.arange(rows, dtype=jnp.int32)
    starts = jnp.max(jnp.where(bounds[None, :] <= place[:, None], bounds[None, :], 0), axis=1) - first
    return starts[:, None].astype(jnp.int32)


def row_tiles(rows):
    step = ROW_TILE if rows % ROW_TILE == 0 else rows
    return [slice(at, at + step) for at in range(0, rows, step)]


def attention_kernel(halo_rows, reach, starts_ref, queries_ref, own_ref, halo_ref, out_ref, keys, values):
    tile = pl.program_id(0)
    rows = queries_ref.shape[0]
    span = reach + rows

    @pl.when(tile == 0)
    def _():
        keys[:halo_rows, :] = halo_ref[:, :HEAD_WIDTH]
        values[:halo_rows, :] = halo_ref[:, HEAD_WIDTH:]
        keys[halo_rows:, :] = own_ref[:, :HEAD_WIDTH]
        values[halo_rows:, :] = own_ref[:, HEAD_WIDTH:]

    first = pl.multiple_of(tile * rows + (halo_rows - reach), rows)
    near_keys = keys[pl.ds(first, span), :]
    near_values = values[pl.ds(first, span), :]
    key_place = lax.broadcasted_iota(jnp.int32, (rows, span), 1)
    query_place = lax.broadcasted_iota(jnp.int32, (rows, span), 0) + reach
    start = starts_ref[...] - (first - halo_rows)
    allowed = (key_place <= query_place) & (key_place >= start)
    for g in range(GROUP):
        cols = slice(g * HEAD_WIDTH, (g + 1) * HEAD_WIDTH)
        scores = lax.dot_general(
            queries_ref[:, cols], near_keys, (((1,), (1,)), ((), ())), preferred_element_type=jnp.float32
        ) * (HEAD_WIDTH ** (-0.5))
        masked = jnp.where(allowed, scores, -1e30)
        row_max = jnp.max(masked, axis=1, keepdims=True)
        weights = jnp.exp(masked - row_max)
        totals = jnp.sum(weights, axis=1, keepdims=True)
        summed = jnp.dot(weights.astype(jnp.bfloat16), near_values, preferred_element_type=jnp.float32)
        out_ref[:, cols] = (summed / totals).astype(jnp.bfloat16)


def attention(packed, halo, halo_at, starts, reach):
    rows = packed.shape[0]
    halo_rows = halo.shape[0]
    return pl.pallas_call(
        functools.partial(attention_kernel, halo_rows, reach),
        grid=(rows // QUERY_TILE,),
        in_specs=[
            pl.BlockSpec((QUERY_TILE, 1), lambda t: (t, 0)),
            pl.BlockSpec((QUERY_TILE, Q_COLS), lambda t: (t, 0)),
            pl.BlockSpec((rows, KV_COLS), lambda t: (0, Q_COLS // KV_COLS)),
            pl.BlockSpec((halo_rows, KV_COLS), lambda t: (0, halo_at)),
        ],
        out_specs=pl.BlockSpec((QUERY_TILE, Q_COLS), lambda t: (t, 0)),
        out_shape=jax.ShapeDtypeStruct((rows, Q_COLS), jnp.bfloat16),
        scratch_shapes=[
            pltpu.VMEM((halo_rows + rows, HEAD_WIDTH), jnp.bfloat16),
            pltpu.VMEM((halo_rows + rows, HEAD_WIDTH), jnp.bfloat16),
        ],
        compiler_params=pltpu.CompilerParams(vmem_limit_bytes=VMEM_LIMIT),
        cost_estimate=pl.CostEstimate(
            flops=4 * rows * (reach + QUERY_TILE) * Q_COLS,
            bytes_accessed=rows * 4 * Q_COLS,
            transcendentals=rows * (reach + QUERY_TILE) * GROUP,
        ),
        name="attention",
    )(starts, packed, packed, halo)


def cut_kernel(gain_ref, gate_up_ref, down_ref, *out_refs):
    rows, cols = out_refs[0].shape[1], out_refs[-1].shape[2]
    for part in range(PARTS):
        at = slice(part * rows, (part + 1) * rows)
        for which in range(2):
            scaled = gate_up_ref[which, at].astype(jnp.float32) * gain_ref[at]
            out_refs[2 * part + which][0] = scaled.astype(jnp.bfloat16)
        out_refs[2 * PARTS + part][0] = down_ref[:, part * cols : (part + 1) * cols]


def cut_weights(w_gate_up, w_down, gain, outer_count):
    _, features, width = w_gate_up.shape
    cols = width // outer_count
    rows = features // PARTS
    if cols % HEAD_WIDTH:
        wide = (w_gate_up.astype(jnp.float32) * gain[None]).astype(jnp.bfloat16)
        wide = jnp.transpose(wide.reshape(2, PARTS, rows, outer_count, cols), (1, 0, 3, 2, 4))
        tall = jnp.transpose(w_down.reshape(outer_count, cols, PARTS, rows), (2, 0, 1, 3))
        return [wide[part, which] for part in range(PARTS) for which in range(2)] + [tall[part] for part in range(PARTS)]
    return pl.pallas_call(
        cut_kernel,
        grid=(outer_count,),
        in_specs=[
            pl.BlockSpec((features, 1), lambda p: (0, 0)),
            pl.BlockSpec((2, features, cols), lambda p: (0, 0, p)),
            pl.BlockSpec((cols, features), lambda p: (p, 0)),
        ],
        out_specs=[pl.BlockSpec((1, rows, cols), lambda p: (p, 0, 0))] * (2 * PARTS)
        + [pl.BlockSpec((1, cols, rows), lambda p: (p, 0, 0))] * PARTS,
        out_shape=[jax.ShapeDtypeStruct((outer_count, rows, cols), jnp.bfloat16)] * (2 * PARTS)
        + [jax.ShapeDtypeStruct((outer_count, cols, rows), jnp.bfloat16)] * PARTS,
        compiler_params=pltpu.CompilerParams(vmem_limit_bytes=VMEM_LIMIT),
        cost_estimate=pl.CostEstimate(flops=2 * features * width, bytes_accessed=12 * features * width, transcendentals=0),
        name="cut_weights",
    )(gain, w_gate_up, w_down)


def projection_kernel(block_count, place_ref, *refs):
    blocks, weights_ref = refs[:block_count], refs[block_count]
    kept_ref, sent_ref = refs[block_count + 1 : block_count + 3]
    inner, head = place_ref[0], place_ref[1]
    half, depth = kept_ref.shape[0], blocks[0].shape[1]
    for e in range(sent_ref.shape[0] + 1):
        rows = pl.ds(pl.multiple_of((head ^ e) * half, half), half)
        total = jnp.zeros(kept_ref.shape, jnp.float32)
        for a, block in enumerate(blocks):
            at = pl.ds(pl.multiple_of((inner ^ a) * depth, depth), depth) if block_count > 1 else slice(None)
            total = total + jnp.dot(block[rows, :], weights_ref[at, :], preferred_element_type=jnp.float32)
        if e == 0:
            kept_ref[...] = total.astype(jnp.bfloat16)
        else:
            sent_ref[e - 1] = total.astype(jnp.bfloat16)
    if block_count > 1:
        context_ref = refs[block_count + 3]
        tokens = context_ref.shape[0]
        own = pl.ds(pl.multiple_of(inner * tokens, tokens), tokens)
        for a, block in enumerate(blocks):
            context_ref[:, pl.ds(pl.multiple_of((inner ^ a) * depth, depth), depth)] = block[own, :]


def projection(blocks, weights, place, head_count, inner_count):
    rows, depth = blocks[0].shape
    half, width = rows // head_count, weights.shape[1]
    outs = [(half, width), (head_count - 1, half, width)]
    if len(blocks) > 1:
        outs.append((rows // inner_count, len(blocks) * depth))
    return pl.pallas_call(
        functools.partial(projection_kernel, len(blocks)),
        in_specs=[SMEM] + [VMEM] * (len(blocks) + 1),
        out_specs=[VMEM] * len(outs),
        out_shape=[jax.ShapeDtypeStruct(shape, jnp.bfloat16) for shape in outs],
        compiler_params=pltpu.CompilerParams(vmem_limit_bytes=VMEM_LIMIT),
        cost_estimate=pl.CostEstimate(
            flops=2 * rows * weights.size, bytes_accessed=2 * (weights.size + rows * 2 * width), transcendentals=0
        ),
        name="projection",
    )(place, *blocks, weights)


def gate_up_kernel(block_count, head_count, *refs):
    tokens = refs[: block_count * head_count]
    weights = refs[len(tokens) : len(tokens) + 2 * PARTS * block_count]
    out_ref, held, near, sums, token_sems, weight_sems = refs[len(tokens) + len(weights) :]
    rows, depth = tokens[0].shape
    copies = []
    for a in range(block_count):
        group = []
        for e in range(head_count):
            j = a * head_count + e
            target = held.at[pl.ds(e * rows, rows), pl.ds(a * depth, depth)]
            group.append(pltpu.make_async_copy(tokens[j], target, token_sems.at[j]))
        for j in range(2 * PARTS * a, 2 * PARTS * (a + 1)):
            target = near.at[j % 2, a, :, (j // 2) % PARTS]
            group.append(pltpu.make_async_copy(weights[j], target, weight_sems.at[j]))
        copies.append(group)
    for group in copies:
        for copy in group:
            copy.start()
    for a, group in enumerate(copies):
        for copy in group:
            copy.wait()
        for which in range(2):
            block = near[which, a].reshape(depth, -1)
            for tile in row_tiles(held.shape[0]):
                product = jnp.dot(held[tile, a * depth : (a + 1) * depth], block, preferred_element_type=jnp.float32)
                total = product if a == 0 else sums[which, tile, :] + product
                if a < block_count - 1:
                    sums[which, tile, :] = total
                else:
                    out_ref[which, tile, :] = total.astype(jnp.bfloat16)


def gate_up(tokens, blocks):
    head_count = len(tokens[0])
    rows, depth = tokens[0][0].shape
    sources, stream_rows, cols = blocks[0][0].shape
    tokens = [piece for block in tokens for piece in block]
    weights = [stream for block in blocks for stream in block]
    rows, all_depth = rows * head_count, depth * len(blocks)
    return pl.pallas_call(
        functools.partial(gate_up_kernel, len(blocks), head_count),
        in_specs=[ANY] * (len(tokens) + len(weights)),
        out_specs=VMEM,
        out_shape=jax.ShapeDtypeStruct((2, rows, cols), jnp.bfloat16),
        scratch_shapes=[
            pltpu.VMEM((rows, all_depth), jnp.bfloat16),
            pltpu.VMEM((2, len(blocks), sources, PARTS, stream_rows, cols), jnp.bfloat16),
            pltpu.VMEM((2, rows, cols), jnp.float32),
            pltpu.SemaphoreType.DMA((len(tokens),)),
            pltpu.SemaphoreType.DMA((len(weights),)),
        ],
        compiler_params=pltpu.CompilerParams(vmem_limit_bytes=VMEM_LIMIT),
        cost_estimate=pl.CostEstimate(
            flops=4 * rows * all_depth * cols,
            bytes_accessed=2 * (rows * all_depth + 2 * all_depth * cols + 2 * rows * cols),
            transcendentals=0,
        ),
        name="gate_up",
    )(*tokens, *weights)


def activation_kernel(here_ref, there_ref, out_ref):
    gate = here_ref[0].astype(jnp.float32) + there_ref[0].astype(jnp.float32)
    up = here_ref[1].astype(jnp.float32) + there_ref[1].astype(jnp.float32)
    out_ref[...] = (gate / (1.0 + jnp.exp(-gate)) * up).astype(jnp.bfloat16)


def activation(here, there):
    _, rows, cols = here.shape
    step = min(rows, ROW_TILE)
    return pl.pallas_call(
        activation_kernel,
        grid=(rows // step,),
        in_specs=[pl.BlockSpec((2, step, cols), lambda t: (0, t, 0))] * 2,
        out_specs=pl.BlockSpec((step, cols), lambda t: (t, 0)),
        out_shape=jax.ShapeDtypeStruct((rows, cols), jnp.bfloat16),
        compiler_params=pltpu.CompilerParams(vmem_limit_bytes=VMEM_LIMIT),
        cost_estimate=pl.CostEstimate(flops=8 * rows * cols, bytes_accessed=10 * rows * cols, transcendentals=rows * cols),
        name="activation",
    )(here, there)


def down_kernel(activated_ref, weights_ref, kept_ref, sent_ref):
    sources, _, cols = weights_ref.shape
    kept_rows = kept_ref.shape[0]
    if cols % HEAD_WIDTH:
        blocks = [weights_ref[s] for s in range(sources)]
    else:
        blocks = [jnp.concatenate([weights_ref[s] for s in range(sources)], axis=1)]
    for e in range(sent_ref.shape[0] + 1):
        rows = activated_ref[e * kept_rows : (e + 1) * kept_rows, :]
        for s, block in enumerate(blocks):
            at = slice(s * block.shape[1], (s + 1) * block.shape[1])
            product = jnp.dot(rows, block, preferred_element_type=jnp.float32)
            if e == 0:
                kept_ref[:, at] = product.astype(jnp.bfloat16)
            else:
                sent_ref[e - 1, :, at] = product.astype(jnp.bfloat16)


def down_product(activated, weights, head_count):
    rows = activated.shape[0] // head_count
    sources, depth, cols = weights.shape
    return pl.pallas_call(
        down_kernel,
        in_specs=[VMEM, VMEM],
        out_specs=[VMEM, VMEM],
        out_shape=[
            jax.ShapeDtypeStruct((rows, sources * cols), jnp.bfloat16),
            jax.ShapeDtypeStruct((head_count - 1, rows, sources * cols), jnp.bfloat16),
        ],
        compiler_params=pltpu.CompilerParams(vmem_limit_bytes=VMEM_LIMIT),
        cost_estimate=pl.CostEstimate(
            flops=2 * activated.size * sources * cols,
            bytes_accessed=2 * (activated.size + weights.size + head_count * rows * sources * cols),
            transcendentals=0,
        ),
        name="down",
    )(activated, weights)


def per_device(query, key, value, doc_lengths, resid, norm_gain, w_out, w_gate_up, w_down):
    inner_count = lax.axis_size("inner")
    outer_count = lax.axis_size("outer")
    head_count = lax.axis_size("head")
    outer, inner, head = lax.axis_index("outer"), lax.axis_index("inner"), lax.axis_index("head")
    rows = query.shape[0]
    plane_rows = rows * inner_count * head_count
    reach = plane_rows * outer_count // WINDOW_PER_DOC
    feature_rows = w_gate_up.shape[1]
    hidden_cols = w_gate_up.shape[2] // outer_count
    bounds = jnp.cumsum(doc_lengths)
    hops = reach // plane_rows
    token_rows = plane_rows // inner_count
    half = plane_rows // head_count
    packing = (rows, head_count, KEY_VALUE_HEADS // head_count, -1)

    weights_out = lax.all_gather(w_out, "outer", axis=1, tiled=True)
    if packing[2] == inner_count and hops == 1:
        earlier = [lax.ppermute(part, "outer", [(s, s + 1) for s in range(outer_count - 1)]) for part in (key, value)]
        groups = jnp.concatenate([part.reshape(packing) for part in (query, key, value, *earlier)], axis=3)
        groups = jnp.transpose(groups, (2, 1, 0, 3)).reshape(inner_count * head_count, rows, -1)
        packed = lax.all_to_all(groups, ("inner", "head"), split_axis=0, concat_axis=0, tiled=True)
        packed = packed.reshape(plane_rows, -1)
        starts = document_starts(bounds, outer * plane_rows, plane_rows)
        own_context = attention(packed, packed, Q_COLS // KV_COLS + 1, starts, reach)
        blocks = blocks_over_inner(own_context)
    else:
        groups = jnp.concatenate([part.reshape(packing) for part in (query, key, value)], axis=3)
        groups = jnp.transpose(groups[:, :, 0], (1, 0, 2))
        packed = lax.all_to_all(groups, "head", split_axis=0, concat_axis=0, tiled=True).reshape(token_rows, -1)
        plane_kv = lax.all_gather(packed[:, Q_COLS:], "inner", axis=0, tiled=True)
        every_kv = jnp.concatenate([earlier_planes(plane_kv, hops), plane_kv], axis=0)
        halo = lax.dynamic_slice_in_dim(every_kv, inner * token_rows, reach, 0)
        starts = document_starts(bounds, outer * plane_rows + inner * token_rows, token_rows)
        own_context = attention(packed, halo, 0, starts, reach)
        blocks = [lax.all_gather(own_context, "inner", axis=0, tiled=True)]

    spread = functools.partial(lax.all_to_all, axis_name="outer", split_axis=0, concat_axis=0, tiled=True)
    over_y = functools.partial(swap, axis="inner", distance=2)
    fence = lambda *arrays: lax.optimization_barrier(arrays)
    own_gain = lax.dynamic_slice_in_dim(norm_gain, outer * feature_rows, feature_rows, 0)
    cut = cut_weights(w_gate_up, w_down, own_gain[:, None], outer_count)

    place = jnp.stack([inner, head]).astype(jnp.int32)
    first = spread(after(cut[0], weights_out))
    kept, sent, *whole = projection(blocks, weights_out, place, head_count, inner_count)
    context = whole[0] if whole else own_context
    projected = kept.astype(jnp.float32)
    for e in range(1, head_count):
        projected = projected + swap(sent[e - 1], "head", e).astype(jnp.float32)
    projected, first = fence(projected, first)
    own_resid = lax.dynamic_slice_in_dim(resid, head * half, half, 0)
    hidden_part = (own_resid.astype(jnp.float32) + projected).astype(jnp.bfloat16)

    second = spread(after(cut[1], first))
    upper = inner // 2
    own_rows = half // 2
    mine = lax.dynamic_slice_in_dim(hidden_part, upper * own_rows, own_rows, 0)
    others = lax.dynamic_slice_in_dim(hidden_part, (1 - upper) * own_rows, own_rows, 0)
    state = [mine.astype(jnp.float32), over_y(others).astype(jnp.float32)]
    squares = sum([jnp.sum(block * block, axis=1) for block in state])
    squares = squares + swap(squares, "inner", 1)
    inverse = lax.rsqrt(squares / D + 1e-05)[:, None]
    part_rows = feature_rows // PARTS
    normed = [(block * inverse).astype(jnp.bfloat16) for block in state]
    *normed, first, second = fence(*normed, first, second)
    state = [block.reshape(own_rows, outer_count, PARTS, part_rows) for block in state]
    state = [[block[:, :, part].reshape(own_rows, -1) for part in range(PARTS)] for block in state]

    tokens = []
    for block in normed:
        block = lax.all_gather(block, "outer", axis=0, tiled=True)
        tokens.append([swap(block, "head", e) if e else block for e in range(head_count)])

    third, first_y, second_y = fence(spread(after(cut[2], normed[0])), over_y(first), over_y(second))
    fourth, third_y, state = fence(spread(after(cut[3], third)), over_y(third), state)
    fifth, fourth_y, tokens = fence(spread(after(cut[4], fourth)), over_y(fourth), tokens)
    sums = gate_up(tokens, [[first, second, third, fourth], [first_y, second_y, third_y, fourth_y]])
    activated = activation(sums, swap(sums, "inner", 1))

    def over_heads(weights):
        kept, sent = down_product(activated, weights, head_count)
        paired = kept.astype(jnp.float32)
        for e in range(1, head_count):
            paired = paired + swap(sent[e - 1], "head", e).astype(jnp.float32)
        return paired.reshape(outer_count, own_rows, -1)

    paired = {(0, 0): over_heads(fifth)}
    sixth, fifth_y, paired[0, 0] = fence(spread(after(cut[5], fifth)), over_y(fifth), paired[0, 0])
    sixth_y = over_y(sixth)
    paired[1, 0] = over_heads(fifth_y)
    paired[0, 1] = over_heads(sixth)
    paired[1, 1] = over_heads(after(sixth_y, paired[1, 0]))

    pieces = [[None] * PARTS, [None] * PARTS]
    for part in range(PARTS):
        for a in range(2):
            total = state[a][part] + lax.dynamic_index_in_dim(paired[a, part], outer, 0, False)
            for d in range(1, outer_count):
                sent = lax.dynamic_index_in_dim(paired[a, part], outer ^ d, 0, False).astype(jnp.bfloat16)
                total = total + swap(sent, "outer", d).astype(jnp.float32)
            total = total.astype(jnp.bfloat16)
            pieces[a][part] = (over_y(total) if a else total).reshape(own_rows, outer_count, 1, part_rows)
    halves = [jnp.concatenate(parts, axis=2).reshape(own_rows, -1) for parts in pieces]
    layer_out = jnp.zeros((half, halves[0].shape[1]), jnp.bfloat16)
    layer_out = lax.dynamic_update_slice(layer_out, halves[0], (upper * own_rows, 0))
    layer_out = lax.dynamic_update_slice(layer_out, halves[1], ((1 - upper) * own_rows, 0))
    return (context, layer_out)


def solution(mesh):
    placed = (
        P(("outer", "inner", "head"), None),
        P(("outer", "inner", "head"), None),
        P(("outer", "inner", "head"), None),
        P(),
        P("outer", "inner"),
        P("inner"),
        P("head", ("inner", "outer")),
        P(None, ("inner", "outer"), "head"),
        P("head", ("inner", "outer")),
    )
    return jax.shard_map(
        per_device,
        mesh=mesh,
        in_specs=placed,
        out_specs=(P(("outer", "inner"), "head"), P(("outer", "head"), "inner")),
        check_vma=False,
    )
```

```python
import functools

import jax
import jax.numpy as jnp
from jax import lax
from jax.experimental import pallas as pl
from jax.experimental.pallas import tpu as pltpu
from jax.sharding import PartitionSpec as P

D = 4096
QUERY_HEADS = 32
KEY_VALUE_HEADS = 8
HEAD_WIDTH = 128
GROUP = QUERY_HEADS // KEY_VALUE_HEADS
Q_COLS = GROUP * HEAD_WIDTH
KV_COLS = 2 * HEAD_WIDTH
WINDOW_PER_DOC = 4
QUERY_TILE = 128
ROW_TILE = 256
PARTS = 2
VMEM_LIMIT = 48 * 1024 * 1024
BRIEF = pl.CostEstimate(flops=1, bytes_accessed=1, transcendentals=0)
ANY = pl.BlockSpec(memory_space=pl.ANY)
VMEM = pl.BlockSpec(memory_space=pltpu.VMEM)
SMEM = pl.BlockSpec(memory_space=pltpu.SMEM)


def swap(array, axis, distance):
    if distance == 0:
        return array
    count = lax.axis_size(axis)
    return lax.ppermute(array, axis, [(s, s ^ distance) for s in range(count)])


def after(array, earlier):
    return lax.optimization_barrier((array, earlier))[0]


def blocks_over_inner(block):
    across = swap(block, "inner", 2)
    return [block, swap(block, "inner", 1), across, swap(across, "inner", 1)]


def earlier_planes(kv, hops):
    count = lax.axis_size("outer")
    moved = [lax.ppermute(kv, "outer", [(s, s + d) for s in range(count - d)]) for d in range(hops, 0, -1)]
    return jnp.concatenate(moved, axis=0)


def document_starts(bounds, first, rows):
    place = first + jnp.arange(rows, dtype=jnp.int32)
    starts = jnp.max(jnp.where(bounds[None, :] <= place[:, None], bounds[None, :], 0), axis=1) - first
    return starts[:, None].astype(jnp.int32)


def row_tiles(rows):
    step = ROW_TILE if rows % ROW_TILE == 0 else rows
    return [slice(at, at + step) for at in range(0, rows, step)]


def attention_kernel(halo_rows, reach, starts_ref, queries_ref, own_ref, halo_ref, out_ref, keys, values):
    tile = pl.program_id(0)
    rows = queries_ref.shape[0]
    span = reach + rows

    @pl.when(tile == 0)
    def _():
        keys[:halo_rows, :] = halo_ref[:, :HEAD_WIDTH]
        values[:halo_rows, :] = halo_ref[:, HEAD_WIDTH:]
        keys[halo_rows:, :] = own_ref[:, :HEAD_WIDTH]
        values[halo_rows:, :] = own_ref[:, HEAD_WIDTH:]

    first = pl.multiple_of(tile * rows + (halo_rows - reach), rows)
    near_keys = keys[pl.ds(first, span), :]
    near_values = values[pl.ds(first, span), :]
    key_place = lax.broadcasted_iota(jnp.int32, (rows, span), 1)
    query_place = lax.broadcasted_iota(jnp.int32, (rows, span), 0) + reach
    start = starts_ref[...] - (first - halo_rows)
    allowed = (key_place <= query_place) & (key_place >= start)
    for g in range(GROUP):
        cols = slice(g * HEAD_WIDTH, (g + 1) * HEAD_WIDTH)
        scores = lax.dot_general(
            queries_ref[:, cols], near_keys, (((1,), (1,)), ((), ())), preferred_element_type=jnp.float32
        ) * (HEAD_WIDTH ** (-0.5))
        masked = jnp.where(allowed, scores, -1e30)
        row_max = jnp.max(masked, axis=1, keepdims=True)
        weights = jnp.exp(masked - row_max)
        totals = jnp.sum(weights, axis=1, keepdims=True)
        summed = jnp.dot(weights.astype(jnp.bfloat16), near_values, preferred_element_type=jnp.float32)
        out_ref[:, cols] = (summed / totals).astype(jnp.bfloat16)


def attention(packed, halo, halo_at, starts, reach):
    rows = packed.shape[0]
    halo_rows = halo.shape[0]
    return pl.pallas_call(
        functools.partial(attention_kernel, halo_rows, reach),
        grid=(rows // QUERY_TILE,),
        in_specs=[
            pl.BlockSpec((QUERY_TILE, 1), lambda t: (t, 0)),
            pl.BlockSpec((QUERY_TILE, Q_COLS), lambda t: (t, 0)),
            pl.BlockSpec((rows, KV_COLS), lambda t: (0, Q_COLS // KV_COLS)),
            pl.BlockSpec((halo_rows, KV_COLS), lambda t: (0, halo_at)),
        ],
        out_specs=pl.BlockSpec((QUERY_TILE, Q_COLS), lambda t: (t, 0)),
        out_shape=jax.ShapeDtypeStruct((rows, Q_COLS), jnp.bfloat16),
        scratch_shapes=[
            pltpu.VMEM((halo_rows + rows, HEAD_WIDTH), jnp.bfloat16),
            pltpu.VMEM((halo_rows + rows, HEAD_WIDTH), jnp.bfloat16),
        ],
        compiler_params=pltpu.CompilerParams(vmem_limit_bytes=VMEM_LIMIT),
        cost_estimate=BRIEF,
        name="attention",
    )(starts, packed, packed, halo)


def cut_kernel(gain_ref, gate_up_ref, down_ref, both_ref, gate_ref, up_ref, *down_refs):
    rows, cols = gate_ref.shape[1], down_refs[0].shape[2]
    for which, second_ref in enumerate((gate_ref, up_ref)):
        scaled = (gate_up_ref[which].astype(jnp.float32) * gain_ref[...]).astype(jnp.bfloat16)
        both_ref[0, which] = scaled[:rows]
        second_ref[0] = scaled[rows:]
    for part, out_ref in enumerate(down_refs):
        out_ref[0] = down_ref[:, part * cols : (part + 1) * cols]


def cut_weights(w_gate_up, w_down, gain, outer_count):
    _, features, width = w_gate_up.shape
    cols = width // outer_count
    rows = features // PARTS
    if cols % HEAD_WIDTH:
        wide = (w_gate_up.astype(jnp.float32) * gain[None]).astype(jnp.bfloat16)
        wide = jnp.transpose(wide.reshape(2, PARTS, rows, outer_count, cols), (1, 3, 0, 2, 4))
        tall = jnp.transpose(w_down.reshape(outer_count, cols, PARTS, rows), (2, 0, 1, 3))
        return [wide[0], wide[1, :, 0], wide[1, :, 1], *tall]
    return pl.pallas_call(
        cut_kernel,
        grid=(outer_count,),
        in_specs=[
            pl.BlockSpec((features, 1), lambda p: (0, 0)),
            pl.BlockSpec((2, features, cols), lambda p: (0, 0, p)),
            pl.BlockSpec((cols, features), lambda p: (p, 0)),
        ],
        out_specs=[pl.BlockSpec((1, 2, rows, cols), lambda p: (p, 0, 0, 0))]
        + [pl.BlockSpec((1, rows, cols), lambda p: (p, 0, 0))] * 2
        + [pl.BlockSpec((1, cols, rows), lambda p: (p, 0, 0))] * PARTS,
        out_shape=[jax.ShapeDtypeStruct((outer_count, 2, rows, cols), jnp.bfloat16)]
        + [jax.ShapeDtypeStruct((outer_count, rows, cols), jnp.bfloat16)] * 2
        + [jax.ShapeDtypeStruct((outer_count, cols, rows), jnp.bfloat16)] * PARTS,
        compiler_params=pltpu.CompilerParams(vmem_limit_bytes=VMEM_LIMIT),
        cost_estimate=BRIEF,
        name="cut_weights",
    )(gain, w_gate_up, w_down)


def projection_kernel(block_count, place_ref, *refs):
    blocks, weights_ref = refs[:block_count], refs[block_count]
    kept_ref, sent_ref = refs[block_count + 1 : block_count + 3]
    inner, head = place_ref[0], place_ref[1]
    half, depth = kept_ref.shape[0], blocks[0].shape[1]
    for e in range(sent_ref.shape[0] + 1):
        rows = pl.ds(pl.multiple_of((head ^ e) * half, half), half)
        total = jnp.zeros(kept_ref.shape, jnp.float32)
        for a, block in enumerate(blocks):
            at = pl.ds(pl.multiple_of((inner ^ a) * depth, depth), depth) if block_count > 1 else slice(None)
            total = total + jnp.dot(block[rows, :], weights_ref[at, :], preferred_element_type=jnp.float32)
        if e == 0:
            kept_ref[...] = total.astype(jnp.bfloat16)
        else:
            sent_ref[e - 1] = total.astype(jnp.bfloat16)
    if block_count > 1:
        context_ref = refs[block_count + 3]
        tokens = context_ref.shape[0]
        own = pl.ds(pl.multiple_of(inner * tokens, tokens), tokens)
        for a, block in enumerate(blocks):
            context_ref[:, pl.ds(pl.multiple_of((inner ^ a) * depth, depth), depth)] = block[own, :]


def projection(blocks, weights, place, head_count, inner_count):
    rows, depth = blocks[0].shape
    half, width = rows // head_count, weights.shape[1]
    outs = [(half, width), (head_count - 1, half, width)]
    if len(blocks) > 1:
        outs.append((rows // inner_count, len(blocks) * depth))
    return pl.pallas_call(
        functools.partial(projection_kernel, len(blocks)),
        in_specs=[SMEM] + [VMEM] * (len(blocks) + 1),
        out_specs=[VMEM] * len(outs),
        out_shape=[jax.ShapeDtypeStruct(shape, jnp.bfloat16) for shape in outs],
        compiler_params=pltpu.CompilerParams(vmem_limit_bytes=VMEM_LIMIT),
        cost_estimate=BRIEF,
        name="projection",
    )(place, *blocks, weights)


def gate_up_kernel(head_count, *refs):
    tokens = refs[:head_count]
    both, gate, up = refs[head_count : head_count + 3]
    *earlier, out_ref, held, near, token_sems, weight_sems = refs[head_count + 3 :]
    rows, depth = tokens[0].shape
    copies = [
        [pltpu.make_async_copy(both.at[:, which], near.at[which, :, 0], weight_sems.at[which, 0]),
         pltpu.make_async_copy(second, near.at[which, :, 1], weight_sems.at[which, 1])]
        for which, second in enumerate((gate, up))
    ]
    for e, token_ref in enumerate(tokens):
        copies[0].append(pltpu.make_async_copy(token_ref, held.at[pl.ds(e * rows, rows)], token_sems.at[e]))
    for group in copies:
        for copy in group:
            copy.start()
    for which, group in enumerate(copies):
        for copy in group:
            copy.wait()
        block = near[which].reshape(depth, -1)
        for tile in row_tiles(held.shape[0]):
            product = jnp.dot(held[tile, :], block, preferred_element_type=jnp.float32)
            if earlier:
                product = earlier[0][which, tile, :].astype(jnp.float32) + product
            out_ref[which, tile, :] = product.astype(jnp.bfloat16)


def gate_up(tokens, streams, earlier=()):
    rows, depth = tokens[0].shape
    sources, stream_rows, cols = streams[1].shape
    all_rows = rows * len(tokens)
    return pl.pallas_call(
        functools.partial(gate_up_kernel, len(tokens)),
        in_specs=[ANY] * (len(tokens) + len(streams)) + [VMEM] * len(earlier),
        out_specs=VMEM,
        out_shape=jax.ShapeDtypeStruct((2, all_rows, cols), jnp.bfloat16),
        scratch_shapes=[
            pltpu.VMEM((all_rows, depth), jnp.bfloat16),
            pltpu.VMEM((2, sources, PARTS, stream_rows, cols), jnp.bfloat16),
            pltpu.SemaphoreType.DMA((len(tokens),)),
            pltpu.SemaphoreType.DMA((2, PARTS)),
        ],
        compiler_params=pltpu.CompilerParams(vmem_limit_bytes=VMEM_LIMIT),
        cost_estimate=BRIEF,
        name="gate_up",
    )(*tokens, *streams, *earlier)


def activation_kernel(here_ref, there_ref, out_ref):
    gate = here_ref[0].astype(jnp.float32) + there_ref[0].astype(jnp.float32)
    up = here_ref[1].astype(jnp.float32) + there_ref[1].astype(jnp.float32)
    out_ref[...] = (gate / (1.0 + jnp.exp(-gate)) * up).astype(jnp.bfloat16)


def activation(here, there):
    _, rows, cols = here.shape
    step = min(rows, ROW_TILE)
    return pl.pallas_call(
        activation_kernel,
        grid=(rows // step,),
        in_specs=[pl.BlockSpec((2, step, cols), lambda t: (0, t, 0))] * 2,
        out_specs=pl.BlockSpec((step, cols), lambda t: (t, 0)),
        out_shape=jax.ShapeDtypeStruct((rows, cols), jnp.bfloat16),
        compiler_params=pltpu.CompilerParams(vmem_limit_bytes=VMEM_LIMIT),
        cost_estimate=BRIEF,
        name="activation",
    )(here, there)


def down_kernel(activated_ref, weights_ref, kept_ref, sent_ref):
    sources, _, cols = weights_ref.shape
    kept_rows = kept_ref.shape[0]
    if cols % HEAD_WIDTH:
        blocks = [weights_ref[s] for s in range(sources)]
    else:
        blocks = [jnp.concatenate([weights_ref[s] for s in range(sources)], axis=1)]
    for e in range(sent_ref.shape[0] + 1):
        rows = activated_ref[e * kept_rows : (e + 1) * kept_rows, :]
        for s, block in enumerate(blocks):
            at = slice(s * block.shape[1], (s + 1) * block.shape[1])
            product = jnp.dot(rows, block, preferred_element_type=jnp.float32)
            if e == 0:
                kept_ref[:, at] = product.astype(jnp.bfloat16)
            else:
                sent_ref[e - 1, :, at] = product.astype(jnp.bfloat16)


def down_product(activated, weights, head_count):
    rows = activated.shape[0] // head_count
    sources, depth, cols = weights.shape
    return pl.pallas_call(
        down_kernel,
        in_specs=[VMEM, VMEM],
        out_specs=[VMEM, VMEM],
        out_shape=[
            jax.ShapeDtypeStruct((rows, sources * cols), jnp.bfloat16),
            jax.ShapeDtypeStruct((head_count - 1, rows, sources * cols), jnp.bfloat16),
        ],
        compiler_params=pltpu.CompilerParams(vmem_limit_bytes=VMEM_LIMIT),
        cost_estimate=BRIEF,
        name="down",
    )(activated, weights)


def per_device(query, key, value, doc_lengths, resid, norm_gain, w_out, w_gate_up, w_down):
    inner_count = lax.axis_size("inner")
    outer_count = lax.axis_size("outer")
    head_count = lax.axis_size("head")
    outer, inner, head = lax.axis_index("outer"), lax.axis_index("inner"), lax.axis_index("head")
    rows = query.shape[0]
    plane_rows = rows * inner_count * head_count
    reach = plane_rows * outer_count // WINDOW_PER_DOC
    feature_rows = w_gate_up.shape[1]
    hidden_cols = w_gate_up.shape[2] // outer_count
    bounds = jnp.cumsum(doc_lengths)
    hops = reach // plane_rows
    token_rows = plane_rows // inner_count
    half = plane_rows // head_count
    packing = (rows, head_count, KEY_VALUE_HEADS // head_count, -1)

    weights_out = lax.all_gather(w_out, "outer", axis=1, tiled=True)
    if packing[2] == inner_count and hops == 1:
        earlier = [lax.ppermute(part, "outer", [(s, s + 1) for s in range(outer_count - 1)]) for part in (key, value)]
        groups = jnp.concatenate([part.reshape(packing) for part in (query, key, value, *earlier)], axis=3)
        groups = jnp.transpose(groups, (2, 1, 0, 3)).reshape(inner_count * head_count, rows, -1)
        packed = lax.all_to_all(groups, ("inner", "head"), split_axis=0, concat_axis=0, tiled=True)
        packed = packed.reshape(plane_rows, -1)
        starts = document_starts(bounds, outer * plane_rows, plane_rows)
        own_context = attention(packed, packed, Q_COLS // KV_COLS + 1, starts, reach)
        blocks = blocks_over_inner(own_context)
    else:
        groups = jnp.concatenate([part.reshape(packing) for part in (query, key, value)], axis=3)
        groups = jnp.transpose(groups[:, :, 0], (1, 0, 2))
        packed = lax.all_to_all(groups, "head", split_axis=0, concat_axis=0, tiled=True).reshape(token_rows, -1)
        plane_kv = lax.all_gather(packed[:, Q_COLS:], "inner", axis=0, tiled=True)
        every_kv = jnp.concatenate([earlier_planes(plane_kv, hops), plane_kv], axis=0)
        halo = lax.dynamic_slice_in_dim(every_kv, inner * token_rows, reach, 0)
        starts = document_starts(bounds, outer * plane_rows + inner * token_rows, token_rows)
        own_context = attention(packed, halo, 0, starts, reach)
        blocks = [lax.all_gather(own_context, "inner", axis=0, tiled=True)]

    spread = functools.partial(lax.all_to_all, axis_name="outer", split_axis=0, concat_axis=0, tiled=True)
    over_y = functools.partial(swap, axis="inner", distance=2)
    fence = lambda *arrays: lax.optimization_barrier(arrays)
    own_gain = lax.dynamic_slice_in_dim(norm_gain, outer * feature_rows, feature_rows, 0)
    cut = cut_weights(w_gate_up, w_down, own_gain[:, None], outer_count)

    place = jnp.stack([inner, head]).astype(jnp.int32)
    first = spread(after(cut[0], weights_out))
    kept, sent, *whole = projection(blocks, weights_out, place, head_count, inner_count)
    context = whole[0] if whole else own_context
    projected = kept.astype(jnp.float32)
    for e in range(1, head_count):
        projected = projected + swap(sent[e - 1], "head", e).astype(jnp.float32)
    own_resid = lax.dynamic_slice_in_dim(resid, head * half, half, 0)
    hidden_part = (own_resid.astype(jnp.float32) + projected).astype(jnp.bfloat16)

    upper = inner // 2
    own_rows = half // 2
    mine = lax.dynamic_slice_in_dim(hidden_part, upper * own_rows, own_rows, 0)
    others = lax.dynamic_slice_in_dim(hidden_part, (1 - upper) * own_rows, own_rows, 0)
    others, first = fence(over_y(others), first)
    state = [mine.astype(jnp.float32), others.astype(jnp.float32)]
    squares = sum([jnp.sum(block * block, axis=1) for block in state])
    squares = squares + swap(squares, "inner", 1)
    inverse = lax.rsqrt(squares / D + 1e-05)[:, None]
    part_rows = feature_rows // PARTS
    normed = [(block * inverse).astype(jnp.bfloat16) for block in state]
    state = [block.reshape(own_rows, outer_count, PARTS, part_rows) for block in state]
    state = [[block[:, :, part].reshape(own_rows, -1) for part in range(PARTS)] for block in state]

    tokens = [lax.all_gather(block, "outer", axis=0, tiled=True) for block in normed]
    second, first_y, tokens, state = fence(spread(after(cut[1], normed[0])), over_y(first), tokens, state)
    tokens = [[swap(block, "head", e) if e else block for e in range(head_count)] for block in tokens]
    third, second_y, tokens[0] = fence(spread(after(cut[2], second)), over_y(second), tokens[0])
    own_sums = gate_up(tokens[0], [first, second, third])
    fourth, third_y, own_sums = fence(spread(after(cut[3], third)), over_y(third), own_sums)
    sums = gate_up(tokens[1], [first_y, second_y, third_y], [own_sums])
    activated = activation(sums, swap(sums, "inner", 1))

    def over_heads(weights):
        kept, sent = down_product(activated, weights, head_count)
        paired = kept.astype(jnp.float32)
        for e in range(1, head_count):
            paired = paired + swap(sent[e - 1], "head", e).astype(jnp.float32)
        return paired.reshape(outer_count, own_rows, -1)

    fifth, fourth_y, activated = fence(spread(after(cut[4], fourth)), over_y(fourth), activated)
    fifth_y = over_y(fifth)
    paired = {(0, 0): over_heads(fourth), (1, 0): over_heads(fourth_y), (0, 1): over_heads(fifth)}
    paired[1, 1] = over_heads(after(fifth_y, paired[0, 0]))

    pieces = [[None] * PARTS, [None] * PARTS]
    for part in range(PARTS):
        for a in range(2):
            total = state[a][part] + lax.dynamic_index_in_dim(paired[a, part], outer, 0, False)
            for d in range(1, outer_count):
                sent = lax.dynamic_index_in_dim(paired[a, part], outer ^ d, 0, False).astype(jnp.bfloat16)
                total = total + swap(sent, "outer", d).astype(jnp.float32)
            total = total.astype(jnp.bfloat16)
            pieces[a][part] = (over_y(total) if a else total).reshape(own_rows, outer_count, 1, part_rows)
    halves = [jnp.concatenate(parts, axis=2).reshape(own_rows, -1) for parts in pieces]
    layer_out = jnp.zeros((half, halves[0].shape[1]), jnp.bfloat16)
    layer_out = lax.dynamic_update_slice(layer_out, halves[0], (upper * own_rows, 0))
    layer_out = lax.dynamic_update_slice(layer_out, halves[1], ((1 - upper) * own_rows, 0))
    return (context, layer_out)


def solution(mesh):
    placed = (
        P(("outer", "inner", "head"), None),
        P(("outer", "inner", "head"), None),
        P(("outer", "inner", "head"), None),
        P(),
        P("outer", "inner"),
        P("inner"),
        P("head", ("inner", "outer")),
        P(None, ("inner", "outer"), "head"),
        P("head", ("inner", "outer")),
    )
    return jax.shard_map(
        per_device,
        mesh=mesh,
        in_specs=placed,
        out_specs=(P(("outer", "inner"), "head"), P(("outer", "head"), "inner")),
        check_vma=False,
    )
```

```python
import functools

import jax
import jax.numpy as jnp
from jax import lax
from jax.experimental import pallas as pl
from jax.experimental.pallas import tpu as pltpu
from jax.sharding import PartitionSpec as P

D = 4096
QUERY_HEADS = 32
KEY_VALUE_HEADS = 8
HEAD_WIDTH = 128
GROUP = QUERY_HEADS // KEY_VALUE_HEADS
Q_COLS = GROUP * HEAD_WIDTH
KV_COLS = 2 * HEAD_WIDTH
WINDOW_PER_DOC = 4
QUERY_TILE = 128
ROW_TILE = 256
PARTS = 2
VMEM_LIMIT = 48 * 1024 * 1024
BRIEF = pl.CostEstimate(flops=1, bytes_accessed=1, transcendentals=0)
ANY = pl.BlockSpec(memory_space=pl.ANY)
VMEM = pl.BlockSpec(memory_space=pltpu.VMEM)
SMEM = pl.BlockSpec(memory_space=pltpu.SMEM)


def swap(array, axis, distance):
    if distance == 0:
        return array
    count = lax.axis_size(axis)
    return lax.ppermute(array, axis, [(s, s ^ distance) for s in range(count)])


def after(array, earlier):
    return lax.optimization_barrier((array, earlier))[0]


def blocks_over_inner(block):
    across = swap(block, "inner", 2)
    return [block, swap(block, "inner", 1), across, swap(across, "inner", 1)]


def earlier_planes(kv, hops):
    count = lax.axis_size("outer")
    moved = [lax.ppermute(kv, "outer", [(s, s + d) for s in range(count - d)]) for d in range(hops, 0, -1)]
    return jnp.concatenate(moved, axis=0)


def document_starts(bounds, first, rows):
    place = first + jnp.arange(rows, dtype=jnp.int32)
    starts = jnp.max(jnp.where(bounds[None, :] <= place[:, None], bounds[None, :], 0), axis=1) - first
    return starts[:, None].astype(jnp.int32)


def row_tiles(rows):
    step = ROW_TILE if rows % ROW_TILE == 0 else rows
    return [slice(at, at + step) for at in range(0, rows, step)]


def attention_kernel(halo_rows, reach, starts_ref, queries_ref, own_ref, halo_ref, out_ref, keys, values):
    tile = pl.program_id(0)
    rows = queries_ref.shape[0]
    span = reach + rows

    @pl.when(tile == 0)
    def _():
        keys[:halo_rows, :] = halo_ref[:, :HEAD_WIDTH]
        values[:halo_rows, :] = halo_ref[:, HEAD_WIDTH:]
        keys[halo_rows:, :] = own_ref[:, :HEAD_WIDTH]
        values[halo_rows:, :] = own_ref[:, HEAD_WIDTH:]

    first = pl.multiple_of(tile * rows + (halo_rows - reach), rows)
    near_keys = keys[pl.ds(first, span), :]
    near_values = values[pl.ds(first, span), :]
    key_place = lax.broadcasted_iota(jnp.int32, (rows, span), 1)
    query_place = lax.broadcasted_iota(jnp.int32, (rows, span), 0) + reach
    start = starts_ref[...] - (first - halo_rows)
    allowed = (key_place <= query_place) & (key_place >= start)
    for g in range(GROUP):
        cols = slice(g * HEAD_WIDTH, (g + 1) * HEAD_WIDTH)
        scores = lax.dot_general(
            queries_ref[:, cols], near_keys, (((1,), (1,)), ((), ())), preferred_element_type=jnp.float32
        ) * (HEAD_WIDTH ** (-0.5))
        masked = jnp.where(allowed, scores, -1e30)
        row_max = jnp.max(masked, axis=1, keepdims=True)
        weights = jnp.exp(masked - row_max)
        totals = jnp.sum(weights, axis=1, keepdims=True)
        summed = jnp.dot(weights.astype(jnp.bfloat16), near_values, preferred_element_type=jnp.float32)
        out_ref[:, cols] = (summed / totals).astype(jnp.bfloat16)


def attention(packed, halo, halo_at, starts, reach):
    rows = packed.shape[0]
    halo_rows = halo.shape[0]
    return pl.pallas_call(
        functools.partial(attention_kernel, halo_rows, reach),
        grid=(rows // QUERY_TILE,),
        in_specs=[
            pl.BlockSpec((QUERY_TILE, 1), lambda t: (t, 0)),
            pl.BlockSpec((QUERY_TILE, Q_COLS), lambda t: (t, 0)),
            pl.BlockSpec((rows, KV_COLS), lambda t: (0, Q_COLS // KV_COLS)),
            pl.BlockSpec((halo_rows, KV_COLS), lambda t: (0, halo_at)),
        ],
        out_specs=pl.BlockSpec((QUERY_TILE, Q_COLS), lambda t: (t, 0)),
        out_shape=jax.ShapeDtypeStruct((rows, Q_COLS), jnp.bfloat16),
        scratch_shapes=[
            pltpu.VMEM((halo_rows + rows, HEAD_WIDTH), jnp.bfloat16),
            pltpu.VMEM((halo_rows + rows, HEAD_WIDTH), jnp.bfloat16),
        ],
        compiler_params=pltpu.CompilerParams(vmem_limit_bytes=VMEM_LIMIT),
        cost_estimate=BRIEF,
        name="attention",
    )(starts, packed, packed, halo)


def cut_kernel(gain_ref, gate_up_ref, down_ref, both_ref, gate_ref, up_ref, *down_refs):
    rows, cols = gate_ref.shape[1], down_refs[0].shape[2]
    for which, second_ref in enumerate((gate_ref, up_ref)):
        scaled = (gate_up_ref[which].astype(jnp.float32) * gain_ref[...]).astype(jnp.bfloat16)
        both_ref[0, which] = scaled[:rows]
        second_ref[0] = scaled[rows:]
    for part, out_ref in enumerate(down_refs):
        out_ref[0] = down_ref[:, part * cols : (part + 1) * cols]


def cut_weights(w_gate_up, w_down, gain, outer_count):
    _, features, width = w_gate_up.shape
    cols = width // outer_count
    rows = features // PARTS
    if cols % HEAD_WIDTH:
        wide = (w_gate_up.astype(jnp.float32) * gain[None]).astype(jnp.bfloat16)
        wide = jnp.transpose(wide.reshape(2, PARTS, rows, outer_count, cols), (1, 3, 0, 2, 4))
        tall = jnp.transpose(w_down.reshape(outer_count, cols, PARTS, rows), (2, 0, 1, 3))
        return [wide[0], wide[1, :, 0], wide[1, :, 1], *tall]
    return pl.pallas_call(
        cut_kernel,
        grid=(outer_count,),
        in_specs=[
            pl.BlockSpec((features, 1), lambda p: (0, 0)),
            pl.BlockSpec((2, features, cols), lambda p: (0, 0, p)),
            pl.BlockSpec((cols, features), lambda p: (p, 0)),
        ],
        out_specs=[pl.BlockSpec((1, 2, rows, cols), lambda p: (p, 0, 0, 0))]
        + [pl.BlockSpec((1, rows, cols), lambda p: (p, 0, 0))] * 2
        + [pl.BlockSpec((1, cols, rows), lambda p: (p, 0, 0))] * PARTS,
        out_shape=[jax.ShapeDtypeStruct((outer_count, 2, rows, cols), jnp.bfloat16)]
        + [jax.ShapeDtypeStruct((outer_count, rows, cols), jnp.bfloat16)] * 2
        + [jax.ShapeDtypeStruct((outer_count, cols, rows), jnp.bfloat16)] * PARTS,
        compiler_params=pltpu.CompilerParams(vmem_limit_bytes=VMEM_LIMIT),
        cost_estimate=BRIEF,
        name="cut_weights",
    )(gain, w_gate_up, w_down)


def projection_kernel(block_count, place_ref, *refs):
    blocks, weights_ref = refs[:block_count], refs[block_count]
    kept_ref, sent_ref = refs[block_count + 1 : block_count + 3]
    inner, head = place_ref[0], place_ref[1]
    half, depth = kept_ref.shape[0], blocks[0].shape[1]
    for e in range(sent_ref.shape[0] + 1):
        rows = pl.ds(pl.multiple_of((head ^ e) * half, half), half)
        total = jnp.zeros(kept_ref.shape, jnp.float32)
        for a, block in enumerate(blocks):
            at = pl.ds(pl.multiple_of((inner ^ a) * depth, depth), depth) if block_count > 1 else slice(None)
            total = total + jnp.dot(block[rows, :], weights_ref[at, :], preferred_element_type=jnp.float32)
        if e == 0:
            kept_ref[...] = total.astype(jnp.bfloat16)
        else:
            sent_ref[e - 1] = total.astype(jnp.bfloat16)
    if block_count > 1:
        context_ref = refs[block_count + 3]
        tokens = context_ref.shape[0]
        own = pl.ds(pl.multiple_of(inner * tokens, tokens), tokens)
        for a, block in enumerate(blocks):
            context_ref[:, pl.ds(pl.multiple_of((inner ^ a) * depth, depth), depth)] = block[own, :]


def projection(blocks, weights, place, head_count, inner_count):
    rows, depth = blocks[0].shape
    half, width = rows // head_count, weights.shape[1]
    outs = [(half, width), (head_count - 1, half, width)]
    if len(blocks) > 1:
        outs.append((rows // inner_count, len(blocks) * depth))
    return pl.pallas_call(
        functools.partial(projection_kernel, len(blocks)),
        in_specs=[SMEM] + [VMEM] * (len(blocks) + 1),
        out_specs=[VMEM] * len(outs),
        out_shape=[jax.ShapeDtypeStruct(shape, jnp.bfloat16) for shape in outs],
        compiler_params=pltpu.CompilerParams(vmem_limit_bytes=VMEM_LIMIT),
        cost_estimate=BRIEF,
        name="projection",
    )(place, *blocks, weights)


def gate_up_kernel(head_count, *refs):
    tokens = refs[:head_count]
    both, gate, up = refs[head_count : head_count + 3]
    *earlier, out_ref, held, near, token_sems, weight_sems = refs[head_count + 3 :]
    rows, depth = tokens[0].shape
    copies = [
        [pltpu.make_async_copy(both.at[:, which], near.at[which, :, 0], weight_sems.at[which, 0]),
         pltpu.make_async_copy(second, near.at[which, :, 1], weight_sems.at[which, 1])]
        for which, second in enumerate((gate, up))
    ]
    for e, token_ref in enumerate(tokens):
        copies[0].append(pltpu.make_async_copy(token_ref, held.at[pl.ds(e * rows, rows)], token_sems.at[e]))
    for group in copies:
        for copy in group:
            copy.start()
    for which, group in enumerate(copies):
        for copy in group:
            copy.wait()
        block = near[which].reshape(depth, -1)
        for tile in row_tiles(held.shape[0]):
            product = jnp.dot(held[tile, :], block, preferred_element_type=jnp.float32)
            if earlier:
                product = earlier[0][which, tile, :].astype(jnp.float32) + product
            out_ref[which, tile, :] = product.astype(jnp.bfloat16)


def gate_up(tokens, streams, earlier=()):
    rows, depth = tokens[0].shape
    sources, stream_rows, cols = streams[1].shape
    all_rows = rows * len(tokens)
    return pl.pallas_call(
        functools.partial(gate_up_kernel, len(tokens)),
        in_specs=[ANY] * (len(tokens) + len(streams)) + [VMEM] * len(earlier),
        out_specs=VMEM,
        out_shape=jax.ShapeDtypeStruct((2, all_rows, cols), jnp.bfloat16),
        scratch_shapes=[
            pltpu.VMEM((all_rows, depth), jnp.bfloat16),
            pltpu.VMEM((2, sources, PARTS, stream_rows, cols), jnp.bfloat16),
            pltpu.SemaphoreType.DMA((len(tokens),)),
            pltpu.SemaphoreType.DMA((2, PARTS)),
        ],
        compiler_params=pltpu.CompilerParams(vmem_limit_bytes=VMEM_LIMIT),
        cost_estimate=BRIEF,
        name="gate_up",
    )(*tokens, *streams, *earlier)


def activation_kernel(here_ref, there_ref, out_ref):
    gate = here_ref[0].astype(jnp.float32) + there_ref[0].astype(jnp.float32)
    up = here_ref[1].astype(jnp.float32) + there_ref[1].astype(jnp.float32)
    out_ref[...] = (gate / (1.0 + jnp.exp(-gate)) * up).astype(jnp.bfloat16)


def activation(here, there):
    _, rows, cols = here.shape
    step = min(rows, ROW_TILE)
    return pl.pallas_call(
        activation_kernel,
        grid=(rows // step,),
        in_specs=[pl.BlockSpec((2, step, cols), lambda t: (0, t, 0))] * 2,
        out_specs=pl.BlockSpec((step, cols), lambda t: (t, 0)),
        out_shape=jax.ShapeDtypeStruct((rows, cols), jnp.bfloat16),
        compiler_params=pltpu.CompilerParams(vmem_limit_bytes=VMEM_LIMIT),
        cost_estimate=BRIEF,
        name="activation",
    )(here, there)


def down_kernel(activated_ref, weights_ref, kept_ref, sent_ref):
    sources, _, cols = weights_ref.shape
    kept_rows = kept_ref.shape[0]
    if cols % HEAD_WIDTH:
        blocks = [weights_ref[s] for s in range(sources)]
    else:
        blocks = [jnp.concatenate([weights_ref[s] for s in range(sources)], axis=1)]
    for e in range(sent_ref.shape[0] + 1):
        rows = activated_ref[e * kept_rows : (e + 1) * kept_rows, :]
        for s, block in enumerate(blocks):
            at = slice(s * block.shape[1], (s + 1) * block.shape[1])
            product = jnp.dot(rows, block, preferred_element_type=jnp.float32)
            if e == 0:
                kept_ref[:, at] = product.astype(jnp.bfloat16)
            else:
                sent_ref[e - 1, :, at] = product.astype(jnp.bfloat16)


def down_product(activated, weights, head_count):
    rows = activated.shape[0] // head_count
    sources, depth, cols = weights.shape
    return pl.pallas_call(
        down_kernel,
        in_specs=[VMEM, VMEM],
        out_specs=[VMEM, VMEM],
        out_shape=[
            jax.ShapeDtypeStruct((rows, sources * cols), jnp.bfloat16),
            jax.ShapeDtypeStruct((head_count - 1, rows, sources * cols), jnp.bfloat16),
        ],
        compiler_params=pltpu.CompilerParams(vmem_limit_bytes=VMEM_LIMIT),
        cost_estimate=BRIEF,
        name="down",
    )(activated, weights)


def per_device(query, key, value, doc_lengths, resid, norm_gain, w_out, w_gate_up, w_down):
    inner_count = lax.axis_size("inner")
    outer_count = lax.axis_size("outer")
    head_count = lax.axis_size("head")
    outer, inner, head = lax.axis_index("outer"), lax.axis_index("inner"), lax.axis_index("head")
    rows = query.shape[0]
    plane_rows = rows * inner_count * head_count
    reach = plane_rows * outer_count // WINDOW_PER_DOC
    feature_rows = w_gate_up.shape[1]
    hidden_cols = w_gate_up.shape[2] // outer_count
    bounds = jnp.cumsum(doc_lengths)
    hops = reach // plane_rows
    token_rows = plane_rows // inner_count
    half = plane_rows // head_count
    packing = (rows, head_count, KEY_VALUE_HEADS // head_count, -1)

    weights_out = lax.all_gather(w_out, "outer", axis=1, tiled=True)
    if packing[2] == inner_count and hops == 1:
        earlier = [lax.ppermute(part, "outer", [(s, s + 1) for s in range(outer_count - 1)]) for part in (key, value)]
        groups = jnp.concatenate([part.reshape(packing) for part in (query, key, value, *earlier)], axis=3)
        groups = jnp.transpose(groups, (2, 1, 0, 3)).reshape(inner_count * head_count, rows, -1)
        packed = lax.all_to_all(groups, ("inner", "head"), split_axis=0, concat_axis=0, tiled=True)
        packed = packed.reshape(plane_rows, -1)
        starts = document_starts(bounds, outer * plane_rows, plane_rows)
        own_context = attention(packed, packed, Q_COLS // KV_COLS + 1, starts, reach)
        blocks = blocks_over_inner(own_context)
    else:
        groups = jnp.concatenate([part.reshape(packing) for part in (query, key, value)], axis=3)
        groups = jnp.transpose(groups[:, :, 0], (1, 0, 2))
        packed = lax.all_to_all(groups, "head", split_axis=0, concat_axis=0, tiled=True).reshape(token_rows, -1)
        plane_kv = lax.all_gather(packed[:, Q_COLS:], "inner", axis=0, tiled=True)
        every_kv = jnp.concatenate([earlier_planes(plane_kv, hops), plane_kv], axis=0)
        halo = lax.dynamic_slice_in_dim(every_kv, inner * token_rows, reach, 0)
        starts = document_starts(bounds, outer * plane_rows + inner * token_rows, token_rows)
        own_context = attention(packed, halo, 0, starts, reach)
        blocks = [lax.all_gather(own_context, "inner", axis=0, tiled=True)]

    spread = functools.partial(lax.all_to_all, axis_name="outer", split_axis=0, concat_axis=0, tiled=True)
    over_y = functools.partial(swap, axis="inner", distance=2)
    fence = lambda *arrays: lax.optimization_barrier(arrays)
    own_gain = lax.dynamic_slice_in_dim(norm_gain, outer * feature_rows, feature_rows, 0)
    cut = cut_weights(w_gate_up, w_down, own_gain[:, None], outer_count)

    place = jnp.stack([inner, head]).astype(jnp.int32)
    weights_out, *blocks = fence(weights_out, *blocks)
    first = spread(after(cut[0], weights_out))
    kept, sent, *whole = projection(blocks, weights_out, place, head_count, inner_count)
    context = whole[0] if whole else own_context
    projected = kept.astype(jnp.float32)
    for e in range(1, head_count):
        projected = projected + swap(sent[e - 1], "head", e).astype(jnp.float32)
    own_resid = lax.dynamic_slice_in_dim(resid, head * half, half, 0)
    hidden_part = (own_resid.astype(jnp.float32) + projected).astype(jnp.bfloat16)

    upper = inner // 2
    own_rows = half // 2
    mine = lax.dynamic_slice_in_dim(hidden_part, upper * own_rows, own_rows, 0)
    others = lax.dynamic_slice_in_dim(hidden_part, (1 - upper) * own_rows, own_rows, 0)
    others, first = fence(over_y(others), first)
    state = [mine.astype(jnp.float32), others.astype(jnp.float32)]
    squares = sum([jnp.sum(block * block, axis=1) for block in state])
    squares = squares + swap(squares, "inner", 1)
    inverse = lax.rsqrt(squares / D + 1e-05)[:, None]
    part_rows = feature_rows // PARTS
    normed = jnp.concatenate([block * inverse for block in state], axis=1).astype(jnp.bfloat16)
    state = [block.reshape(own_rows, outer_count, PARTS, part_rows) for block in state]
    state = [[block[:, :, part].reshape(own_rows, -1) for part in range(PARTS)] for block in state]

    tokens = lax.all_gather(normed, "outer", axis=0, tiled=True)
    second, first_y, tokens, state = fence(spread(after(cut[1], normed)), over_y(first), tokens, state)
    tokens = jnp.split(tokens, 2, axis=1)
    tokens = [[swap(block, "head", e) if e else block for e in range(head_count)] for block in tokens]
    third, second_y, tokens[0] = fence(spread(after(cut[2], second)), over_y(second), tokens[0])
    own_sums = gate_up(tokens[0], [first, second, third])
    fourth, third_y, own_sums = fence(spread(after(cut[3], third)), over_y(third), own_sums)
    sums = gate_up(tokens[1], [first_y, second_y, third_y], [own_sums])
    activated = activation(sums, swap(sums, "inner", 1))

    def over_heads(weights):
        kept, sent = down_product(activated, weights, head_count)
        paired = kept.astype(jnp.float32)
        for e in range(1, head_count):
            paired = paired + swap(sent[e - 1], "head", e).astype(jnp.float32)
        return paired.reshape(outer_count, own_rows, -1)

    paired = {(0, 0): over_heads(fourth)}
    fifth, fourth_y, paired[0, 0] = fence(spread(after(cut[4], fourth)), over_y(fourth), paired[0, 0])
    fifth_y = over_y(fifth)
    paired[1, 0] = over_heads(fourth_y)
    paired[0, 1] = over_heads(fifth)
    paired[1, 1] = over_heads(after(fifth_y, paired[1, 0]))

    pieces = [[None] * PARTS, [None] * PARTS]
    for part in range(PARTS):
        for a in range(2):
            total = state[a][part] + lax.dynamic_index_in_dim(paired[a, part], outer, 0, False)
            for d in range(1, outer_count):
                sent = lax.dynamic_index_in_dim(paired[a, part], outer ^ d, 0, False).astype(jnp.bfloat16)
                total = total + swap(sent, "outer", d).astype(jnp.float32)
            total = total.astype(jnp.bfloat16)
            pieces[a][part] = (over_y(total) if a else total).reshape(own_rows, outer_count, 1, part_rows)
    halves = [jnp.concatenate(parts, axis=2).reshape(own_rows, -1) for parts in pieces]
    layer_out = jnp.zeros((half, halves[0].shape[1]), jnp.bfloat16)
    layer_out = lax.dynamic_update_slice(layer_out, halves[0], (upper * own_rows, 0))
    layer_out = lax.dynamic_update_slice(layer_out, halves[1], ((1 - upper) * own_rows, 0))
    return (context, layer_out)


def solution(mesh):
    placed = (
        P(("outer", "inner", "head"), None),
        P(("outer", "inner", "head"), None),
        P(("outer", "inner", "head"), None),
        P(),
        P("outer", "inner"),
        P("inner"),
        P("head", ("inner", "outer")),
        P(None, ("inner", "outer"), "head"),
        P("head", ("inner", "outer")),
    )
    return jax.shard_map(
        per_device,
        mesh=mesh,
        in_specs=placed,
        out_specs=(P(("outer", "inner"), "head"), P(("outer", "head"), "inner")),
        check_vma=False,
    )
```

```python
import functools

import jax
import jax.numpy as jnp
from jax import lax
from jax.experimental import pallas as pl
from jax.experimental.pallas import tpu as pltpu
from jax.sharding import PartitionSpec as P

D = 4096
QUERY_HEADS = 32
KEY_VALUE_HEADS = 8
HEAD_WIDTH = 128
GROUP = QUERY_HEADS // KEY_VALUE_HEADS
Q_COLS = GROUP * HEAD_WIDTH
KV_COLS = 2 * HEAD_WIDTH
WINDOW_PER_DOC = 4
QUERY_TILE = 128
ROW_TILE = 256
PARTS = 2
VMEM_LIMIT = 48 * 1024 * 1024
BRIEF = pl.CostEstimate(flops=1, bytes_accessed=1, transcendentals=0)
ANY = pl.BlockSpec(memory_space=pl.ANY)
VMEM = pl.BlockSpec(memory_space=pltpu.VMEM)
SMEM = pl.BlockSpec(memory_space=pltpu.SMEM)


def swap(array, axis, distance):
    if distance == 0:
        return array
    count = lax.axis_size(axis)
    return lax.ppermute(array, axis, [(s, s ^ distance) for s in range(count)])


def after(array, earlier):
    return lax.optimization_barrier((array, earlier))[0]


def blocks_over_inner(block):
    across = swap(block, "inner", 2)
    return [block, swap(block, "inner", 1), across, swap(across, "inner", 1)]


def earlier_planes(kv, hops):
    count = lax.axis_size("outer")
    moved = [lax.ppermute(kv, "outer", [(s, s + d) for s in range(count - d)]) for d in range(hops, 0, -1)]
    return jnp.concatenate(moved, axis=0)


def document_starts(bounds, first, rows):
    place = first + jnp.arange(rows, dtype=jnp.int32)
    starts = jnp.max(jnp.where(bounds[None, :] <= place[:, None], bounds[None, :], 0), axis=1) - first
    return starts[:, None].astype(jnp.int32)


def row_tiles(rows):
    step = ROW_TILE if rows % ROW_TILE == 0 else rows
    return [slice(at, at + step) for at in range(0, rows, step)]


def attention_kernel(halo_rows, reach, starts_ref, queries_ref, own_ref, halo_ref, out_ref, keys, values):
    tile = pl.program_id(0)
    rows = queries_ref.shape[0]
    span = reach + rows

    @pl.when(tile == 0)
    def _():
        keys[:halo_rows, :] = halo_ref[:, :HEAD_WIDTH]
        values[:halo_rows, :] = halo_ref[:, HEAD_WIDTH:]
        keys[halo_rows:, :] = own_ref[:, :HEAD_WIDTH]
        values[halo_rows:, :] = own_ref[:, HEAD_WIDTH:]

    first = pl.multiple_of(tile * rows + (halo_rows - reach), rows)
    near_keys = keys[pl.ds(first, span), :]
    near_values = values[pl.ds(first, span), :]
    key_place = lax.broadcasted_iota(jnp.int32, (rows, span), 1)
    query_place = lax.broadcasted_iota(jnp.int32, (rows, span), 0) + reach
    start = starts_ref[...] - (first - halo_rows)
    allowed = (key_place <= query_place) & (key_place >= start)
    for g in range(GROUP):
        cols = slice(g * HEAD_WIDTH, (g + 1) * HEAD_WIDTH)
        scores = lax.dot_general(
            queries_ref[:, cols], near_keys, (((1,), (1,)), ((), ())), preferred_element_type=jnp.float32
        ) * (HEAD_WIDTH ** (-0.5))
        masked = jnp.where(allowed, scores, -1e30)
        row_max = jnp.max(masked, axis=1, keepdims=True)
        weights = jnp.exp(masked - row_max)
        totals = jnp.sum(weights, axis=1, keepdims=True)
        summed = jnp.dot(weights.astype(jnp.bfloat16), near_values, preferred_element_type=jnp.float32)
        out_ref[:, cols] = (summed / totals).astype(jnp.bfloat16)


def attention(packed, halo, halo_at, starts, reach):
    rows = packed.shape[0]
    halo_rows = halo.shape[0]
    return pl.pallas_call(
        functools.partial(attention_kernel, halo_rows, reach),
        grid=(rows // QUERY_TILE,),
        in_specs=[
            pl.BlockSpec((QUERY_TILE, 1), lambda t: (t, 0)),
            pl.BlockSpec((QUERY_TILE, Q_COLS), lambda t: (t, 0)),
            pl.BlockSpec((rows, KV_COLS), lambda t: (0, Q_COLS // KV_COLS)),
            pl.BlockSpec((halo_rows, KV_COLS), lambda t: (0, halo_at)),
        ],
        out_specs=pl.BlockSpec((QUERY_TILE, Q_COLS), lambda t: (t, 0)),
        out_shape=jax.ShapeDtypeStruct((rows, Q_COLS), jnp.bfloat16),
        scratch_shapes=[
            pltpu.VMEM((halo_rows + rows, HEAD_WIDTH), jnp.bfloat16),
            pltpu.VMEM((halo_rows + rows, HEAD_WIDTH), jnp.bfloat16),
        ],
        compiler_params=pltpu.CompilerParams(vmem_limit_bytes=VMEM_LIMIT),
        cost_estimate=BRIEF,
        name="attention",
    )(starts, packed, packed, halo)


def cut_kernel(gain_ref, gate_up_ref, down_ref, both_ref, gate_ref, up_ref, out_ref):
    rows, cols = gate_ref.shape[1], out_ref.shape[3]
    for which, second_ref in enumerate((gate_ref, up_ref)):
        scaled = (gate_up_ref[which].astype(jnp.float32) * gain_ref[...]).astype(jnp.bfloat16)
        both_ref[0, which] = scaled[:rows]
        second_ref[0] = scaled[rows:]
    for part in range(PARTS):
        out_ref[0, part] = down_ref[:, part * cols : (part + 1) * cols]


def cut_weights(w_gate_up, w_down, gain, outer_count):
    _, features, width = w_gate_up.shape
    cols = width // outer_count
    rows = features // PARTS
    if cols % HEAD_WIDTH:
        wide = (w_gate_up.astype(jnp.float32) * gain[None]).astype(jnp.bfloat16)
        wide = jnp.transpose(wide.reshape(2, PARTS, rows, outer_count, cols), (1, 3, 0, 2, 4))
        tall = jnp.transpose(w_down.reshape(outer_count, cols, PARTS, rows), (0, 2, 1, 3))
        return [wide[0], wide[1, :, 0], wide[1, :, 1], tall]
    return pl.pallas_call(
        cut_kernel,
        grid=(outer_count,),
        in_specs=[
            pl.BlockSpec((features, 1), lambda p: (0, 0)),
            pl.BlockSpec((2, features, cols), lambda p: (0, 0, p)),
            pl.BlockSpec((cols, features), lambda p: (p, 0)),
        ],
        out_specs=[pl.BlockSpec((1, 2, rows, cols), lambda p: (p, 0, 0, 0))]
        + [pl.BlockSpec((1, rows, cols), lambda p: (p, 0, 0))] * 2
        + [pl.BlockSpec((1, PARTS, cols, rows), lambda p: (p, 0, 0, 0))],
        out_shape=[jax.ShapeDtypeStruct((outer_count, 2, rows, cols), jnp.bfloat16)]
        + [jax.ShapeDtypeStruct((outer_count, rows, cols), jnp.bfloat16)] * 2
        + [jax.ShapeDtypeStruct((outer_count, PARTS, cols, rows), jnp.bfloat16)],
        compiler_params=pltpu.CompilerParams(vmem_limit_bytes=VMEM_LIMIT),
        cost_estimate=BRIEF,
        name="cut_weights",
    )(gain, w_gate_up, w_down)


def projection_kernel(block_count, place_ref, *refs):
    blocks, weights_ref = refs[:block_count], refs[block_count]
    kept_ref, sent_ref = refs[block_count + 1 : block_count + 3]
    inner, head = place_ref[0], place_ref[1]
    half, depth = kept_ref.shape[0], blocks[0].shape[1]
    for e in range(sent_ref.shape[0] + 1):
        rows = pl.ds(pl.multiple_of((head ^ e) * half, half), half)
        total = jnp.zeros(kept_ref.shape, jnp.float32)
        for a, block in enumerate(blocks):
            at = pl.ds(pl.multiple_of((inner ^ a) * depth, depth), depth) if block_count > 1 else slice(None)
            total = total + jnp.dot(block[rows, :], weights_ref[at, :], preferred_element_type=jnp.float32)
        if e == 0:
            kept_ref[...] = total.astype(jnp.bfloat16)
        else:
            sent_ref[e - 1] = total.astype(jnp.bfloat16)
    if block_count > 1:
        context_ref = refs[block_count + 3]
        tokens = context_ref.shape[0]
        own = pl.ds(pl.multiple_of(inner * tokens, tokens), tokens)
        for a, block in enumerate(blocks):
            context_ref[:, pl.ds(pl.multiple_of((inner ^ a) * depth, depth), depth)] = block[own, :]


def projection(blocks, weights, place, head_count, inner_count):
    rows, depth = blocks[0].shape
    half, width = rows // head_count, weights.shape[1]
    outs = [(half, width), (head_count - 1, half, width)]
    if len(blocks) > 1:
        outs.append((rows // inner_count, len(blocks) * depth))
    return pl.pallas_call(
        functools.partial(projection_kernel, len(blocks)),
        in_specs=[SMEM] + [VMEM] * (len(blocks) + 1),
        out_specs=[VMEM] * len(outs),
        out_shape=[jax.ShapeDtypeStruct(shape, jnp.bfloat16) for shape in outs],
        compiler_params=pltpu.CompilerParams(vmem_limit_bytes=VMEM_LIMIT),
        cost_estimate=BRIEF,
        name="projection",
    )(place, *blocks, weights)


def gate_up_kernel(head_count, *refs):
    tokens = refs[:head_count]
    both, gate, up = refs[head_count : head_count + 3]
    *earlier, out_ref, held, near, token_sems, weight_sems = refs[head_count + 3 :]
    rows, depth = tokens[0].shape
    copies = [
        [pltpu.make_async_copy(both.at[:, which], near.at[which, :, 0], weight_sems.at[which, 0]),
         pltpu.make_async_copy(second, near.at[which, :, 1], weight_sems.at[which, 1])]
        for which, second in enumerate((gate, up))
    ]
    for e, token_ref in enumerate(tokens):
        copies[0].append(pltpu.make_async_copy(token_ref, held.at[pl.ds(e * rows, rows)], token_sems.at[e]))
    for group in copies:
        for copy in group:
            copy.start()
    for which, group in enumerate(copies):
        for copy in group:
            copy.wait()
        block = near[which].reshape(depth, -1)
        for tile in row_tiles(held.shape[0]):
            product = jnp.dot(held[tile, :], block, preferred_element_type=jnp.float32)
            if earlier:
                product = earlier[0][which, tile, :].astype(jnp.float32) + product
            out_ref[which, tile, :] = product.astype(jnp.bfloat16)


def gate_up(tokens, streams, earlier=()):
    rows, depth = tokens[0].shape
    sources, stream_rows, cols = streams[1].shape
    all_rows = rows * len(tokens)
    return pl.pallas_call(
        functools.partial(gate_up_kernel, len(tokens)),
        in_specs=[ANY] * (len(tokens) + len(streams)) + [VMEM] * len(earlier),
        out_specs=VMEM,
        out_shape=jax.ShapeDtypeStruct((2, all_rows, cols), jnp.bfloat16),
        scratch_shapes=[
            pltpu.VMEM((all_rows, depth), jnp.bfloat16),
            pltpu.VMEM((2, sources, PARTS, stream_rows, cols), jnp.bfloat16),
            pltpu.SemaphoreType.DMA((len(tokens),)),
            pltpu.SemaphoreType.DMA((2, PARTS)),
        ],
        compiler_params=pltpu.CompilerParams(vmem_limit_bytes=VMEM_LIMIT),
        cost_estimate=BRIEF,
        name="gate_up",
    )(*tokens, *streams, *earlier)


def activation_kernel(here_ref, there_ref, out_ref):
    gate = here_ref[0].astype(jnp.float32) + there_ref[0].astype(jnp.float32)
    up = here_ref[1].astype(jnp.float32) + there_ref[1].astype(jnp.float32)
    out_ref[...] = (gate / (1.0 + jnp.exp(-gate)) * up).astype(jnp.bfloat16)


def activation(here, there):
    _, rows, cols = here.shape
    step = min(rows, ROW_TILE)
    return pl.pallas_call(
        activation_kernel,
        grid=(rows // step,),
        in_specs=[pl.BlockSpec((2, step, cols), lambda t: (0, t, 0))] * 2,
        out_specs=pl.BlockSpec((step, cols), lambda t: (t, 0)),
        out_shape=jax.ShapeDtypeStruct((rows, cols), jnp.bfloat16),
        compiler_params=pltpu.CompilerParams(vmem_limit_bytes=VMEM_LIMIT),
        cost_estimate=BRIEF,
        name="activation",
    )(here, there)


def down_kernel(activated_ref, weights_ref, kept_ref, sent_ref):
    sources, _, _, cols = weights_ref.shape
    kept_rows = kept_ref.shape[0]
    if cols % HEAD_WIDTH:
        blocks = [weights_ref[s, 0] for s in range(sources)]
    else:
        blocks = [jnp.concatenate([weights_ref[s, 0] for s in range(sources)], axis=1)]
    for e in range(sent_ref.shape[0] + 1):
        rows = activated_ref[e * kept_rows : (e + 1) * kept_rows, :]
        for s, block in enumerate(blocks):
            at = slice(s * block.shape[1], (s + 1) * block.shape[1])
            product = jnp.dot(rows, block, preferred_element_type=jnp.float32)
            if e == 0:
                kept_ref[:, at] = product.astype(jnp.bfloat16)
            else:
                sent_ref[e - 1, :, at] = product.astype(jnp.bfloat16)


def down_product(activated, weights, part, head_count):
    rows = activated.shape[0] // head_count
    sources, _, depth, cols = weights.shape
    wide = sources * cols
    return pl.pallas_call(
        down_kernel,
        grid=(1,),
        in_specs=[
            pl.BlockSpec(activated.shape, lambda t: (0, 0)),
            pl.BlockSpec((sources, 1, depth, cols), lambda t: (0, part, 0, 0)),
        ],
        out_specs=[
            pl.BlockSpec((rows, wide), lambda t: (0, 0)),
            pl.BlockSpec((head_count - 1, rows, wide), lambda t: (0, 0, 0)),
        ],
        out_shape=[
            jax.ShapeDtypeStruct((rows, sources * cols), jnp.bfloat16),
            jax.ShapeDtypeStruct((head_count - 1, rows, sources * cols), jnp.bfloat16),
        ],
        compiler_params=pltpu.CompilerParams(vmem_limit_bytes=VMEM_LIMIT),
        cost_estimate=BRIEF,
        name="down",
    )(activated, weights)


def per_device(query, key, value, doc_lengths, resid, norm_gain, w_out, w_gate_up, w_down):
    inner_count = lax.axis_size("inner")
    outer_count = lax.axis_size("outer")
    head_count = lax.axis_size("head")
    outer, inner, head = lax.axis_index("outer"), lax.axis_index("inner"), lax.axis_index("head")
    rows = query.shape[0]
    plane_rows = rows * inner_count * head_count
    reach = plane_rows * outer_count // WINDOW_PER_DOC
    feature_rows = w_gate_up.shape[1]
    hidden_cols = w_gate_up.shape[2] // outer_count
    bounds = jnp.cumsum(doc_lengths)
    hops = reach // plane_rows
    token_rows = plane_rows // inner_count
    half = plane_rows // head_count
    packing = (rows, head_count, KEY_VALUE_HEADS // head_count, -1)

    weights_out = lax.all_gather(w_out, "outer", axis=1, tiled=True)
    if packing[2] == inner_count and hops == 1:
        earlier = [lax.ppermute(part, "outer", [(s, s + 1) for s in range(outer_count - 1)]) for part in (key, value)]
        groups = jnp.concatenate([part.reshape(packing) for part in (query, key, value, *earlier)], axis=3)
        groups = jnp.transpose(groups, (2, 1, 0, 3)).reshape(inner_count * head_count, rows, -1)
        packed = lax.all_to_all(groups, ("inner", "head"), split_axis=0, concat_axis=0, tiled=True)
        packed = packed.reshape(plane_rows, -1)
        starts = document_starts(bounds, outer * plane_rows, plane_rows)
        own_context = attention(packed, packed, Q_COLS // KV_COLS + 1, starts, reach)
        blocks = blocks_over_inner(own_context)
    else:
        groups = jnp.concatenate([part.reshape(packing) for part in (query, key, value)], axis=3)
        groups = jnp.transpose(groups[:, :, 0], (1, 0, 2))
        packed = lax.all_to_all(groups, "head", split_axis=0, concat_axis=0, tiled=True).reshape(token_rows, -1)
        plane_kv = lax.all_gather(packed[:, Q_COLS:], "inner", axis=0, tiled=True)
        every_kv = jnp.concatenate([earlier_planes(plane_kv, hops), plane_kv], axis=0)
        halo = lax.dynamic_slice_in_dim(every_kv, inner * token_rows, reach, 0)
        starts = document_starts(bounds, outer * plane_rows + inner * token_rows, token_rows)
        own_context = attention(packed, halo, 0, starts, reach)
        blocks = [lax.all_gather(own_context, "inner", axis=0, tiled=True)]

    spread = functools.partial(lax.all_to_all, axis_name="outer", split_axis=0, concat_axis=0, tiled=True)
    over_y = functools.partial(swap, axis="inner", distance=2)
    fence = lambda *arrays: lax.optimization_barrier(arrays)
    own_gain = lax.dynamic_slice_in_dim(norm_gain, outer * feature_rows, feature_rows, 0)
    cut = cut_weights(w_gate_up, w_down, own_gain[:, None], outer_count)

    place = jnp.stack([inner, head]).astype(jnp.int32)
    weights_out, *blocks = fence(weights_out, *blocks)
    first = spread(after(cut[0], weights_out))
    kept, sent, *whole = projection(blocks, weights_out, place, head_count, inner_count)
    context = whole[0] if whole else own_context
    projected = kept.astype(jnp.float32)
    for e in range(1, head_count):
        projected = projected + swap(sent[e - 1], "head", e).astype(jnp.float32)
    own_resid = lax.dynamic_slice_in_dim(resid, head * half, half, 0)
    hidden_part = (own_resid.astype(jnp.float32) + projected).astype(jnp.bfloat16)

    upper = inner // 2
    own_rows = half // 2
    mine = lax.dynamic_slice_in_dim(hidden_part, upper * own_rows, own_rows, 0)
    others = lax.dynamic_slice_in_dim(hidden_part, (1 - upper) * own_rows, own_rows, 0)
    state = [mine.astype(jnp.float32), over_y(others).astype(jnp.float32)]
    squares = sum([jnp.sum(block * block, axis=1) for block in state])
    squares = squares + swap(squares, "inner", 1)
    inverse = lax.rsqrt(squares / D + 1e-05)[:, None]
    part_rows = feature_rows // PARTS
    normed = jnp.concatenate([block * inverse for block in state], axis=1).astype(jnp.bfloat16)
    state = [block.reshape(own_rows, outer_count, PARTS, part_rows) for block in state]
    state = [[block[:, :, part].reshape(own_rows, -1) for part in range(PARTS)] for block in state]

    tokens = lax.all_gather(normed, "outer", axis=0, tiled=True)
    first = after(first, normed)
    second, first_y, state = fence(spread(after(cut[1], tokens)), over_y(first), state)
    tokens = jnp.split(tokens, 2, axis=1)
    tokens = [[swap(block, "head", e) if e else block for e in range(head_count)] for block in tokens]
    third, second_y, tokens[0] = fence(spread(after(cut[2], second)), over_y(second), tokens[0])
    own_sums = gate_up(tokens[0], [first, second, third])
    fourth = spread(after(cut[3], third))
    third_y, own_sums = fence(over_y(third), own_sums)
    sums = gate_up(tokens[1], [first_y, second_y, third_y], [own_sums])
    activated = activation(sums, swap(sums, "inner", 1))

    def over_heads(weights, part):
        kept, sent = down_product(activated, weights, part, head_count)
        moved = kept.astype(jnp.float32)
        for e in range(1, head_count):
            moved = moved + swap(sent[e - 1], "head", e).astype(jnp.float32)
        return moved.reshape(outer_count, own_rows, -1)

    fourth_y = [over_y(fourth[:, part : part + 1]) for part in range(PARTS)]
    paired = {(0, part): over_heads(fourth, part) for part in range(PARTS)}
    for part in range(PARTS):
        paired[1, part] = over_heads(after(fourth_y[part], paired[0, part]), 0)

    pieces = [[None] * PARTS, [None] * PARTS]
    for part in range(PARTS):
        for a in range(2):
            total = state[a][part] + lax.dynamic_index_in_dim(paired[a, part], outer, 0, False)
            for d in range(1, outer_count):
                sent = lax.dynamic_index_in_dim(paired[a, part], outer ^ d, 0, False).astype(jnp.bfloat16)
                total = total + swap(sent, "outer", d).astype(jnp.float32)
            total = total.astype(jnp.bfloat16)
            pieces[a][part] = (over_y(total) if a else total).reshape(own_rows, outer_count, 1, part_rows)
    halves = [jnp.concatenate(parts, axis=2).reshape(own_rows, -1) for parts in pieces]
    layer_out = jnp.zeros((half, halves[0].shape[1]), jnp.bfloat16)
    layer_out = lax.dynamic_update_slice(layer_out, halves[0], (upper * own_rows, 0))
    layer_out = lax.dynamic_update_slice(layer_out, halves[1], ((1 - upper) * own_rows, 0))
    return (context, layer_out)


def solution(mesh):
    placed = (
        P(("outer", "inner", "head"), None),
        P(("outer", "inner", "head"), None),
        P(("outer", "inner", "head"), None),
        P(),
        P("outer", "inner"),
        P("inner"),
        P("head", ("inner", "outer")),
        P(None, ("inner", "outer"), "head"),
        P("head", ("inner", "outer")),
    )
    return jax.shard_map(
        per_device,
        mesh=mesh,
        in_specs=placed,
        out_specs=(P(("outer", "inner"), "head"), P(("outer", "head"), "inner")),
        check_vma=False,
    )
```

```python
import functools

import jax
import jax.numpy as jnp
from jax import lax
from jax.experimental import pallas as pl
from jax.experimental.pallas import tpu as pltpu
from jax.sharding import PartitionSpec as P

D = 4096
QUERY_HEADS = 32
KEY_VALUE_HEADS = 8
HEAD_WIDTH = 128
GROUP = QUERY_HEADS // KEY_VALUE_HEADS
Q_COLS = GROUP * HEAD_WIDTH
KV_COLS = 2 * HEAD_WIDTH
WINDOW_PER_DOC = 4
QUERY_TILE = 128
ROW_TILE = 256
PARTS = 2
VMEM_LIMIT = 48 * 1024 * 1024
BRIEF = pl.CostEstimate(flops=1, bytes_accessed=1, transcendentals=0)
ANY = pl.BlockSpec(memory_space=pl.ANY)
VMEM = pl.BlockSpec(memory_space=pltpu.VMEM)
SMEM = pl.BlockSpec(memory_space=pltpu.SMEM)


def swap(array, axis, distance):
    if distance == 0:
        return array
    count = lax.axis_size(axis)
    return lax.ppermute(array, axis, [(s, s ^ distance) for s in range(count)])


def after(array, earlier):
    return lax.optimization_barrier((array, earlier))[0]


def blocks_over_inner(block):
    across = swap(block, "inner", 2)
    return [block, swap(block, "inner", 1), across, swap(across, "inner", 1)]


def earlier_planes(kv, hops):
    count = lax.axis_size("outer")
    moved = [lax.ppermute(kv, "outer", [(s, s + d) for s in range(count - d)]) for d in range(hops, 0, -1)]
    return jnp.concatenate(moved, axis=0)


def document_starts(bounds, first, rows):
    place = first + jnp.arange(rows, dtype=jnp.int32)
    starts = jnp.max(jnp.where(bounds[None, :] <= place[:, None], bounds[None, :], 0), axis=1) - first
    return starts[:, None].astype(jnp.int32)


def row_tiles(rows):
    step = ROW_TILE if rows % ROW_TILE == 0 else rows
    return [slice(at, at + step) for at in range(0, rows, step)]


def attention_kernel(halo_rows, reach, starts_ref, queries_ref, own_ref, halo_ref, out_ref, keys, values):
    tile = pl.program_id(0)
    rows = queries_ref.shape[0]
    span = reach + rows

    @pl.when(tile == 0)
    def _():
        keys[:halo_rows, :] = halo_ref[:, :HEAD_WIDTH]
        values[:halo_rows, :] = halo_ref[:, HEAD_WIDTH:]
        keys[halo_rows:, :] = own_ref[:, :HEAD_WIDTH]
        values[halo_rows:, :] = own_ref[:, HEAD_WIDTH:]

    first = pl.multiple_of(tile * rows + (halo_rows - reach), rows)
    near_keys = keys[pl.ds(first, span), :]
    near_values = values[pl.ds(first, span), :]
    key_place = lax.broadcasted_iota(jnp.int32, (rows, span), 1)
    query_place = lax.broadcasted_iota(jnp.int32, (rows, span), 0) + reach
    start = starts_ref[...] - (first - halo_rows)
    allowed = (key_place <= query_place) & (key_place >= start)
    for g in range(GROUP):
        cols = slice(g * HEAD_WIDTH, (g + 1) * HEAD_WIDTH)
        scores = lax.dot_general(
            queries_ref[:, cols], near_keys, (((1,), (1,)), ((), ())), preferred_element_type=jnp.float32
        ) * (HEAD_WIDTH ** (-0.5))
        masked = jnp.where(allowed, scores, -1e30)
        row_max = jnp.max(masked, axis=1, keepdims=True)
        weights = jnp.exp(masked - row_max)
        totals = jnp.sum(weights, axis=1, keepdims=True)
        summed = jnp.dot(weights.astype(jnp.bfloat16), near_values, preferred_element_type=jnp.float32)
        out_ref[:, cols] = (summed / totals).astype(jnp.bfloat16)


def attention(packed, halo, halo_at, starts, reach):
    rows = packed.shape[0]
    halo_rows = halo.shape[0]
    return pl.pallas_call(
        functools.partial(attention_kernel, halo_rows, reach),
        grid=(rows // QUERY_TILE,),
        in_specs=[
            pl.BlockSpec((QUERY_TILE, 1), lambda t: (t, 0)),
            pl.BlockSpec((QUERY_TILE, Q_COLS), lambda t: (t, 0)),
            pl.BlockSpec((rows, KV_COLS), lambda t: (0, Q_COLS // KV_COLS)),
            pl.BlockSpec((halo_rows, KV_COLS), lambda t: (0, halo_at)),
        ],
        out_specs=pl.BlockSpec((QUERY_TILE, Q_COLS), lambda t: (t, 0)),
        out_shape=jax.ShapeDtypeStruct((rows, Q_COLS), jnp.bfloat16),
        scratch_shapes=[
            pltpu.VMEM((halo_rows + rows, HEAD_WIDTH), jnp.bfloat16),
            pltpu.VMEM((halo_rows + rows, HEAD_WIDTH), jnp.bfloat16),
        ],
        compiler_params=pltpu.CompilerParams(vmem_limit_bytes=VMEM_LIMIT),
        cost_estimate=BRIEF,
        name="attention",
    )(starts, packed, packed, halo)


def cut_kernel(gain_ref, gate_up_ref, down_ref, both_ref, gate_ref, up_ref, *down_refs):
    rows, cols = gate_ref.shape[1], down_refs[0].shape[2]
    for which, second_ref in enumerate((gate_ref, up_ref)):
        scaled = (gate_up_ref[which].astype(jnp.float32) * gain_ref[...]).astype(jnp.bfloat16)
        both_ref[0, which] = scaled[:rows]
        second_ref[0] = scaled[rows:]
    for part, out_ref in enumerate(down_refs):
        out_ref[0] = down_ref[:, part * cols : (part + 1) * cols]


def cut_weights(w_gate_up, w_down, gain, outer_count):
    _, features, width = w_gate_up.shape
    cols = width // outer_count
    rows = features // PARTS
    if cols % HEAD_WIDTH:
        wide = (w_gate_up.astype(jnp.float32) * gain[None]).astype(jnp.bfloat16)
        wide = jnp.transpose(wide.reshape(2, PARTS, rows, outer_count, cols), (1, 3, 0, 2, 4))
        tall = jnp.transpose(w_down.reshape(outer_count, cols, PARTS, rows), (2, 0, 1, 3))
        return [wide[0], wide[1, :, 0], wide[1, :, 1], *tall]
    return pl.pallas_call(
        cut_kernel,
        grid=(outer_count,),
        in_specs=[
            pl.BlockSpec((features, 1), lambda p: (0, 0)),
            pl.BlockSpec((2, features, cols), lambda p: (0, 0, p)),
            pl.BlockSpec((cols, features), lambda p: (p, 0)),
        ],
        out_specs=[pl.BlockSpec((1, 2, rows, cols), lambda p: (p, 0, 0, 0))]
        + [pl.BlockSpec((1, rows, cols), lambda p: (p, 0, 0))] * 2
        + [pl.BlockSpec((1, cols, rows), lambda p: (p, 0, 0))] * PARTS,
        out_shape=[jax.ShapeDtypeStruct((outer_count, 2, rows, cols), jnp.bfloat16)]
        + [jax.ShapeDtypeStruct((outer_count, rows, cols), jnp.bfloat16)] * 2
        + [jax.ShapeDtypeStruct((outer_count, cols, rows), jnp.bfloat16)] * PARTS,
        compiler_params=pltpu.CompilerParams(vmem_limit_bytes=VMEM_LIMIT),
        cost_estimate=BRIEF,
        name="cut_weights",
    )(gain, w_gate_up, w_down)


def projection_kernel(block_count, place_ref, *refs):
    blocks, weights_ref = refs[:block_count], refs[block_count]
    kept_ref, sent_ref = refs[block_count + 1 : block_count + 3]
    inner, head = place_ref[0], place_ref[1]
    half, depth = kept_ref.shape[0], blocks[0].shape[1]
    for e in range(sent_ref.shape[0] + 1):
        rows = pl.ds(pl.multiple_of((head ^ e) * half, half), half)
        total = jnp.zeros(kept_ref.shape, jnp.float32)
        for a, block in enumerate(blocks):
            at = pl.ds(pl.multiple_of((inner ^ a) * depth, depth), depth) if block_count > 1 else slice(None)
            total = total + jnp.dot(block[rows, :], weights_ref[at, :], preferred_element_type=jnp.float32)
        if e == 0:
            kept_ref[...] = total.astype(jnp.bfloat16)
        else:
            sent_ref[e - 1] = total.astype(jnp.bfloat16)
    if block_count > 1:
        context_ref = refs[block_count + 3]
        tokens = context_ref.shape[0]
        own = pl.ds(pl.multiple_of(inner * tokens, tokens), tokens)
        for a, block in enumerate(blocks):
            context_ref[:, pl.ds(pl.multiple_of((inner ^ a) * depth, depth), depth)] = block[own, :]


def projection(blocks, weights, place, head_count, inner_count):
    rows, depth = blocks[0].shape
    half, width = rows // head_count, weights.shape[1]
    outs = [(half, width), (head_count - 1, half, width)]
    if len(blocks) > 1:
        outs.append((rows // inner_count, len(blocks) * depth))
    return pl.pallas_call(
        functools.partial(projection_kernel, len(blocks)),
        in_specs=[SMEM] + [VMEM] * (len(blocks) + 1),
        out_specs=[VMEM] * len(outs),
        out_shape=[jax.ShapeDtypeStruct(shape, jnp.bfloat16) for shape in outs],
        compiler_params=pltpu.CompilerParams(vmem_limit_bytes=VMEM_LIMIT),
        cost_estimate=BRIEF,
        name="projection",
    )(place, *blocks, weights)


def gate_up_kernel(tokens, both, gate, up, *refs):
    *earlier, out_ref, held, near, token_sem, weight_sems = refs
    depth = held.shape[1]
    copies = [
        [pltpu.make_async_copy(both.at[:, which], near.at[which, :, 0], weight_sems.at[which, 0]),
         pltpu.make_async_copy(second, near.at[which, :, 1], weight_sems.at[which, 1])]
        for which, second in enumerate((gate, up))
    ]
    copies[0].append(pltpu.make_async_copy(tokens, held, token_sem))
    for group in copies:
        for copy in group:
            copy.start()
    for which, group in enumerate(copies):
        for copy in group:
            copy.wait()
        block = near[which].reshape(depth, -1)
        for tile in row_tiles(held.shape[0]):
            product = jnp.dot(held[tile, :], block, preferred_element_type=jnp.float32)
            if earlier:
                product = earlier[0][which, tile, :].astype(jnp.float32) + product
            out_ref[which, tile, :] = product.astype(jnp.bfloat16)


def gate_up(tokens, streams, earlier=()):
    rows, depth = tokens.shape
    sources, stream_rows, cols = streams[1].shape
    return pl.pallas_call(
        gate_up_kernel,
        in_specs=[ANY] * (1 + len(streams)) + [VMEM] * len(earlier),
        out_specs=VMEM,
        out_shape=jax.ShapeDtypeStruct((2, rows, cols), jnp.bfloat16),
        scratch_shapes=[
            pltpu.VMEM((rows, depth), jnp.bfloat16),
            pltpu.VMEM((2, sources, PARTS, stream_rows, cols), jnp.bfloat16),
            pltpu.SemaphoreType.DMA,
            pltpu.SemaphoreType.DMA((2, PARTS)),
        ],
        compiler_params=pltpu.CompilerParams(vmem_limit_bytes=VMEM_LIMIT),
        cost_estimate=BRIEF,
        name="gate_up",
    )(tokens, *streams, *earlier)


def activation_kernel(here_ref, there_ref, out_ref):
    gate = here_ref[0].astype(jnp.float32) + there_ref[0].astype(jnp.float32)
    up = here_ref[1].astype(jnp.float32) + there_ref[1].astype(jnp.float32)
    out_ref[...] = (gate / (1.0 + jnp.exp(-gate)) * up).astype(jnp.bfloat16)


def activation(here, there):
    _, rows, cols = here.shape
    step = min(rows, ROW_TILE)
    return pl.pallas_call(
        activation_kernel,
        grid=(rows // step,),
        in_specs=[pl.BlockSpec((2, step, cols), lambda t: (0, t, 0))] * 2,
        out_specs=pl.BlockSpec((step, cols), lambda t: (t, 0)),
        out_shape=jax.ShapeDtypeStruct((rows, cols), jnp.bfloat16),
        compiler_params=pltpu.CompilerParams(vmem_limit_bytes=VMEM_LIMIT),
        cost_estimate=BRIEF,
        name="activation",
    )(here, there)


def down_kernel(activated_ref, weights_ref, out_ref):
    sources, _, cols = weights_ref.shape
    if cols % HEAD_WIDTH:
        blocks = [weights_ref[s] for s in range(sources)]
    else:
        blocks = [jnp.concatenate([weights_ref[s] for s in range(sources)], axis=1)]
    for s, block in enumerate(blocks):
        product = jnp.dot(activated_ref[...], block, preferred_element_type=jnp.float32)
        out_ref[:, s * block.shape[1] : (s + 1) * block.shape[1]] = product.astype(jnp.bfloat16)


def down_product(activated, weights):
    sources, _, cols = weights.shape
    return pl.pallas_call(
        down_kernel,
        in_specs=[VMEM, VMEM],
        out_specs=VMEM,
        out_shape=jax.ShapeDtypeStruct((activated.shape[0], sources * cols), jnp.bfloat16),
        compiler_params=pltpu.CompilerParams(vmem_limit_bytes=VMEM_LIMIT),
        cost_estimate=BRIEF,
        name="down",
    )(activated, weights)


def per_device(query, key, value, doc_lengths, resid, norm_gain, w_out, w_gate_up, w_down):
    inner_count = lax.axis_size("inner")
    outer_count = lax.axis_size("outer")
    head_count = lax.axis_size("head")
    outer, inner, head = lax.axis_index("outer"), lax.axis_index("inner"), lax.axis_index("head")
    rows = query.shape[0]
    plane_rows = rows * inner_count * head_count
    reach = plane_rows * outer_count // WINDOW_PER_DOC
    feature_rows = w_gate_up.shape[1]
    hidden_cols = w_gate_up.shape[2] // outer_count
    bounds = jnp.cumsum(doc_lengths)
    hops = reach // plane_rows
    token_rows = plane_rows // inner_count
    half = plane_rows // head_count
    packing = (rows, head_count, KEY_VALUE_HEADS // head_count, -1)

    weights_out = lax.all_gather(w_out, "outer", axis=1, tiled=True)
    if packing[2] == inner_count and hops == 1:
        earlier = [lax.ppermute(part, "outer", [(s, s + 1) for s in range(outer_count - 1)]) for part in (key, value)]
        groups = jnp.concatenate([part.reshape(packing) for part in (query, key, value, *earlier)], axis=3)
        groups = jnp.transpose(groups, (2, 1, 0, 3)).reshape(inner_count * head_count, rows, -1)
        packed = lax.all_to_all(groups, ("inner", "head"), split_axis=0, concat_axis=0, tiled=True)
        packed = packed.reshape(plane_rows, -1)
        starts = document_starts(bounds, outer * plane_rows, plane_rows)
        own_context = attention(packed, packed, Q_COLS // KV_COLS + 1, starts, reach)
        blocks = blocks_over_inner(own_context)
    else:
        groups = jnp.concatenate([part.reshape(packing) for part in (query, key, value)], axis=3)
        groups = jnp.transpose(groups[:, :, 0], (1, 0, 2))
        packed = lax.all_to_all(groups, "head", split_axis=0, concat_axis=0, tiled=True).reshape(token_rows, -1)
        plane_kv = lax.all_gather(packed[:, Q_COLS:], "inner", axis=0, tiled=True)
        every_kv = jnp.concatenate([earlier_planes(plane_kv, hops), plane_kv], axis=0)
        halo = lax.dynamic_slice_in_dim(every_kv, inner * token_rows, reach, 0)
        starts = document_starts(bounds, outer * plane_rows + inner * token_rows, token_rows)
        own_context = attention(packed, halo, 0, starts, reach)
        blocks = [lax.all_gather(own_context, "inner", axis=0, tiled=True)]

    spread = functools.partial(lax.all_to_all, axis_name="outer", split_axis=0, concat_axis=0, tiled=True)
    over_y = functools.partial(swap, axis="inner", distance=2)
    fence = lambda *arrays: lax.optimization_barrier(arrays)
    own_gain = lax.dynamic_slice_in_dim(norm_gain, outer * feature_rows, feature_rows, 0)
    cut = cut_weights(w_gate_up, w_down, own_gain[:, None], outer_count)

    place = jnp.stack([inner, head]).astype(jnp.int32)
    weights_out, *blocks = fence(weights_out, *blocks)
    first = spread(after(cut[0], weights_out))
    kept, sent, *whole = projection(blocks, weights_out, place, head_count, inner_count)
    context = whole[0] if whole else own_context
    projected = kept.astype(jnp.float32)
    for e in range(1, head_count):
        projected = projected + swap(sent[e - 1], "head", e).astype(jnp.float32)
    own_resid = lax.dynamic_slice_in_dim(resid, head * half, half, 0)
    hidden_part = (own_resid.astype(jnp.float32) + projected).astype(jnp.bfloat16)

    upper = inner // 2
    own_rows = half // 2
    mine = lax.dynamic_slice_in_dim(hidden_part, upper * own_rows, own_rows, 0)
    others = lax.dynamic_slice_in_dim(hidden_part, (1 - upper) * own_rows, own_rows, 0)
    others, first = fence(over_y(others), first)
    state = [mine.astype(jnp.float32), others.astype(jnp.float32)]
    squares = sum([jnp.sum(block * block, axis=1) for block in state])
    squares = squares + swap(squares, "inner", 1)
    inverse = lax.rsqrt(squares / D + 1e-05)[:, None]
    part_rows = feature_rows // PARTS
    normed = jnp.concatenate([block * inverse for block in state], axis=1).astype(jnp.bfloat16)
    state = [block.reshape(own_rows, outer_count, PARTS, part_rows) for block in state]
    state = [[block[:, :, part].reshape(own_rows, -1) for part in range(PARTS)] for block in state]

    tokens = lax.all_gather(normed, "outer", axis=0, tiled=True)
    second, first_y, tokens, state = fence(spread(after(cut[1], normed)), over_y(first), tokens, state)
    tokens = jnp.split(tokens, 2, axis=1)
    tokens = [[swap(block, "head", e) if e else block for e in range(head_count)] for block in tokens]
    third, second_y, tokens[0] = fence(spread(after(cut[2], second)), over_y(second), tokens[0])
    own_sums = [gate_up(rows_of, [first, second, third]) for rows_of in tokens[0]]
    fourth, third_y, own_sums = fence(spread(after(cut[3], third)), over_y(third), own_sums)
    streams = [first_y, second_y, third_y]
    activated, earlier = {}, first_y
    for e in [*range(1, head_count), 0]:
        sums = gate_up(tokens[1][e], streams, [after(own_sums[e], earlier)])
        activated[e] = activation(sums, swap(sums, "inner", 1))
        earlier = sums

    def over_heads(weights):
        sent = [down_product(activated[e], weights) for e in range(1, head_count)]
        moved = [swap(rows_of, "head", e) for e, rows_of in enumerate(sent, 1)]
        total = down_product(after(activated[0], sent[-1]), weights).astype(jnp.float32)
        for rows_of in moved:
            total = total + rows_of.astype(jnp.float32)
        return total.reshape(outer_count, own_rows, -1)

    paired = {(0, 0): over_heads(fourth)}
    fifth, fourth_y, paired[0, 0] = fence(spread(after(cut[4], fourth)), over_y(fourth), paired[0, 0])
    fifth_y = over_y(fifth)
    paired[1, 0] = over_heads(fourth_y)
    paired[0, 1] = over_heads(fifth)
    paired[1, 1] = over_heads(after(fifth_y, paired[1, 0]))

    pieces = [[None] * PARTS, [None] * PARTS]
    for part in range(PARTS):
        for a in range(2):
            total = state[a][part] + lax.dynamic_index_in_dim(paired[a, part], outer, 0, False)
            for d in range(1, outer_count):
                sent = lax.dynamic_index_in_dim(paired[a, part], outer ^ d, 0, False).astype(jnp.bfloat16)
                total = total + swap(sent, "outer", d).astype(jnp.float32)
            total = total.astype(jnp.bfloat16)
            pieces[a][part] = (over_y(total) if a else total).reshape(own_rows, outer_count, 1, part_rows)
    halves = [jnp.concatenate(parts, axis=2).reshape(own_rows, -1) for parts in pieces]
    layer_out = jnp.zeros((half, halves[0].shape[1]), jnp.bfloat16)
    layer_out = lax.dynamic_update_slice(layer_out, halves[0], (upper * own_rows, 0))
    layer_out = lax.dynamic_update_slice(layer_out, halves[1], ((1 - upper) * own_rows, 0))
    return (context, layer_out)


def solution(mesh):
    placed = (
        P(("outer", "inner", "head"), None),
        P(("outer", "inner", "head"), None),
        P(("outer", "inner", "head"), None),
        P(),
        P("outer", "inner"),
        P("inner"),
        P("head", ("inner", "outer")),
        P(None, ("inner", "outer"), "head"),
        P("head", ("inner", "outer")),
    )
    return jax.shard_map(
        per_device,
        mesh=mesh,
        in_specs=placed,
        out_specs=(P(("outer", "inner"), "head"), P(("outer", "head"), "inner")),
        check_vma=False,
    )
```

```python
import functools

import jax
import jax.numpy as jnp
from jax import lax
from jax.experimental import pallas as pl
from jax.experimental.pallas import tpu as pltpu
from jax.sharding import PartitionSpec as P

D = 4096
QUERY_HEADS = 32
KEY_VALUE_HEADS = 8
HEAD_WIDTH = 128
GROUP = QUERY_HEADS // KEY_VALUE_HEADS
Q_COLS = GROUP * HEAD_WIDTH
KV_COLS = 2 * HEAD_WIDTH
WINDOW_PER_DOC = 4
QUERY_TILE = 128
ROW_TILE = 256
PARTS = 2
VMEM_LIMIT = 48 * 1024 * 1024
BRIEF = pl.CostEstimate(flops=1, bytes_accessed=1, transcendentals=0)
ANY = pl.BlockSpec(memory_space=pl.ANY)
VMEM = pl.BlockSpec(memory_space=pltpu.VMEM)
SMEM = pl.BlockSpec(memory_space=pltpu.SMEM)


def swap(array, axis, distance):
    if distance == 0:
        return array
    count = lax.axis_size(axis)
    return lax.ppermute(array, axis, [(s, s ^ distance) for s in range(count)])


def after(array, earlier):
    return lax.optimization_barrier((array, earlier))[0]


def blocks_over_inner(block):
    across = swap(block, "inner", 2)
    return [block, swap(block, "inner", 1), across, swap(across, "inner", 1)]


def earlier_planes(kv, hops):
    count = lax.axis_size("outer")
    moved = [lax.ppermute(kv, "outer", [(s, s + d) for s in range(count - d)]) for d in range(hops, 0, -1)]
    return jnp.concatenate(moved, axis=0)


def document_starts(bounds, first, rows):
    place = first + jnp.arange(rows, dtype=jnp.int32)
    starts = jnp.max(jnp.where(bounds[None, :] <= place[:, None], bounds[None, :], 0), axis=1) - first
    return starts[:, None].astype(jnp.int32)


def row_tiles(rows):
    step = ROW_TILE if rows % ROW_TILE == 0 else rows
    return [slice(at, at + step) for at in range(0, rows, step)]


def attention_kernel(halo_rows, reach, starts_ref, queries_ref, own_ref, halo_ref, out_ref, keys, values):
    tile = pl.program_id(0)
    rows = queries_ref.shape[0]
    span = reach + rows

    @pl.when(tile == 0)
    def _():
        keys[:halo_rows, :] = halo_ref[:, :HEAD_WIDTH]
        values[:halo_rows, :] = halo_ref[:, HEAD_WIDTH:]
        keys[halo_rows:, :] = own_ref[:, :HEAD_WIDTH]
        values[halo_rows:, :] = own_ref[:, HEAD_WIDTH:]

    first = pl.multiple_of(tile * rows + (halo_rows - reach), rows)
    near_keys = keys[pl.ds(first, span), :]
    near_values = values[pl.ds(first, span), :]
    key_place = lax.broadcasted_iota(jnp.int32, (rows, span), 1)
    query_place = lax.broadcasted_iota(jnp.int32, (rows, span), 0) + reach
    start = starts_ref[...] - (first - halo_rows)
    allowed = (key_place <= query_place) & (key_place >= start)
    for g in range(GROUP):
        cols = slice(g * HEAD_WIDTH, (g + 1) * HEAD_WIDTH)
        scores = lax.dot_general(
            queries_ref[:, cols], near_keys, (((1,), (1,)), ((), ())), preferred_element_type=jnp.float32
        ) * (HEAD_WIDTH ** (-0.5))
        masked = jnp.where(allowed, scores, -1e30)
        row_max = jnp.max(masked, axis=1, keepdims=True)
        weights = jnp.exp(masked - row_max)
        totals = jnp.sum(weights, axis=1, keepdims=True)
        summed = jnp.dot(weights.astype(jnp.bfloat16), near_values, preferred_element_type=jnp.float32)
        out_ref[:, cols] = (summed / totals).astype(jnp.bfloat16)


def attention(packed, halo, halo_at, starts, reach):
    rows = packed.shape[0]
    halo_rows = halo.shape[0]
    return pl.pallas_call(
        functools.partial(attention_kernel, halo_rows, reach),
        grid=(rows // QUERY_TILE,),
        in_specs=[
            pl.BlockSpec((QUERY_TILE, 1), lambda t: (t, 0)),
            pl.BlockSpec((QUERY_TILE, Q_COLS), lambda t: (t, 0)),
            pl.BlockSpec((rows, KV_COLS), lambda t: (0, Q_COLS // KV_COLS)),
            pl.BlockSpec((halo_rows, KV_COLS), lambda t: (0, halo_at)),
        ],
        out_specs=pl.BlockSpec((QUERY_TILE, Q_COLS), lambda t: (t, 0)),
        out_shape=jax.ShapeDtypeStruct((rows, Q_COLS), jnp.bfloat16),
        scratch_shapes=[
            pltpu.VMEM((halo_rows + rows, HEAD_WIDTH), jnp.bfloat16),
            pltpu.VMEM((halo_rows + rows, HEAD_WIDTH), jnp.bfloat16),
        ],
        compiler_params=pltpu.CompilerParams(vmem_limit_bytes=VMEM_LIMIT),
        cost_estimate=BRIEF,
        name="attention",
    )(starts, packed, packed, halo)


def cut_kernel(gain_ref, gate_up_ref, down_ref, both_ref, gate_ref, up_ref, *down_refs):
    rows, cols = gate_ref.shape[1], down_refs[0].shape[2]
    for which, second_ref in enumerate((gate_ref, up_ref)):
        scaled = (gate_up_ref[which].astype(jnp.float32) * gain_ref[...]).astype(jnp.bfloat16)
        both_ref[0, which] = scaled[:rows]
        second_ref[0] = scaled[rows:]
    for part, out_ref in enumerate(down_refs):
        out_ref[0] = down_ref[:, part * cols : (part + 1) * cols]


def cut_weights(w_gate_up, w_down, gain, outer_count):
    _, features, width = w_gate_up.shape
    cols = width // outer_count
    rows = features // PARTS
    if cols % HEAD_WIDTH:
        wide = (w_gate_up.astype(jnp.float32) * gain[None]).astype(jnp.bfloat16)
        wide = jnp.transpose(wide.reshape(2, PARTS, rows, outer_count, cols), (1, 3, 0, 2, 4))
        tall = jnp.transpose(w_down.reshape(outer_count, cols, PARTS, rows), (2, 0, 1, 3))
        return [wide[0], wide[1, :, 0], wide[1, :, 1], *tall]
    return pl.pallas_call(
        cut_kernel,
        grid=(outer_count,),
        in_specs=[
            pl.BlockSpec((features, 1), lambda p: (0, 0)),
            pl.BlockSpec((2, features, cols), lambda p: (0, 0, p)),
            pl.BlockSpec((cols, features), lambda p: (p, 0)),
        ],
        out_specs=[pl.BlockSpec((1, 2, rows, cols), lambda p: (p, 0, 0, 0))]
        + [pl.BlockSpec((1, rows, cols), lambda p: (p, 0, 0))] * 2
        + [pl.BlockSpec((1, cols, rows), lambda p: (p, 0, 0))] * PARTS,
        out_shape=[jax.ShapeDtypeStruct((outer_count, 2, rows, cols), jnp.bfloat16)]
        + [jax.ShapeDtypeStruct((outer_count, rows, cols), jnp.bfloat16)] * 2
        + [jax.ShapeDtypeStruct((outer_count, cols, rows), jnp.bfloat16)] * PARTS,
        compiler_params=pltpu.CompilerParams(vmem_limit_bytes=VMEM_LIMIT),
        cost_estimate=BRIEF,
        name="cut_weights",
    )(gain, w_gate_up, w_down)


def projection_kernel(block_count, place_ref, *refs):
    blocks, weights_ref = refs[:block_count], refs[block_count]
    kept_ref, sent_ref = refs[block_count + 1 : block_count + 3]
    inner, head = place_ref[0], place_ref[1]
    half, depth = kept_ref.shape[0], blocks[0].shape[1]
    for e in range(sent_ref.shape[0] + 1):
        rows = pl.ds(pl.multiple_of((head ^ e) * half, half), half)
        total = jnp.zeros(kept_ref.shape, jnp.float32)
        for a, block in enumerate(blocks):
            at = pl.ds(pl.multiple_of((inner ^ a) * depth, depth), depth) if block_count > 1 else slice(None)
            total = total + jnp.dot(block[rows, :], weights_ref[at, :], preferred_element_type=jnp.float32)
        if e == 0:
            kept_ref[...] = total.astype(jnp.bfloat16)
        else:
            sent_ref[e - 1] = total.astype(jnp.bfloat16)
    if block_count > 1:
        context_ref = refs[block_count + 3]
        tokens = context_ref.shape[0]
        own = pl.ds(pl.multiple_of(inner * tokens, tokens), tokens)
        for a, block in enumerate(blocks):
            context_ref[:, pl.ds(pl.multiple_of((inner ^ a) * depth, depth), depth)] = block[own, :]


def projection(blocks, weights, place, head_count, inner_count):
    rows, depth = blocks[0].shape
    half, width = rows // head_count, weights.shape[1]
    outs = [(half, width), (head_count - 1, half, width)]
    if len(blocks) > 1:
        outs.append((rows // inner_count, len(blocks) * depth))
    return pl.pallas_call(
        functools.partial(projection_kernel, len(blocks)),
        in_specs=[SMEM] + [VMEM] * (len(blocks) + 1),
        out_specs=[VMEM] * len(outs),
        out_shape=[jax.ShapeDtypeStruct(shape, jnp.bfloat16) for shape in outs],
        compiler_params=pltpu.CompilerParams(vmem_limit_bytes=VMEM_LIMIT),
        cost_estimate=BRIEF,
        name="projection",
    )(place, *blocks, weights)


def gate_up_kernel(tokens, both, gate, up, *refs):
    *earlier, out_ref, held, near, token_sem, weight_sems = refs
    depth = held.shape[1]
    copies = [
        [pltpu.make_async_copy(both.at[:, which], near.at[which, :, 0], weight_sems.at[which, 0]),
         pltpu.make_async_copy(second, near.at[which, :, 1], weight_sems.at[which, 1])]
        for which, second in enumerate((gate, up))
    ]
    copies[0].append(pltpu.make_async_copy(tokens, held, token_sem))
    for group in copies:
        for copy in group:
            copy.start()
    for which, group in enumerate(copies):
        for copy in group:
            copy.wait()
        block = near[which].reshape(depth, -1)
        for tile in row_tiles(held.shape[0]):
            product = jnp.dot(held[tile, :], block, preferred_element_type=jnp.float32)
            if earlier:
                product = earlier[0][which, tile, :].astype(jnp.float32) + product
            out_ref[which, tile, :] = product.astype(jnp.bfloat16)


def gate_up(tokens, streams, earlier=()):
    rows, depth = tokens.shape
    sources, stream_rows, cols = streams[1].shape
    return pl.pallas_call(
        gate_up_kernel,
        in_specs=[ANY] * (1 + len(streams)) + [VMEM] * len(earlier),
        out_specs=VMEM,
        out_shape=jax.ShapeDtypeStruct((2, rows, cols), jnp.bfloat16),
        scratch_shapes=[
            pltpu.VMEM((rows, depth), jnp.bfloat16),
            pltpu.VMEM((2, sources, PARTS, stream_rows, cols), jnp.bfloat16),
            pltpu.SemaphoreType.DMA,
            pltpu.SemaphoreType.DMA((2, PARTS)),
        ],
        compiler_params=pltpu.CompilerParams(vmem_limit_bytes=VMEM_LIMIT),
        cost_estimate=BRIEF,
        name="gate_up",
    )(tokens, *streams, *earlier)


def activation_kernel(here_ref, there_ref, out_ref):
    gate = here_ref[0].astype(jnp.float32) + there_ref[0].astype(jnp.float32)
    up = here_ref[1].astype(jnp.float32) + there_ref[1].astype(jnp.float32)
    out_ref[...] = (gate / (1.0 + jnp.exp(-gate)) * up).astype(jnp.bfloat16)


def activation(here, there):
    _, rows, cols = here.shape
    step = min(rows, ROW_TILE)
    return pl.pallas_call(
        activation_kernel,
        grid=(rows // step,),
        in_specs=[pl.BlockSpec((2, step, cols), lambda t: (0, t, 0))] * 2,
        out_specs=pl.BlockSpec((step, cols), lambda t: (t, 0)),
        out_shape=jax.ShapeDtypeStruct((rows, cols), jnp.bfloat16),
        compiler_params=pltpu.CompilerParams(vmem_limit_bytes=VMEM_LIMIT),
        cost_estimate=BRIEF,
        name="activation",
    )(here, there)


def down_kernel(activated_ref, weights_ref, out_ref):
    sources, _, cols = weights_ref.shape
    if cols % HEAD_WIDTH:
        blocks = [weights_ref[s] for s in range(sources)]
    else:
        blocks = [jnp.concatenate([weights_ref[s] for s in range(sources)], axis=1)]
    for s, block in enumerate(blocks):
        product = jnp.dot(activated_ref[...], block, preferred_element_type=jnp.float32)
        out_ref[:, s * block.shape[1] : (s + 1) * block.shape[1]] = product.astype(jnp.bfloat16)


def down_product(activated, weights):
    sources, _, cols = weights.shape
    return pl.pallas_call(
        down_kernel,
        in_specs=[VMEM, VMEM],
        out_specs=VMEM,
        out_shape=jax.ShapeDtypeStruct((activated.shape[0], sources * cols), jnp.bfloat16),
        compiler_params=pltpu.CompilerParams(vmem_limit_bytes=VMEM_LIMIT),
        cost_estimate=BRIEF,
        name="down",
    )(activated, weights)


def per_device(query, key, value, doc_lengths, resid, norm_gain, w_out, w_gate_up, w_down):
    inner_count = lax.axis_size("inner")
    outer_count = lax.axis_size("outer")
    head_count = lax.axis_size("head")
    outer, inner, head = lax.axis_index("outer"), lax.axis_index("inner"), lax.axis_index("head")
    rows = query.shape[0]
    plane_rows = rows * inner_count * head_count
    reach = plane_rows * outer_count // WINDOW_PER_DOC
    feature_rows = w_gate_up.shape[1]
    hidden_cols = w_gate_up.shape[2] // outer_count
    bounds = jnp.cumsum(doc_lengths)
    hops = reach // plane_rows
    token_rows = plane_rows // inner_count
    half = plane_rows // head_count
    packing = (rows, head_count, KEY_VALUE_HEADS // head_count, -1)

    weights_out = lax.all_gather(w_out, "outer", axis=1, tiled=True)
    if packing[2] == inner_count and hops == 1:
        earlier = [lax.ppermute(part, "outer", [(s, s + 1) for s in range(outer_count - 1)]) for part in (key, value)]
        groups = jnp.concatenate([part.reshape(packing) for part in (query, key, value, *earlier)], axis=3)
        groups = jnp.transpose(groups, (2, 1, 0, 3)).reshape(inner_count * head_count, rows, -1)
        packed = lax.all_to_all(groups, ("inner", "head"), split_axis=0, concat_axis=0, tiled=True)
        packed = packed.reshape(plane_rows, -1)
        starts = document_starts(bounds, outer * plane_rows, plane_rows)
        own_context = attention(packed, packed, Q_COLS // KV_COLS + 1, starts, reach)
        blocks = blocks_over_inner(own_context)
    else:
        groups = jnp.concatenate([part.reshape(packing) for part in (query, key, value)], axis=3)
        groups = jnp.transpose(groups[:, :, 0], (1, 0, 2))
        packed = lax.all_to_all(groups, "head", split_axis=0, concat_axis=0, tiled=True).reshape(token_rows, -1)
        plane_kv = lax.all_gather(packed[:, Q_COLS:], "inner", axis=0, tiled=True)
        every_kv = jnp.concatenate([earlier_planes(plane_kv, hops), plane_kv], axis=0)
        halo = lax.dynamic_slice_in_dim(every_kv, inner * token_rows, reach, 0)
        starts = document_starts(bounds, outer * plane_rows + inner * token_rows, token_rows)
        own_context = attention(packed, halo, 0, starts, reach)
        blocks = [lax.all_gather(own_context, "inner", axis=0, tiled=True)]

    spread = functools.partial(lax.all_to_all, axis_name="outer", split_axis=0, concat_axis=0, tiled=True)
    over_y = functools.partial(swap, axis="inner", distance=2)
    fence = lambda *arrays: lax.optimization_barrier(arrays)
    own_gain = lax.dynamic_slice_in_dim(norm_gain, outer * feature_rows, feature_rows, 0)
    cut = cut_weights(w_gate_up, w_down, own_gain[:, None], outer_count)

    place = jnp.stack([inner, head]).astype(jnp.int32)
    weights_out, *blocks = fence(weights_out, *blocks)
    first = spread(after(cut[0], weights_out))
    kept, sent, *whole = projection(blocks, weights_out, place, head_count, inner_count)
    context = whole[0] if whole else own_context
    projected = kept.astype(jnp.float32)
    for e in range(1, head_count):
        projected = projected + swap(sent[e - 1], "head", e).astype(jnp.float32)
    own_resid = lax.dynamic_slice_in_dim(resid, head * half, half, 0)
    hidden_part = (own_resid.astype(jnp.float32) + projected).astype(jnp.bfloat16)

    upper = inner // 2
    own_rows = half // 2
    mine = lax.dynamic_slice_in_dim(hidden_part, upper * own_rows, own_rows, 0)
    others = lax.dynamic_slice_in_dim(hidden_part, (1 - upper) * own_rows, own_rows, 0)
    others, first = fence(over_y(others), first)
    state = [mine.astype(jnp.float32), others.astype(jnp.float32)]
    squares = sum([jnp.sum(block * block, axis=1) for block in state])
    squares = squares + swap(squares, "inner", 1)
    inverse = lax.rsqrt(squares / D + 1e-05)[:, None]
    part_rows = feature_rows // PARTS
    normed = jnp.concatenate([block * inverse for block in state], axis=1).astype(jnp.bfloat16)
    state = [block.reshape(own_rows, outer_count, PARTS, part_rows) for block in state]
    state = [[block[:, :, part].reshape(own_rows, -1) for part in range(PARTS)] for block in state]

    tokens = lax.all_gather(normed, "outer", axis=0, tiled=True)
    second, first_y, state = fence(spread(after(cut[1], normed)), over_y(first), state)
    tokens = jnp.split(tokens, 2, axis=1)
    tokens = [[swap(block, "head", e) if e else block for e in range(head_count)] for block in tokens]
    third, second_y, tokens[0] = fence(spread(after(cut[2], second)), over_y(second), tokens[0])
    own_sums = [gate_up(rows_of, [first, second, third]) for rows_of in tokens[0]]
    fourth, third_y, own_sums = fence(spread(after(cut[3], third)), over_y(third), own_sums)
    streams = [first_y, second_y, third_y]
    activated, first_sent = {}, []
    for e in [*range(1, head_count), 0]:
        sums = gate_up(tokens[1][e], streams, [own_sums[e] if e else after(own_sums[e], first_sent)])
        activated[e] = activation(sums, swap(sums, "inner", 1))
        if e:
            first_sent.append(down_product(activated[e], fourth))

    def over_heads(weights, sent=None):
        if sent is None:
            sent = [down_product(activated[e], weights) for e in range(1, head_count)]
        moved = [swap(rows_of, "head", e) for e, rows_of in enumerate(sent, 1)]
        total = down_product(after(activated[0], sent[-1]), weights).astype(jnp.float32)
        for rows_of in moved:
            total = total + rows_of.astype(jnp.float32)
        return total.reshape(outer_count, own_rows, -1)

    paired = {(0, 0): over_heads(fourth, first_sent)}
    fifth, fourth_y, paired[0, 0] = fence(spread(after(cut[4], fourth)), over_y(fourth), paired[0, 0])
    fifth_y = over_y(fifth)
    paired[1, 0] = over_heads(fourth_y)
    paired[0, 1] = over_heads(fifth)
    paired[1, 1] = over_heads(after(fifth_y, paired[1, 0]))

    pieces = [[None] * PARTS, [None] * PARTS]
    for part in range(PARTS):
        for a in range(2):
            total = state[a][part] + lax.dynamic_index_in_dim(paired[a, part], outer, 0, False)
            for d in range(1, outer_count):
                sent = lax.dynamic_index_in_dim(paired[a, part], outer ^ d, 0, False).astype(jnp.bfloat16)
                total = total + swap(sent, "outer", d).astype(jnp.float32)
            total = total.astype(jnp.bfloat16)
            pieces[a][part] = (over_y(total) if a else total).reshape(own_rows, outer_count, 1, part_rows)
    halves = [jnp.concatenate(parts, axis=2).reshape(own_rows, -1) for parts in pieces]
    layer_out = jnp.zeros((half, halves[0].shape[1]), jnp.bfloat16)
    layer_out = lax.dynamic_update_slice(layer_out, halves[0], (upper * own_rows, 0))
    layer_out = lax.dynamic_update_slice(layer_out, halves[1], ((1 - upper) * own_rows, 0))
    return (context, layer_out)


def solution(mesh):
    placed = (
        P(("outer", "inner", "head"), None),
        P(("outer", "inner", "head"), None),
        P(("outer", "inner", "head"), None),
        P(),
        P("outer", "inner"),
        P("inner"),
        P("head", ("inner", "outer")),
        P(None, ("inner", "outer"), "head"),
        P("head", ("inner", "outer")),
    )
    return jax.shard_map(
        per_device,
        mesh=mesh,
        in_specs=placed,
        out_specs=(P(("outer", "inner"), "head"), P(("outer", "head"), "inner")),
        check_vma=False,
    )
```

```python
import functools

import jax
import jax.numpy as jnp
from jax import lax
from jax.experimental import pallas as pl
from jax.experimental.pallas import tpu as pltpu
from jax.sharding import PartitionSpec as P

D = 4096
QUERY_HEADS = 32
KEY_VALUE_HEADS = 8
HEAD_WIDTH = 128
GROUP = QUERY_HEADS // KEY_VALUE_HEADS
Q_COLS = GROUP * HEAD_WIDTH
KV_COLS = 2 * HEAD_WIDTH
WINDOW_PER_DOC = 4
QUERY_TILE = 128
ROW_TILE = 256
PARTS = 2
VMEM_LIMIT = 48 * 1024 * 1024
BRIEF = pl.CostEstimate(flops=1, bytes_accessed=1, transcendentals=0)
ANY = pl.BlockSpec(memory_space=pl.ANY)
VMEM = pl.BlockSpec(memory_space=pltpu.VMEM)
SMEM = pl.BlockSpec(memory_space=pltpu.SMEM)


def swap(array, axis, distance):
    if distance == 0:
        return array
    count = lax.axis_size(axis)
    return lax.ppermute(array, axis, [(s, s ^ distance) for s in range(count)])


def after(array, earlier):
    return lax.optimization_barrier((array, earlier))[0]


def blocks_over_inner(block):
    across = swap(block, "inner", 2)
    return [block, swap(block, "inner", 1), across, swap(across, "inner", 1)]


def earlier_planes(kv, hops):
    count = lax.axis_size("outer")
    moved = [lax.ppermute(kv, "outer", [(s, s + d) for s in range(count - d)]) for d in range(hops, 0, -1)]
    return jnp.concatenate(moved, axis=0)


def document_starts(bounds, first, rows):
    place = first + jnp.arange(rows, dtype=jnp.int32)
    starts = jnp.max(jnp.where(bounds[None, :] <= place[:, None], bounds[None, :], 0), axis=1) - first
    return starts[:, None].astype(jnp.int32)


def row_tiles(rows):
    step = ROW_TILE if rows % ROW_TILE == 0 else rows
    return [slice(at, at + step) for at in range(0, rows, step)]


def attention_kernel(halo_rows, reach, starts_ref, queries_ref, own_ref, halo_ref, out_ref, keys, values):
    tile = pl.program_id(0)
    rows = queries_ref.shape[0]
    span = reach + rows

    @pl.when(tile == 0)
    def _():
        keys[:halo_rows, :] = halo_ref[:, :HEAD_WIDTH]
        values[:halo_rows, :] = halo_ref[:, HEAD_WIDTH:]
        keys[halo_rows:, :] = own_ref[:, :HEAD_WIDTH]
        values[halo_rows:, :] = own_ref[:, HEAD_WIDTH:]

    first = pl.multiple_of(tile * rows + (halo_rows - reach), rows)
    near_keys = keys[pl.ds(first, span), :]
    near_values = values[pl.ds(first, span), :]
    key_place = lax.broadcasted_iota(jnp.int32, (rows, span), 1)
    query_place = lax.broadcasted_iota(jnp.int32, (rows, span), 0) + reach
    start = starts_ref[...] - (first - halo_rows)
    allowed = (key_place <= query_place) & (key_place >= start)
    for g in range(GROUP):
        cols = slice(g * HEAD_WIDTH, (g + 1) * HEAD_WIDTH)
        scores = lax.dot_general(
            queries_ref[:, cols], near_keys, (((1,), (1,)), ((), ())), preferred_element_type=jnp.float32
        ) * (HEAD_WIDTH ** (-0.5))
        masked = jnp.where(allowed, scores, -1e30)
        row_max = jnp.max(masked, axis=1, keepdims=True)
        weights = jnp.exp(masked - row_max)
        totals = jnp.sum(weights, axis=1, keepdims=True)
        summed = jnp.dot(weights.astype(jnp.bfloat16), near_values, preferred_element_type=jnp.float32)
        out_ref[:, cols] = (summed / totals).astype(jnp.bfloat16)


def attention(packed, halo, halo_at, starts, reach):
    rows = packed.shape[0]
    halo_rows = halo.shape[0]
    return pl.pallas_call(
        functools.partial(attention_kernel, halo_rows, reach),
        grid=(rows // QUERY_TILE,),
        in_specs=[
            pl.BlockSpec((QUERY_TILE, 1), lambda t: (t, 0)),
            pl.BlockSpec((QUERY_TILE, Q_COLS), lambda t: (t, 0)),
            pl.BlockSpec((rows, KV_COLS), lambda t: (0, Q_COLS // KV_COLS)),
            pl.BlockSpec((halo_rows, KV_COLS), lambda t: (0, halo_at)),
        ],
        out_specs=pl.BlockSpec((QUERY_TILE, Q_COLS), lambda t: (t, 0)),
        out_shape=jax.ShapeDtypeStruct((rows, Q_COLS), jnp.bfloat16),
        scratch_shapes=[
            pltpu.VMEM((halo_rows + rows, HEAD_WIDTH), jnp.bfloat16),
            pltpu.VMEM((halo_rows + rows, HEAD_WIDTH), jnp.bfloat16),
        ],
        compiler_params=pltpu.CompilerParams(vmem_limit_bytes=VMEM_LIMIT),
        cost_estimate=BRIEF,
        name="attention",
    )(starts, packed, packed, halo)


def cut_kernel(gain_ref, gate_up_ref, down_ref, both_ref, gate_ref, up_ref, *down_refs):
    rows, cols = gate_ref.shape[1], down_refs[0].shape[2]
    for which, second_ref in enumerate((gate_ref, up_ref)):
        scaled = (gate_up_ref[which].astype(jnp.float32) * gain_ref[...]).astype(jnp.bfloat16)
        both_ref[0, which] = scaled[:rows]
        second_ref[0] = scaled[rows:]
    for part, out_ref in enumerate(down_refs):
        out_ref[0] = down_ref[:, part * cols : (part + 1) * cols]


def cut_weights(w_gate_up, w_down, gain, outer_count):
    _, features, width = w_gate_up.shape
    cols = width // outer_count
    rows = features // PARTS
    if cols % HEAD_WIDTH:
        wide = (w_gate_up.astype(jnp.float32) * gain[None]).astype(jnp.bfloat16)
        wide = jnp.transpose(wide.reshape(2, PARTS, rows, outer_count, cols), (1, 3, 0, 2, 4))
        tall = jnp.transpose(w_down.reshape(outer_count, cols, PARTS, rows), (2, 0, 1, 3))
        return [wide[0], wide[1, :, 0], wide[1, :, 1], *tall]
    return pl.pallas_call(
        cut_kernel,
        grid=(outer_count,),
        in_specs=[
            pl.BlockSpec((features, 1), lambda p: (0, 0)),
            pl.BlockSpec((2, features, cols), lambda p: (0, 0, p)),
            pl.BlockSpec((cols, features), lambda p: (p, 0)),
        ],
        out_specs=[pl.BlockSpec((1, 2, rows, cols), lambda p: (p, 0, 0, 0))]
        + [pl.BlockSpec((1, rows, cols), lambda p: (p, 0, 0))] * 2
        + [pl.BlockSpec((1, cols, rows), lambda p: (p, 0, 0))] * PARTS,
        out_shape=[jax.ShapeDtypeStruct((outer_count, 2, rows, cols), jnp.bfloat16)]
        + [jax.ShapeDtypeStruct((outer_count, rows, cols), jnp.bfloat16)] * 2
        + [jax.ShapeDtypeStruct((outer_count, cols, rows), jnp.bfloat16)] * PARTS,
        compiler_params=pltpu.CompilerParams(vmem_limit_bytes=VMEM_LIMIT),
        cost_estimate=BRIEF,
        name="cut_weights",
    )(gain, w_gate_up, w_down)


def projection_kernel(block_count, place_ref, *refs):
    blocks, weights_ref = refs[:block_count], refs[block_count]
    kept_ref, sent_ref = refs[block_count + 1 : block_count + 3]
    inner, head = place_ref[0], place_ref[1]
    half, depth = kept_ref.shape[0], blocks[0].shape[1]
    for e in range(sent_ref.shape[0] + 1):
        rows = pl.ds(pl.multiple_of((head ^ e) * half, half), half)
        total = jnp.zeros(kept_ref.shape, jnp.float32)
        for a, block in enumerate(blocks):
            at = pl.ds(pl.multiple_of((inner ^ a) * depth, depth), depth) if block_count > 1 else slice(None)
            total = total + jnp.dot(block[rows, :], weights_ref[at, :], preferred_element_type=jnp.float32)
        if e == 0:
            kept_ref[...] = total.astype(jnp.bfloat16)
        else:
            sent_ref[e - 1] = total.astype(jnp.bfloat16)
    if block_count > 1:
        context_ref = refs[block_count + 3]
        tokens = context_ref.shape[0]
        own = pl.ds(pl.multiple_of(inner * tokens, tokens), tokens)
        for a, block in enumerate(blocks):
            context_ref[:, pl.ds(pl.multiple_of((inner ^ a) * depth, depth), depth)] = block[own, :]


def projection(blocks, weights, place, head_count, inner_count):
    rows, depth = blocks[0].shape
    half, width = rows // head_count, weights.shape[1]
    outs = [(half, width), (head_count - 1, half, width)]
    if len(blocks) > 1:
        outs.append((rows // inner_count, len(blocks) * depth))
    return pl.pallas_call(
        functools.partial(projection_kernel, len(blocks)),
        in_specs=[SMEM] + [VMEM] * (len(blocks) + 1),
        out_specs=[VMEM] * len(outs),
        out_shape=[jax.ShapeDtypeStruct(shape, jnp.bfloat16) for shape in outs],
        compiler_params=pltpu.CompilerParams(vmem_limit_bytes=VMEM_LIMIT),
        cost_estimate=BRIEF,
        name="projection",
    )(place, *blocks, weights)


def gate_up_kernel(head_count, *refs):
    tokens = refs[:head_count]
    both, gate, up = refs[head_count : head_count + 3]
    *earlier, out_ref, held, near, token_sems, weight_sems = refs[head_count + 3 :]
    rows, depth = tokens[0].shape
    copies = [
        [pltpu.make_async_copy(both.at[:, which], near.at[which, :, 0], weight_sems.at[which, 0]),
         pltpu.make_async_copy(second, near.at[which, :, 1], weight_sems.at[which, 1])]
        for which, second in enumerate((gate, up))
    ]
    for e, token_ref in enumerate(tokens):
        copies[0].append(pltpu.make_async_copy(token_ref, held.at[pl.ds(e * rows, rows)], token_sems.at[e]))
    for group in copies:
        for copy in group:
            copy.start()
    for which, group in enumerate(copies):
        for copy in group:
            copy.wait()
        block = near[which].reshape(depth, -1)
        for tile in row_tiles(held.shape[0]):
            product = jnp.dot(held[tile, :], block, preferred_element_type=jnp.float32)
            if earlier:
                product = earlier[0][which, tile, :].astype(jnp.float32) + product
            out_ref[which, tile, :] = product.astype(jnp.bfloat16)


def gate_up(tokens, streams, earlier=()):
    rows, depth = tokens[0].shape
    sources, stream_rows, cols = streams[1].shape
    all_rows = rows * len(tokens)
    return pl.pallas_call(
        functools.partial(gate_up_kernel, len(tokens)),
        in_specs=[ANY] * (len(tokens) + len(streams)) + [VMEM] * len(earlier),
        out_specs=VMEM,
        out_shape=jax.ShapeDtypeStruct((2, all_rows, cols), jnp.bfloat16),
        scratch_shapes=[
            pltpu.VMEM((all_rows, depth), jnp.bfloat16),
            pltpu.VMEM((2, sources, PARTS, stream_rows, cols), jnp.bfloat16),
            pltpu.SemaphoreType.DMA((len(tokens),)),
            pltpu.SemaphoreType.DMA((2, PARTS)),
        ],
        compiler_params=pltpu.CompilerParams(vmem_limit_bytes=VMEM_LIMIT),
        cost_estimate=BRIEF,
        name="gate_up",
    )(*tokens, *streams, *earlier)


def activation_kernel(here_ref, there_ref, out_ref):
    gate = here_ref[0].astype(jnp.float32) + there_ref[0].astype(jnp.float32)
    up = here_ref[1].astype(jnp.float32) + there_ref[1].astype(jnp.float32)
    out_ref[...] = (gate / (1.0 + jnp.exp(-gate)) * up).astype(jnp.bfloat16)


def activation(here, there, part, parts):
    _, rows, cols = here.shape
    rows = rows // parts
    step = min(rows, ROW_TILE)
    first = part * rows // step
    return pl.pallas_call(
        activation_kernel,
        grid=(rows // step,),
        in_specs=[pl.BlockSpec((2, step, cols), lambda t: (0, first + t, 0))] * 2,
        out_specs=pl.BlockSpec((step, cols), lambda t: (t, 0)),
        out_shape=jax.ShapeDtypeStruct((rows, cols), jnp.bfloat16),
        compiler_params=pltpu.CompilerParams(vmem_limit_bytes=VMEM_LIMIT),
        cost_estimate=BRIEF,
        name="activation",
    )(here, there)


def down_kernel(activated_ref, weights_ref, out_ref):
    sources, _, cols = weights_ref.shape
    if cols % HEAD_WIDTH:
        blocks = [weights_ref[s] for s in range(sources)]
    else:
        blocks = [jnp.concatenate([weights_ref[s] for s in range(sources)], axis=1)]
    for s, block in enumerate(blocks):
        product = jnp.dot(activated_ref[...], block, preferred_element_type=jnp.float32)
        out_ref[:, s * block.shape[1] : (s + 1) * block.shape[1]] = product.astype(jnp.bfloat16)


def down_product(activated, weights):
    sources, _, cols = weights.shape
    return pl.pallas_call(
        down_kernel,
        in_specs=[VMEM, VMEM],
        out_specs=VMEM,
        out_shape=jax.ShapeDtypeStruct((activated.shape[0], sources * cols), jnp.bfloat16),
        compiler_params=pltpu.CompilerParams(vmem_limit_bytes=VMEM_LIMIT),
        cost_estimate=BRIEF,
        name="down",
    )(activated, weights)


def per_device(query, key, value, doc_lengths, resid, norm_gain, w_out, w_gate_up, w_down):
    inner_count = lax.axis_size("inner")
    outer_count = lax.axis_size("outer")
    head_count = lax.axis_size("head")
    outer, inner, head = lax.axis_index("outer"), lax.axis_index("inner"), lax.axis_index("head")
    rows = query.shape[0]
    plane_rows = rows * inner_count * head_count
    reach = plane_rows * outer_count // WINDOW_PER_DOC
    feature_rows = w_gate_up.shape[1]
    hidden_cols = w_gate_up.shape[2] // outer_count
    bounds = jnp.cumsum(doc_lengths)
    hops = reach // plane_rows
    token_rows = plane_rows // inner_count
    half = plane_rows // head_count
    packing = (rows, head_count, KEY_VALUE_HEADS // head_count, -1)

    weights_out = lax.all_gather(w_out, "outer", axis=1, tiled=True)
    if packing[2] == inner_count and hops == 1:
        earlier = [lax.ppermute(part, "outer", [(s, s + 1) for s in range(outer_count - 1)]) for part in (key, value)]
        groups = jnp.concatenate([part.reshape(packing) for part in (query, key, value, *earlier)], axis=3)
        groups = jnp.transpose(groups, (2, 1, 0, 3)).reshape(inner_count * head_count, rows, -1)
        packed = lax.all_to_all(groups, ("inner", "head"), split_axis=0, concat_axis=0, tiled=True)
        packed = packed.reshape(plane_rows, -1)
        starts = document_starts(bounds, outer * plane_rows, plane_rows)
        own_context = attention(packed, packed, Q_COLS // KV_COLS + 1, starts, reach)
        blocks = blocks_over_inner(own_context)
    else:
        groups = jnp.concatenate([part.reshape(packing) for part in (query, key, value)], axis=3)
        groups = jnp.transpose(groups[:, :, 0], (1, 0, 2))
        packed = lax.all_to_all(groups, "head", split_axis=0, concat_axis=0, tiled=True).reshape(token_rows, -1)
        plane_kv = lax.all_gather(packed[:, Q_COLS:], "inner", axis=0, tiled=True)
        every_kv = jnp.concatenate([earlier_planes(plane_kv, hops), plane_kv], axis=0)
        halo = lax.dynamic_slice_in_dim(every_kv, inner * token_rows, reach, 0)
        starts = document_starts(bounds, outer * plane_rows + inner * token_rows, token_rows)
        own_context = attention(packed, halo, 0, starts, reach)
        blocks = [lax.all_gather(own_context, "inner", axis=0, tiled=True)]

    spread = functools.partial(lax.all_to_all, axis_name="outer", split_axis=0, concat_axis=0, tiled=True)
    over_y = functools.partial(swap, axis="inner", distance=2)
    fence = lambda *arrays: lax.optimization_barrier(arrays)
    own_gain = lax.dynamic_slice_in_dim(norm_gain, outer * feature_rows, feature_rows, 0)
    cut = cut_weights(w_gate_up, w_down, own_gain[:, None], outer_count)

    place = jnp.stack([inner, head]).astype(jnp.int32)
    weights_out, *blocks = fence(weights_out, *blocks)
    first = spread(after(cut[0], weights_out))
    kept, sent, *whole = projection(blocks, weights_out, place, head_count, inner_count)
    context = whole[0] if whole else own_context
    projected = kept.astype(jnp.float32)
    for e in range(1, head_count):
        projected = projected + swap(sent[e - 1], "head", e).astype(jnp.float32)
    own_resid = lax.dynamic_slice_in_dim(resid, head * half, half, 0)
    hidden_part = (own_resid.astype(jnp.float32) + projected).astype(jnp.bfloat16)

    upper = inner // 2
    own_rows = half // 2
    mine = lax.dynamic_slice_in_dim(hidden_part, upper * own_rows, own_rows, 0)
    others = lax.dynamic_slice_in_dim(hidden_part, (1 - upper) * own_rows, own_rows, 0)
    others, first = fence(over_y(others), first)
    state = [mine.astype(jnp.float32), others.astype(jnp.float32)]
    squares = sum([jnp.sum(block * block, axis=1) for block in state])
    squares = squares + swap(squares, "inner", 1)
    inverse = lax.rsqrt(squares / D + 1e-05)[:, None]
    part_rows = feature_rows // PARTS
    normed = jnp.concatenate([block * inverse for block in state], axis=1).astype(jnp.bfloat16)
    state = [block.reshape(own_rows, outer_count, PARTS, part_rows) for block in state]
    state = [[block[:, :, part].reshape(own_rows, -1) for part in range(PARTS)] for block in state]

    tokens = lax.all_gather(normed, "outer", axis=0, tiled=True)
    second, first_y, tokens, state = fence(spread(after(cut[1], normed)), over_y(first), tokens, state)
    tokens = jnp.split(tokens, 2, axis=1)
    tokens = [[swap(block, "head", e) if e else block for e in range(head_count)] for block in tokens]
    third, second_y, tokens[0] = fence(spread(after(cut[2], second)), over_y(second), tokens[0])
    own_sums = gate_up(tokens[0], [first, second, third])
    fourth, third_y, own_sums = fence(spread(after(cut[3], third)), over_y(third), own_sums)
    sums = gate_up(tokens[1], [first_y, second_y, third_y], [own_sums])
    other_sums = swap(sums, "inner", 1)
    activated = [activation(sums, other_sums, e, head_count) for e in range(1, head_count)]
    sent = [down_product(rows_of, fourth) for rows_of in activated]
    activated = [activation(after(sums, sent[-1]), other_sums, 0, head_count), *activated]

    def over_heads(weights, moved=None):
        if moved is None:
            sent = [down_product(rows_of, weights) for rows_of in activated[1:]]
            moved = [swap(rows_of, "head", e) for e, rows_of in enumerate(sent, 1)]
        total = down_product(activated[0], weights).astype(jnp.float32)
        for rows_of in moved:
            total = total + rows_of.astype(jnp.float32)
        return total.reshape(outer_count, own_rows, -1)

    moved = [[swap(piece, "head", e) for piece in jnp.split(rows_of, 2)] for e, rows_of in enumerate(sent, 1)]
    fifth, fourth_y, moved[0][0] = fence(spread(after(cut[4], fourth)), over_y(fourth), moved[0][0])
    fifth_y = over_y(fifth)
    paired = {(0, 0): over_heads(fourth, [jnp.concatenate(pieces) for pieces in moved])}
    paired[1, 0] = over_heads(fourth_y)
    paired[0, 1] = over_heads(fifth)
    paired[1, 1] = over_heads(after(fifth_y, paired[0, 0]))

    pieces = [[None] * PARTS, [None] * PARTS]
    for part in range(PARTS):
        for a in range(2):
            total = state[a][part] + lax.dynamic_index_in_dim(paired[a, part], outer, 0, False)
            for d in range(1, outer_count):
                sent = lax.dynamic_index_in_dim(paired[a, part], outer ^ d, 0, False).astype(jnp.bfloat16)
                total = total + swap(sent, "outer", d).astype(jnp.float32)
            total = total.astype(jnp.bfloat16)
            pieces[a][part] = (over_y(total) if a else total).reshape(own_rows, outer_count, 1, part_rows)
    halves = [jnp.concatenate(parts, axis=2).reshape(own_rows, -1) for parts in pieces]
    layer_out = jnp.zeros((half, halves[0].shape[1]), jnp.bfloat16)
    layer_out = lax.dynamic_update_slice(layer_out, halves[0], (upper * own_rows, 0))
    layer_out = lax.dynamic_update_slice(layer_out, halves[1], ((1 - upper) * own_rows, 0))
    return (context, layer_out)


def solution(mesh):
    placed = (
        P(("outer", "inner", "head"), None),
        P(("outer", "inner", "head"), None),
        P(("outer", "inner", "head"), None),
        P(),
        P("outer", "inner"),
        P("inner"),
        P("head", ("inner", "outer")),
        P(None, ("inner", "outer"), "head"),
        P("head", ("inner", "outer")),
    )
    return jax.shard_map(
        per_device,
        mesh=mesh,
        in_specs=placed,
        out_specs=(P(("outer", "inner"), "head"), P(("outer", "head"), "inner")),
        check_vma=False,
    )
```

```python
import functools

import jax
import jax.numpy as jnp
from jax import lax
from jax.experimental import pallas as pl
from jax.experimental.pallas import tpu as pltpu
from jax.sharding import PartitionSpec as P

D = 4096
QUERY_HEADS = 32
KEY_VALUE_HEADS = 8
HEAD_WIDTH = 128
GROUP = QUERY_HEADS // KEY_VALUE_HEADS
Q_COLS = GROUP * HEAD_WIDTH
KV_COLS = 2 * HEAD_WIDTH
WINDOW_PER_DOC = 4
QUERY_TILE = 128
ROW_TILE = 256
PARTS = 2
VMEM_LIMIT = 48 * 1024 * 1024
BRIEF = pl.CostEstimate(flops=1, bytes_accessed=1, transcendentals=0)
ANY = pl.BlockSpec(memory_space=pl.ANY)
VMEM = pl.BlockSpec(memory_space=pltpu.VMEM)
SMEM = pl.BlockSpec(memory_space=pltpu.SMEM)


def swap(array, axis, distance):
    if distance == 0:
        return array
    count = lax.axis_size(axis)
    return lax.ppermute(array, axis, [(s, s ^ distance) for s in range(count)])


def after(array, earlier):
    return lax.optimization_barrier((array, earlier))[0]


def blocks_over_inner(block):
    across = swap(block, "inner", 2)
    return [block, swap(block, "inner", 1), across, swap(across, "inner", 1)]


def earlier_planes(kv, hops):
    count = lax.axis_size("outer")
    moved = [lax.ppermute(kv, "outer", [(s, s + d) for s in range(count - d)]) for d in range(hops, 0, -1)]
    return jnp.concatenate(moved, axis=0)


def document_starts(bounds, first, rows):
    place = first + jnp.arange(rows, dtype=jnp.int32)
    starts = jnp.max(jnp.where(bounds[None, :] <= place[:, None], bounds[None, :], 0), axis=1) - first
    return starts[:, None].astype(jnp.int32)


def row_tiles(rows):
    step = ROW_TILE if rows % ROW_TILE == 0 else rows
    return [slice(at, at + step) for at in range(0, rows, step)]


def attention_kernel(halo_rows, reach, starts_ref, queries_ref, own_ref, halo_ref, out_ref, keys, values):
    tile = pl.program_id(0)
    rows = queries_ref.shape[0]
    span = reach + rows

    @pl.when(tile == 0)
    def _():
        keys[:halo_rows, :] = halo_ref[:, :HEAD_WIDTH]
        values[:halo_rows, :] = halo_ref[:, HEAD_WIDTH:]
        keys[halo_rows:, :] = own_ref[:, :HEAD_WIDTH]
        values[halo_rows:, :] = own_ref[:, HEAD_WIDTH:]

    first = pl.multiple_of(tile * rows + (halo_rows - reach), rows)
    near_keys = keys[pl.ds(first, span), :]
    near_values = values[pl.ds(first, span), :]
    key_place = lax.broadcasted_iota(jnp.int32, (rows, span), 1)
    query_place = lax.broadcasted_iota(jnp.int32, (rows, span), 0) + reach
    start = starts_ref[...] - (first - halo_rows)
    allowed = (key_place <= query_place) & (key_place >= start)
    for g in range(GROUP):
        cols = slice(g * HEAD_WIDTH, (g + 1) * HEAD_WIDTH)
        scores = lax.dot_general(
            queries_ref[:, cols], near_keys, (((1,), (1,)), ((), ())), preferred_element_type=jnp.float32
        ) * (HEAD_WIDTH ** (-0.5))
        masked = jnp.where(allowed, scores, -1e30)
        row_max = jnp.max(masked, axis=1, keepdims=True)
        weights = jnp.exp(masked - row_max)
        totals = jnp.sum(weights, axis=1, keepdims=True)
        summed = jnp.dot(weights.astype(jnp.bfloat16), near_values, preferred_element_type=jnp.float32)
        out_ref[:, cols] = (summed / totals).astype(jnp.bfloat16)


def attention(packed, halo, halo_at, starts, reach):
    rows = packed.shape[0]
    halo_rows = halo.shape[0]
    return pl.pallas_call(
        functools.partial(attention_kernel, halo_rows, reach),
        grid=(rows // QUERY_TILE,),
        in_specs=[
            pl.BlockSpec((QUERY_TILE, 1), lambda t: (t, 0)),
            pl.BlockSpec((QUERY_TILE, Q_COLS), lambda t: (t, 0)),
            pl.BlockSpec((rows, KV_COLS), lambda t: (0, Q_COLS // KV_COLS)),
            pl.BlockSpec((halo_rows, KV_COLS), lambda t: (0, halo_at)),
        ],
        out_specs=pl.BlockSpec((QUERY_TILE, Q_COLS), lambda t: (t, 0)),
        out_shape=jax.ShapeDtypeStruct((rows, Q_COLS), jnp.bfloat16),
        scratch_shapes=[
            pltpu.VMEM((halo_rows + rows, HEAD_WIDTH), jnp.bfloat16),
            pltpu.VMEM((halo_rows + rows, HEAD_WIDTH), jnp.bfloat16),
        ],
        compiler_params=pltpu.CompilerParams(vmem_limit_bytes=VMEM_LIMIT),
        cost_estimate=BRIEF,
        name="attention",
    )(starts, packed, packed, halo)


def cut_kernel(gain_ref, gate_up_ref, down_ref, both_ref, gate_ref, up_ref, out_ref):
    rows, cols = gate_ref.shape[1], out_ref.shape[3]
    for which, second_ref in enumerate((gate_ref, up_ref)):
        scaled = (gate_up_ref[which].astype(jnp.float32) * gain_ref[...]).astype(jnp.bfloat16)
        both_ref[0, which] = scaled[:rows]
        second_ref[0] = scaled[rows:]
    for part in range(PARTS):
        out_ref[0, part] = down_ref[:, part * cols : (part + 1) * cols]


def cut_weights(w_gate_up, w_down, gain, outer_count):
    _, features, width = w_gate_up.shape
    cols = width // outer_count
    rows = features // PARTS
    if cols % HEAD_WIDTH:
        wide = (w_gate_up.astype(jnp.float32) * gain[None]).astype(jnp.bfloat16)
        wide = jnp.transpose(wide.reshape(2, PARTS, rows, outer_count, cols), (1, 3, 0, 2, 4))
        tall = jnp.transpose(w_down.reshape(outer_count, cols, PARTS, rows), (0, 2, 1, 3))
        return [wide[0], wide[1, :, 0], wide[1, :, 1], tall]
    return pl.pallas_call(
        cut_kernel,
        grid=(outer_count,),
        in_specs=[
            pl.BlockSpec((features, 1), lambda p: (0, 0)),
            pl.BlockSpec((2, features, cols), lambda p: (0, 0, p)),
            pl.BlockSpec((cols, features), lambda p: (p, 0)),
        ],
        out_specs=[pl.BlockSpec((1, 2, rows, cols), lambda p: (p, 0, 0, 0))]
        + [pl.BlockSpec((1, rows, cols), lambda p: (p, 0, 0))] * 2
        + [pl.BlockSpec((1, PARTS, cols, rows), lambda p: (p, 0, 0, 0))],
        out_shape=[jax.ShapeDtypeStruct((outer_count, 2, rows, cols), jnp.bfloat16)]
        + [jax.ShapeDtypeStruct((outer_count, rows, cols), jnp.bfloat16)] * 2
        + [jax.ShapeDtypeStruct((outer_count, PARTS, cols, rows), jnp.bfloat16)],
        compiler_params=pltpu.CompilerParams(vmem_limit_bytes=VMEM_LIMIT),
        cost_estimate=BRIEF,
        name="cut_weights",
    )(gain, w_gate_up, w_down)


def projection_kernel(block_count, place_ref, *refs):
    blocks, weights_ref = refs[:block_count], refs[block_count]
    kept_ref, sent_ref = refs[block_count + 1 : block_count + 3]
    inner, head = place_ref[0], place_ref[1]
    half, depth = kept_ref.shape[0], blocks[0].shape[1]
    for e in range(sent_ref.shape[0] + 1):
        rows = pl.ds(pl.multiple_of((head ^ e) * half, half), half)
        total = jnp.zeros(kept_ref.shape, jnp.float32)
        for a, block in enumerate(blocks):
            at = pl.ds(pl.multiple_of((inner ^ a) * depth, depth), depth) if block_count > 1 else slice(None)
            total = total + jnp.dot(block[rows, :], weights_ref[at, :], preferred_element_type=jnp.float32)
        if e == 0:
            kept_ref[...] = total.astype(jnp.bfloat16)
        else:
            sent_ref[e - 1] = total.astype(jnp.bfloat16)
    if block_count > 1:
        context_ref = refs[block_count + 3]
        tokens = context_ref.shape[0]
        own = pl.ds(pl.multiple_of(inner * tokens, tokens), tokens)
        for a, block in enumerate(blocks):
            context_ref[:, pl.ds(pl.multiple_of((inner ^ a) * depth, depth), depth)] = block[own, :]


def projection(blocks, weights, place, head_count, inner_count):
    rows, depth = blocks[0].shape
    half, width = rows // head_count, weights.shape[1]
    outs = [(half, width), (head_count - 1, half, width)]
    if len(blocks) > 1:
        outs.append((rows // inner_count, len(blocks) * depth))
    return pl.pallas_call(
        functools.partial(projection_kernel, len(blocks)),
        in_specs=[SMEM] + [VMEM] * (len(blocks) + 1),
        out_specs=[VMEM] * len(outs),
        out_shape=[jax.ShapeDtypeStruct(shape, jnp.bfloat16) for shape in outs],
        compiler_params=pltpu.CompilerParams(vmem_limit_bytes=VMEM_LIMIT),
        cost_estimate=BRIEF,
        name="projection",
    )(place, *blocks, weights)


def gate_up_kernel(head_count, *refs):
    tokens = refs[:head_count]
    both, gate, up = refs[head_count : head_count + 3]
    *earlier, out_ref, held, near, token_sems, weight_sems = refs[head_count + 3 :]
    rows, depth = tokens[0].shape
    copies = [
        [pltpu.make_async_copy(both.at[:, which], near.at[which, :, 0], weight_sems.at[which, 0]),
         pltpu.make_async_copy(second, near.at[which, :, 1], weight_sems.at[which, 1])]
        for which, second in enumerate((gate, up))
    ]
    for e, token_ref in enumerate(tokens):
        copies[0].append(pltpu.make_async_copy(token_ref, held.at[pl.ds(e * rows, rows)], token_sems.at[e]))
    for group in copies:
        for copy in group:
            copy.start()
    for which, group in enumerate(copies):
        for copy in group:
            copy.wait()
        block = near[which].reshape(depth, -1)
        for tile in row_tiles(held.shape[0]):
            product = jnp.dot(held[tile, :], block, preferred_element_type=jnp.float32)
            if earlier:
                product = earlier[0][which, tile, :].astype(jnp.float32) + product
            out_ref[which, tile, :] = product.astype(jnp.bfloat16)


def gate_up(tokens, streams, earlier=()):
    rows, depth = tokens[0].shape
    sources, stream_rows, cols = streams[1].shape
    all_rows = rows * len(tokens)
    return pl.pallas_call(
        functools.partial(gate_up_kernel, len(tokens)),
        in_specs=[ANY] * (len(tokens) + len(streams)) + [VMEM] * len(earlier),
        out_specs=VMEM,
        out_shape=jax.ShapeDtypeStruct((2, all_rows, cols), jnp.bfloat16),
        scratch_shapes=[
            pltpu.VMEM((all_rows, depth), jnp.bfloat16),
            pltpu.VMEM((2, sources, PARTS, stream_rows, cols), jnp.bfloat16),
            pltpu.SemaphoreType.DMA((len(tokens),)),
            pltpu.SemaphoreType.DMA((2, PARTS)),
        ],
        compiler_params=pltpu.CompilerParams(vmem_limit_bytes=VMEM_LIMIT),
        cost_estimate=BRIEF,
        name="gate_up",
    )(*tokens, *streams, *earlier)


def activation_kernel(here_ref, there_ref, out_ref):
    gate = here_ref[0].astype(jnp.float32) + there_ref[0].astype(jnp.float32)
    up = here_ref[1].astype(jnp.float32) + there_ref[1].astype(jnp.float32)
    out_ref[...] = (gate / (1.0 + jnp.exp(-gate)) * up).astype(jnp.bfloat16)


def activation(here, there, part, parts):
    _, rows, cols = here.shape
    rows = rows // parts
    step = min(rows, ROW_TILE)
    first = part * rows // step
    return pl.pallas_call(
        activation_kernel,
        grid=(rows // step,),
        in_specs=[pl.BlockSpec((2, step, cols), lambda t: (0, first + t, 0))] * 2,
        out_specs=pl.BlockSpec((step, cols), lambda t: (t, 0)),
        out_shape=jax.ShapeDtypeStruct((rows, cols), jnp.bfloat16),
        compiler_params=pltpu.CompilerParams(vmem_limit_bytes=VMEM_LIMIT),
        cost_estimate=BRIEF,
        name="activation",
    )(here, there)


def down_kernel(activated_ref, weights_ref, out_ref):
    sources, _, _, cols = weights_ref.shape
    if cols % HEAD_WIDTH:
        blocks = [weights_ref[s, 0] for s in range(sources)]
    else:
        blocks = [jnp.concatenate([weights_ref[s, 0] for s in range(sources)], axis=1)]
    for s, block in enumerate(blocks):
        product = jnp.dot(activated_ref[...], block, preferred_element_type=jnp.float32)
        out_ref[:, s * block.shape[1] : (s + 1) * block.shape[1]] = product.astype(jnp.bfloat16)


def down_product(activated, weights, part):
    sources, _, depth, cols = weights.shape
    out = (activated.shape[0], sources * cols)
    return pl.pallas_call(
        down_kernel,
        grid=(1,),
        in_specs=[
            pl.BlockSpec(activated.shape, lambda t: (0, 0)),
            pl.BlockSpec((sources, 1, depth, cols), lambda t: (0, part, 0, 0)),
        ],
        out_specs=pl.BlockSpec(out, lambda t: (0, 0)),
        out_shape=jax.ShapeDtypeStruct(out, jnp.bfloat16),
        compiler_params=pltpu.CompilerParams(vmem_limit_bytes=VMEM_LIMIT),
        cost_estimate=BRIEF,
        name="down",
    )(activated, weights)


def per_device(query, key, value, doc_lengths, resid, norm_gain, w_out, w_gate_up, w_down):
    inner_count = lax.axis_size("inner")
    outer_count = lax.axis_size("outer")
    head_count = lax.axis_size("head")
    outer, inner, head = lax.axis_index("outer"), lax.axis_index("inner"), lax.axis_index("head")
    rows = query.shape[0]
    plane_rows = rows * inner_count * head_count
    reach = plane_rows * outer_count // WINDOW_PER_DOC
    feature_rows = w_gate_up.shape[1]
    hidden_cols = w_gate_up.shape[2] // outer_count
    bounds = jnp.cumsum(doc_lengths)
    hops = reach // plane_rows
    token_rows = plane_rows // inner_count
    half = plane_rows // head_count
    packing = (rows, head_count, KEY_VALUE_HEADS // head_count, -1)

    weights_out = lax.all_gather(w_out, "outer", axis=1, tiled=True)
    if packing[2] == inner_count and hops == 1:
        earlier = [lax.ppermute(part, "outer", [(s, s + 1) for s in range(outer_count - 1)]) for part in (key, value)]
        groups = jnp.concatenate([part.reshape(packing) for part in (query, key, value, *earlier)], axis=3)
        groups = jnp.transpose(groups, (2, 1, 0, 3)).reshape(inner_count * head_count, rows, -1)
        packed = lax.all_to_all(groups, ("inner", "head"), split_axis=0, concat_axis=0, tiled=True)
        packed = packed.reshape(plane_rows, -1)
        starts = document_starts(bounds, outer * plane_rows, plane_rows)
        own_context = attention(packed, packed, Q_COLS // KV_COLS + 1, starts, reach)
        blocks = blocks_over_inner(own_context)
    else:
        groups = jnp.concatenate([part.reshape(packing) for part in (query, key, value)], axis=3)
        groups = jnp.transpose(groups[:, :, 0], (1, 0, 2))
        packed = lax.all_to_all(groups, "head", split_axis=0, concat_axis=0, tiled=True).reshape(token_rows, -1)
        plane_kv = lax.all_gather(packed[:, Q_COLS:], "inner", axis=0, tiled=True)
        every_kv = jnp.concatenate([earlier_planes(plane_kv, hops), plane_kv], axis=0)
        halo = lax.dynamic_slice_in_dim(every_kv, inner * token_rows, reach, 0)
        starts = document_starts(bounds, outer * plane_rows + inner * token_rows, token_rows)
        own_context = attention(packed, halo, 0, starts, reach)
        blocks = [lax.all_gather(own_context, "inner", axis=0, tiled=True)]

    spread = functools.partial(lax.all_to_all, axis_name="outer", split_axis=0, concat_axis=0, tiled=True)
    over_y = functools.partial(swap, axis="inner", distance=2)
    fence = lambda *arrays: lax.optimization_barrier(arrays)
    own_gain = lax.dynamic_slice_in_dim(norm_gain, outer * feature_rows, feature_rows, 0)
    cut = cut_weights(w_gate_up, w_down, own_gain[:, None], outer_count)

    place = jnp.stack([inner, head]).astype(jnp.int32)
    weights_out, *blocks = fence(weights_out, *blocks)
    first = spread(after(cut[0], weights_out))
    kept, sent, *whole = projection(blocks, weights_out, place, head_count, inner_count)
    context = whole[0] if whole else own_context
    projected = kept.astype(jnp.float32)
    for e in range(1, head_count):
        projected = projected + swap(sent[e - 1], "head", e).astype(jnp.float32)
    own_resid = lax.dynamic_slice_in_dim(resid, head * half, half, 0)
    hidden_part = (own_resid.astype(jnp.float32) + projected).astype(jnp.bfloat16)

    upper = inner // 2
    own_rows = half // 2
    mine = lax.dynamic_slice_in_dim(hidden_part, upper * own_rows, own_rows, 0)
    others = lax.dynamic_slice_in_dim(hidden_part, (1 - upper) * own_rows, own_rows, 0)
    others, first = fence(over_y(others), first)
    state = [mine.astype(jnp.float32), others.astype(jnp.float32)]
    squares = sum([jnp.sum(block * block, axis=1) for block in state])
    squares = squares + swap(squares, "inner", 1)
    inverse = lax.rsqrt(squares / D + 1e-05)[:, None]
    part_rows = feature_rows // PARTS
    normed = jnp.concatenate([block * inverse for block in state], axis=1).astype(jnp.bfloat16)
    state = [block.reshape(own_rows, outer_count, PARTS, part_rows) for block in state]
    state = [[block[:, :, part].reshape(own_rows, -1) for part in range(PARTS)] for block in state]

    tokens = lax.all_gather(normed, "outer", axis=0, tiled=True)
    second, first_y, tokens, state = fence(spread(after(cut[1], normed)), over_y(first), tokens, state)
    tokens = jnp.split(tokens, 2, axis=1)
    tokens = [[swap(block, "head", e) if e else block for e in range(head_count)] for block in tokens]
    third, second_y, tokens[0] = fence(spread(after(cut[2], second)), over_y(second), tokens[0])
    own_sums = gate_up(tokens[0], [first, second, third])
    fourth = spread(after(cut[3], third))
    third_y, own_sums = fence(over_y(third), own_sums)
    sums = gate_up(tokens[1], [first_y, second_y, third_y], [own_sums])
    fourth, sums = fence(fourth, sums)
    other_sums = swap(sums, "inner", 1)
    fourth_y = [over_y(fourth[:, part : part + 1]) for part in range(PARTS)]
    activated = [activation(sums, other_sums, e, head_count) for e in range(1, head_count)]
    sent = [[down_product(rows_of, fourth, part) for rows_of in activated] for part in range(PARTS)]
    activated = [activation(after(sums, sent[-1][-1]), other_sums, 0, head_count), *activated]

    def over_heads(weights, part, sent=None):
        if sent is None:
            sent = [down_product(rows_of, weights, part) for rows_of in activated[1:]]
        moved = [swap(rows_of, "head", e) for e, rows_of in enumerate(sent, 1)]
        total = down_product(activated[0], weights, part).astype(jnp.float32)
        for rows_of in moved:
            total = total + rows_of.astype(jnp.float32)
        return total.reshape(outer_count, own_rows, -1)

    paired = {(0, part): over_heads(fourth, part, sent[part]) for part in range(PARTS)}
    for part in range(PARTS):
        paired[1, part] = over_heads(after(fourth_y[part], paired[0, part]), 0)

    pieces = [[None] * PARTS, [None] * PARTS]
    for part in range(PARTS):
        for a in range(2):
            total = state[a][part] + lax.dynamic_index_in_dim(paired[a, part], outer, 0, False)
            for d in range(1, outer_count):
                sent = lax.dynamic_index_in_dim(paired[a, part], outer ^ d, 0, False).astype(jnp.bfloat16)
                total = total + swap(sent, "outer", d).astype(jnp.float32)
            total = total.astype(jnp.bfloat16)
            pieces[a][part] = (over_y(total) if a else total).reshape(own_rows, outer_count, 1, part_rows)
    halves = [jnp.concatenate(parts, axis=2).reshape(own_rows, -1) for parts in pieces]
    layer_out = jnp.zeros((half, halves[0].shape[1]), jnp.bfloat16)
    layer_out = lax.dynamic_update_slice(layer_out, halves[0], (upper * own_rows, 0))
    layer_out = lax.dynamic_update_slice(layer_out, halves[1], ((1 - upper) * own_rows, 0))
    return (context, layer_out)


def solution(mesh):
    placed = (
        P(("outer", "inner", "head"), None),
        P(("outer", "inner", "head"), None),
        P(("outer", "inner", "head"), None),
        P(),
        P("outer", "inner"),
        P("inner"),
        P("head", ("inner", "outer")),
        P(None, ("inner", "outer"), "head"),
        P("head", ("inner", "outer")),
    )
    return jax.shard_map(
        per_device,
        mesh=mesh,
        in_specs=placed,
        out_specs=(P(("outer", "inner"), "head"), P(("outer", "head"), "inner")),
        check_vma=False,
    )
```

```python
import functools

import jax
import jax.numpy as jnp
from jax import lax
from jax.experimental import pallas as pl
from jax.experimental.pallas import tpu as pltpu
from jax.sharding import PartitionSpec as P

D = 4096
QUERY_HEADS = 32
KEY_VALUE_HEADS = 8
HEAD_WIDTH = 128
GROUP = QUERY_HEADS // KEY_VALUE_HEADS
Q_COLS = GROUP * HEAD_WIDTH
KV_COLS = 2 * HEAD_WIDTH
WINDOW_PER_DOC = 4
QUERY_TILE = 128
ROW_TILE = 256
PARTS = 2
VMEM_LIMIT = 48 * 1024 * 1024
BRIEF = pl.CostEstimate(flops=1, bytes_accessed=1, transcendentals=0)
ANY = pl.BlockSpec(memory_space=pl.ANY)
VMEM = pl.BlockSpec(memory_space=pltpu.VMEM)
SMEM = pl.BlockSpec(memory_space=pltpu.SMEM)


def swap(array, axis, distance):
    if distance == 0:
        return array
    count = lax.axis_size(axis)
    return lax.ppermute(array, axis, [(s, s ^ distance) for s in range(count)])


def after(array, earlier):
    return lax.optimization_barrier((array, earlier))[0]


def blocks_over_inner(block):
    across = swap(block, "inner", 2)
    return [block, swap(block, "inner", 1), across, swap(across, "inner", 1)]


def earlier_planes(kv, hops):
    count = lax.axis_size("outer")
    moved = [lax.ppermute(kv, "outer", [(s, s + d) for s in range(count - d)]) for d in range(hops, 0, -1)]
    return jnp.concatenate(moved, axis=0)


def document_starts(bounds, first, rows):
    place = first + jnp.arange(rows, dtype=jnp.int32)
    starts = jnp.max(jnp.where(bounds[None, :] <= place[:, None], bounds[None, :], 0), axis=1) - first
    return starts[:, None].astype(jnp.int32)


def row_tiles(rows):
    step = ROW_TILE if rows % ROW_TILE == 0 else rows
    return [slice(at, at + step) for at in range(0, rows, step)]


def attention_kernel(halo_rows, reach, starts_ref, queries_ref, own_ref, halo_ref, out_ref, keys, values):
    tile = pl.program_id(0)
    rows = queries_ref.shape[0]
    span = reach + rows

    @pl.when(tile == 0)
    def _():
        keys[:halo_rows, :] = halo_ref[:, :HEAD_WIDTH]
        values[:halo_rows, :] = halo_ref[:, HEAD_WIDTH:]
        keys[halo_rows:, :] = own_ref[:, :HEAD_WIDTH]
        values[halo_rows:, :] = own_ref[:, HEAD_WIDTH:]

    first = pl.multiple_of(tile * rows + (halo_rows - reach), rows)
    near_keys = keys[pl.ds(first, span), :]
    near_values = values[pl.ds(first, span), :]
    key_place = lax.broadcasted_iota(jnp.int32, (rows, span), 1)
    query_place = lax.broadcasted_iota(jnp.int32, (rows, span), 0) + reach
    start = starts_ref[...] - (first - halo_rows)
    allowed = (key_place <= query_place) & (key_place >= start)
    for g in range(GROUP):
        cols = slice(g * HEAD_WIDTH, (g + 1) * HEAD_WIDTH)
        scores = lax.dot_general(
            queries_ref[:, cols], near_keys, (((1,), (1,)), ((), ())), preferred_element_type=jnp.float32
        ) * (HEAD_WIDTH ** (-0.5))
        masked = jnp.where(allowed, scores, -1e30)
        row_max = jnp.max(masked, axis=1, keepdims=True)
        weights = jnp.exp(masked - row_max)
        totals = jnp.sum(weights, axis=1, keepdims=True)
        summed = jnp.dot(weights.astype(jnp.bfloat16), near_values, preferred_element_type=jnp.float32)
        out_ref[:, cols] = (summed / totals).astype(jnp.bfloat16)


def attention(packed, halo, halo_at, starts, reach):
    rows = packed.shape[0]
    halo_rows = halo.shape[0]
    return pl.pallas_call(
        functools.partial(attention_kernel, halo_rows, reach),
        grid=(rows // QUERY_TILE,),
        in_specs=[
            pl.BlockSpec((QUERY_TILE, 1), lambda t: (t, 0)),
            pl.BlockSpec((QUERY_TILE, Q_COLS), lambda t: (t, 0)),
            pl.BlockSpec((rows, KV_COLS), lambda t: (0, Q_COLS // KV_COLS)),
            pl.BlockSpec((halo_rows, KV_COLS), lambda t: (0, halo_at)),
        ],
        out_specs=pl.BlockSpec((QUERY_TILE, Q_COLS), lambda t: (t, 0)),
        out_shape=jax.ShapeDtypeStruct((rows, Q_COLS), jnp.bfloat16),
        scratch_shapes=[
            pltpu.VMEM((halo_rows + rows, HEAD_WIDTH), jnp.bfloat16),
            pltpu.VMEM((halo_rows + rows, HEAD_WIDTH), jnp.bfloat16),
        ],
        compiler_params=pltpu.CompilerParams(vmem_limit_bytes=VMEM_LIMIT),
        cost_estimate=BRIEF,
        name="attention",
    )(starts, packed, packed, halo)


def cut_kernel(gain_ref, gate_up_ref, down_ref, both_ref, gate_ref, up_ref, out_ref):
    rows, cols = gate_ref.shape[1], out_ref.shape[3]
    for which, second_ref in enumerate((gate_ref, up_ref)):
        scaled = (gate_up_ref[which].astype(jnp.float32) * gain_ref[...]).astype(jnp.bfloat16)
        both_ref[0, which] = scaled[:rows]
        second_ref[0] = scaled[rows:]
    for part in range(PARTS):
        out_ref[0, part] = down_ref[:, part * cols : (part + 1) * cols]


def cut_weights(w_gate_up, w_down, gain, outer_count):
    _, features, width = w_gate_up.shape
    cols = width // outer_count
    rows = features // PARTS
    if cols % HEAD_WIDTH:
        wide = (w_gate_up.astype(jnp.float32) * gain[None]).astype(jnp.bfloat16)
        wide = jnp.transpose(wide.reshape(2, PARTS, rows, outer_count, cols), (1, 3, 0, 2, 4))
        tall = jnp.transpose(w_down.reshape(outer_count, cols, PARTS, rows), (0, 2, 1, 3))
        return [wide[0], wide[1, :, 0], wide[1, :, 1], tall]
    return pl.pallas_call(
        cut_kernel,
        grid=(outer_count,),
        in_specs=[
            pl.BlockSpec((features, 1), lambda p: (0, 0)),
            pl.BlockSpec((2, features, cols), lambda p: (0, 0, p)),
            pl.BlockSpec((cols, features), lambda p: (p, 0)),
        ],
        out_specs=[pl.BlockSpec((1, 2, rows, cols), lambda p: (p, 0, 0, 0))]
        + [pl.BlockSpec((1, rows, cols), lambda p: (p, 0, 0))] * 2
        + [pl.BlockSpec((1, PARTS, cols, rows), lambda p: (p, 0, 0, 0))],
        out_shape=[jax.ShapeDtypeStruct((outer_count, 2, rows, cols), jnp.bfloat16)]
        + [jax.ShapeDtypeStruct((outer_count, rows, cols), jnp.bfloat16)] * 2
        + [jax.ShapeDtypeStruct((outer_count, PARTS, cols, rows), jnp.bfloat16)],
        compiler_params=pltpu.CompilerParams(vmem_limit_bytes=VMEM_LIMIT),
        cost_estimate=BRIEF,
        name="cut_weights",
    )(gain, w_gate_up, w_down)


def projection_kernel(block_count, place_ref, *refs):
    blocks, weights_ref = refs[:block_count], refs[block_count]
    kept_ref, sent_ref = refs[block_count + 1 : block_count + 3]
    inner, head = place_ref[0], place_ref[1]
    half, depth = kept_ref.shape[0], blocks[0].shape[1]
    for e in range(sent_ref.shape[0] + 1):
        rows = pl.ds(pl.multiple_of((head ^ e) * half, half), half)
        total = jnp.zeros(kept_ref.shape, jnp.float32)
        for a, block in enumerate(blocks):
            at = pl.ds(pl.multiple_of((inner ^ a) * depth, depth), depth) if block_count > 1 else slice(None)
            total = total + jnp.dot(block[rows, :], weights_ref[at, :], preferred_element_type=jnp.float32)
        if e == 0:
            kept_ref[...] = total.astype(jnp.bfloat16)
        else:
            sent_ref[e - 1] = total.astype(jnp.bfloat16)
    if block_count > 1:
        context_ref = refs[block_count + 3]
        tokens = context_ref.shape[0]
        own = pl.ds(pl.multiple_of(inner * tokens, tokens), tokens)
        for a, block in enumerate(blocks):
            context_ref[:, pl.ds(pl.multiple_of((inner ^ a) * depth, depth), depth)] = block[own, :]


def projection(blocks, weights, place, head_count, inner_count):
    rows, depth = blocks[0].shape
    half, width = rows // head_count, weights.shape[1]
    outs = [(half, width), (head_count - 1, half, width)]
    if len(blocks) > 1:
        outs.append((rows // inner_count, len(blocks) * depth))
    return pl.pallas_call(
        functools.partial(projection_kernel, len(blocks)),
        in_specs=[SMEM] + [VMEM] * (len(blocks) + 1),
        out_specs=[VMEM] * len(outs),
        out_shape=[jax.ShapeDtypeStruct(shape, jnp.bfloat16) for shape in outs],
        compiler_params=pltpu.CompilerParams(vmem_limit_bytes=VMEM_LIMIT),
        cost_estimate=BRIEF,
        name="projection",
    )(place, *blocks, weights)


def gate_up_kernel(head_count, *refs):
    tokens = refs[:head_count]
    both, gate, up = refs[head_count : head_count + 3]
    *earlier, out_ref, held, near, token_sems, weight_sems = refs[head_count + 3 :]
    rows, depth = tokens[0].shape
    copies = [
        [pltpu.make_async_copy(both.at[:, which], near.at[which, :, 0], weight_sems.at[which, 0]),
         pltpu.make_async_copy(second, near.at[which, :, 1], weight_sems.at[which, 1])]
        for which, second in enumerate((gate, up))
    ]
    for e, token_ref in enumerate(tokens):
        copies[0].append(pltpu.make_async_copy(token_ref, held.at[pl.ds(e * rows, rows)], token_sems.at[e]))
    for group in copies:
        for copy in group:
            copy.start()
    for which, group in enumerate(copies):
        for copy in group:
            copy.wait()
        block = near[which].reshape(depth, -1)
        for tile in row_tiles(held.shape[0]):
            product = jnp.dot(held[tile, :], block, preferred_element_type=jnp.float32)
            if earlier:
                product = earlier[0][which, tile, :].astype(jnp.float32) + product
            out_ref[which, tile, :] = product.astype(jnp.bfloat16)


def gate_up(tokens, streams, earlier=()):
    rows, depth = tokens[0].shape
    sources, stream_rows, cols = streams[1].shape
    all_rows = rows * len(tokens)
    return pl.pallas_call(
        functools.partial(gate_up_kernel, len(tokens)),
        in_specs=[ANY] * (len(tokens) + len(streams)) + [VMEM] * len(earlier),
        out_specs=VMEM,
        out_shape=jax.ShapeDtypeStruct((2, all_rows, cols), jnp.bfloat16),
        scratch_shapes=[
            pltpu.VMEM((all_rows, depth), jnp.bfloat16),
            pltpu.VMEM((2, sources, PARTS, stream_rows, cols), jnp.bfloat16),
            pltpu.SemaphoreType.DMA((len(tokens),)),
            pltpu.SemaphoreType.DMA((2, PARTS)),
        ],
        compiler_params=pltpu.CompilerParams(vmem_limit_bytes=VMEM_LIMIT),
        cost_estimate=BRIEF,
        name="gate_up",
    )(*tokens, *streams, *earlier)


def activation_kernel(here_ref, there_ref, out_ref):
    gate = here_ref[0].astype(jnp.float32) + there_ref[0].astype(jnp.float32)
    up = here_ref[1].astype(jnp.float32) + there_ref[1].astype(jnp.float32)
    out_ref[...] = (gate / (1.0 + jnp.exp(-gate)) * up).astype(jnp.bfloat16)


def activation(here, there, part, parts):
    _, rows, cols = here.shape
    rows = rows // parts
    step = min(rows, ROW_TILE)
    first = part * rows // step
    return pl.pallas_call(
        activation_kernel,
        grid=(rows // step,),
        in_specs=[pl.BlockSpec((2, step, cols), lambda t: (0, first + t, 0))] * 2,
        out_specs=pl.BlockSpec((step, cols), lambda t: (t, 0)),
        out_shape=jax.ShapeDtypeStruct((rows, cols), jnp.bfloat16),
        compiler_params=pltpu.CompilerParams(vmem_limit_bytes=VMEM_LIMIT),
        cost_estimate=BRIEF,
        name="activation",
    )(here, there)


def down_kernel(activated_ref, weights_ref, out_ref):
    sources, _, _, cols = weights_ref.shape
    if cols % HEAD_WIDTH:
        blocks = [weights_ref[s, 0] for s in range(sources)]
    else:
        blocks = [jnp.concatenate([weights_ref[s, 0] for s in range(sources)], axis=1)]
    for s, block in enumerate(blocks):
        product = jnp.dot(activated_ref[...], block, preferred_element_type=jnp.float32)
        out_ref[:, s * block.shape[1] : (s + 1) * block.shape[1]] = product.astype(jnp.bfloat16)


def down_product(activated, weights, part):
    sources, _, depth, cols = weights.shape
    out = (activated.shape[0], sources * cols)
    return pl.pallas_call(
        down_kernel,
        grid=(1,),
        in_specs=[
            pl.BlockSpec(activated.shape, lambda t: (0, 0)),
            pl.BlockSpec((sources, 1, depth, cols), lambda t: (0, part, 0, 0)),
        ],
        out_specs=pl.BlockSpec(out, lambda t: (0, 0)),
        out_shape=jax.ShapeDtypeStruct(out, jnp.bfloat16),
        compiler_params=pltpu.CompilerParams(vmem_limit_bytes=VMEM_LIMIT),
        cost_estimate=BRIEF,
        name="down",
    )(activated, weights)


def per_device(query, key, value, doc_lengths, resid, norm_gain, w_out, w_gate_up, w_down):
    inner_count = lax.axis_size("inner")
    outer_count = lax.axis_size("outer")
    head_count = lax.axis_size("head")
    outer, inner, head = lax.axis_index("outer"), lax.axis_index("inner"), lax.axis_index("head")
    rows = query.shape[0]
    plane_rows = rows * inner_count * head_count
    reach = plane_rows * outer_count // WINDOW_PER_DOC
    feature_rows = w_gate_up.shape[1]
    hidden_cols = w_gate_up.shape[2] // outer_count
    bounds = jnp.cumsum(doc_lengths)
    hops = reach // plane_rows
    token_rows = plane_rows // inner_count
    half = plane_rows // head_count
    packing = (rows, head_count, KEY_VALUE_HEADS // head_count, -1)

    weights_out = lax.all_gather(w_out, "outer", axis=1, tiled=True)
    if packing[2] == inner_count and hops == 1:
        earlier = [lax.ppermute(part, "outer", [(s, s + 1) for s in range(outer_count - 1)]) for part in (key, value)]
        groups = jnp.concatenate([part.reshape(packing) for part in (query, key, value, *earlier)], axis=3)
        groups = jnp.transpose(groups, (2, 1, 0, 3)).reshape(inner_count * head_count, rows, -1)
        packed = lax.all_to_all(groups, ("inner", "head"), split_axis=0, concat_axis=0, tiled=True)
        packed = packed.reshape(plane_rows, -1)
        starts = document_starts(bounds, outer * plane_rows, plane_rows)
        own_context = attention(packed, packed, Q_COLS // KV_COLS + 1, starts, reach)
        blocks = blocks_over_inner(own_context)
    else:
        groups = jnp.concatenate([part.reshape(packing) for part in (query, key, value)], axis=3)
        groups = jnp.transpose(groups[:, :, 0], (1, 0, 2))
        packed = lax.all_to_all(groups, "head", split_axis=0, concat_axis=0, tiled=True).reshape(token_rows, -1)
        plane_kv = lax.all_gather(packed[:, Q_COLS:], "inner", axis=0, tiled=True)
        every_kv = jnp.concatenate([earlier_planes(plane_kv, hops), plane_kv], axis=0)
        halo = lax.dynamic_slice_in_dim(every_kv, inner * token_rows, reach, 0)
        starts = document_starts(bounds, outer * plane_rows + inner * token_rows, token_rows)
        own_context = attention(packed, halo, 0, starts, reach)
        blocks = [lax.all_gather(own_context, "inner", axis=0, tiled=True)]

    spread = functools.partial(lax.all_to_all, axis_name="outer", split_axis=0, concat_axis=0, tiled=True)
    over_y = functools.partial(swap, axis="inner", distance=2)
    fence = lambda *arrays: lax.optimization_barrier(arrays)
    own_gain = lax.dynamic_slice_in_dim(norm_gain, outer * feature_rows, feature_rows, 0)
    cut = cut_weights(w_gate_up, w_down, own_gain[:, None], outer_count)

    place = jnp.stack([inner, head]).astype(jnp.int32)
    weights_out, *blocks = fence(weights_out, *blocks)
    first = spread(after(cut[0], weights_out))
    kept, sent, *whole = projection(blocks, weights_out, place, head_count, inner_count)
    context = whole[0] if whole else own_context
    projected = kept.astype(jnp.float32)
    for e in range(1, head_count):
        projected = projected + swap(sent[e - 1], "head", e).astype(jnp.float32)
    own_resid = lax.dynamic_slice_in_dim(resid, head * half, half, 0)
    hidden_part = (own_resid.astype(jnp.float32) + projected).astype(jnp.bfloat16)

    upper = inner // 2
    own_rows = half // 2
    mine = lax.dynamic_slice_in_dim(hidden_part, upper * own_rows, own_rows, 0)
    others = lax.dynamic_slice_in_dim(hidden_part, (1 - upper) * own_rows, own_rows, 0)
    others, first = fence(over_y(others), first)
    state = [mine.astype(jnp.float32), others.astype(jnp.float32)]
    squares = sum([jnp.sum(block * block, axis=1) for block in state])
    squares = squares + swap(squares, "inner", 1)
    inverse = lax.rsqrt(squares / D + 1e-05)[:, None]
    part_rows = feature_rows // PARTS
    normed = jnp.concatenate([block * inverse for block in state], axis=1).astype(jnp.bfloat16)
    state = [block.reshape(own_rows, outer_count, PARTS, part_rows) for block in state]
    state = [[block[:, :, part].reshape(own_rows, -1) for part in range(PARTS)] for block in state]

    tokens = lax.all_gather(normed, "outer", axis=0, tiled=True)
    second, first_y, tokens, state = fence(spread(after(cut[1], normed)), over_y(first), tokens, state)
    tokens = jnp.split(tokens, 2, axis=1)
    tokens = [[swap(block, "head", e) if e else block for e in range(head_count)] for block in tokens]
    third, second_y, tokens[0] = fence(spread(after(cut[2], second)), over_y(second), tokens[0])
    own_sums = gate_up(tokens[0], [first, second, third])
    fourth = spread(after(cut[3], third))
    third_y, own_sums = fence(over_y(third), own_sums)
    sums = gate_up(tokens[1], [first_y, second_y, third_y], [own_sums])
    fourth, other_sums = fence(fourth, swap(sums, "inner", 1))
    fourth_y = [over_y(fourth[:, part : part + 1]) for part in range(PARTS)]
    activated = [activation(sums, other_sums, e, head_count) for e in range(1, head_count)]
    sent = [[down_product(rows_of, fourth, part) for rows_of in activated] for part in range(PARTS)]
    activated = [activation(after(sums, sent[-1][-1]), other_sums, 0, head_count), *activated]

    def over_heads(weights, part, sent=None):
        if sent is None:
            sent = [down_product(rows_of, weights, part) for rows_of in activated[1:]]
        moved = [swap(rows_of, "head", e) for e, rows_of in enumerate(sent, 1)]
        total = down_product(activated[0], weights, part).astype(jnp.float32)
        for rows_of in moved:
            total = total + rows_of.astype(jnp.float32)
        return total.reshape(outer_count, own_rows, -1)

    paired = {(0, part): over_heads(fourth, part, sent[part]) for part in range(PARTS)}
    for part in range(PARTS):
        paired[1, part] = over_heads(after(fourth_y[part], paired[0, part]), 0)

    pieces = [[None] * PARTS, [None] * PARTS]
    for part in range(PARTS):
        for a in range(2):
            total = state[a][part] + jnp.sum(spread(paired[a, part].astype(jnp.bfloat16)).astype(jnp.float32), axis=0)
            total = total.astype(jnp.bfloat16)
            pieces[a][part] = (over_y(total) if a else total).reshape(own_rows, outer_count, 1, part_rows)
    halves = [jnp.concatenate(parts, axis=2).reshape(own_rows, -1) for parts in pieces]
    layer_out = jnp.zeros((half, halves[0].shape[1]), jnp.bfloat16)
    layer_out = lax.dynamic_update_slice(layer_out, halves[0], (upper * own_rows, 0))
    layer_out = lax.dynamic_update_slice(layer_out, halves[1], ((1 - upper) * own_rows, 0))
    return (context, layer_out)


def solution(mesh):
    placed = (
        P(("outer", "inner", "head"), None),
        P(("outer", "inner", "head"), None),
        P(("outer", "inner", "head"), None),
        P(),
        P("outer", "inner"),
        P("inner"),
        P("head", ("inner", "outer")),
        P(None, ("inner", "outer"), "head"),
        P("head", ("inner", "outer")),
    )
    return jax.shard_map(
        per_device,
        mesh=mesh,
        in_specs=placed,
        out_specs=(P(("outer", "inner"), "head"), P(("outer", "head"), "inner")),
        check_vma=False,
    )
```

```python
import functools

import jax
import jax.numpy as jnp
from jax import lax
from jax.experimental import pallas as pl
from jax.experimental.pallas import tpu as pltpu
from jax.sharding import PartitionSpec as P

D = 4096
QUERY_HEADS = 32
KEY_VALUE_HEADS = 8
HEAD_WIDTH = 128
GROUP = QUERY_HEADS // KEY_VALUE_HEADS
Q_COLS = GROUP * HEAD_WIDTH
KV_COLS = 2 * HEAD_WIDTH
WINDOW_PER_DOC = 4
QUERY_TILE = 128
ROW_TILE = 256
PARTS = 2
VMEM_LIMIT = 48 * 1024 * 1024
BRIEF = pl.CostEstimate(flops=1, bytes_accessed=1, transcendentals=0)
ANY = pl.BlockSpec(memory_space=pl.ANY)
VMEM = pl.BlockSpec(memory_space=pltpu.VMEM)
SMEM = pl.BlockSpec(memory_space=pltpu.SMEM)


def swap(array, axis, distance):
    if distance == 0:
        return array
    count = lax.axis_size(axis)
    return lax.ppermute(array, axis, [(s, s ^ distance) for s in range(count)])


def after(array, earlier):
    return lax.optimization_barrier((array, earlier))[0]


def blocks_over_inner(block):
    across = swap(block, "inner", 2)
    return [block, swap(block, "inner", 1), across, swap(across, "inner", 1)]


def earlier_planes(kv, hops):
    count = lax.axis_size("outer")
    moved = [lax.ppermute(kv, "outer", [(s, s + d) for s in range(count - d)]) for d in range(hops, 0, -1)]
    return jnp.concatenate(moved, axis=0)


def document_starts(bounds, first, rows):
    place = first + jnp.arange(rows, dtype=jnp.int32)
    starts = jnp.max(jnp.where(bounds[None, :] <= place[:, None], bounds[None, :], 0), axis=1) - first
    return starts[:, None].astype(jnp.int32)


def row_tiles(rows):
    step = ROW_TILE if rows % ROW_TILE == 0 else rows
    return [slice(at, at + step) for at in range(0, rows, step)]


def attention_kernel(halo_rows, reach, starts_ref, queries_ref, own_ref, halo_ref, out_ref, keys, values):
    tile = pl.program_id(0)
    rows = queries_ref.shape[0]
    span = reach + rows

    @pl.when(tile == 0)
    def _():
        keys[:halo_rows, :] = halo_ref[:, :HEAD_WIDTH]
        values[:halo_rows, :] = halo_ref[:, HEAD_WIDTH:]
        keys[halo_rows:, :] = own_ref[:, :HEAD_WIDTH]
        values[halo_rows:, :] = own_ref[:, HEAD_WIDTH:]

    first = pl.multiple_of(tile * rows + (halo_rows - reach), rows)
    near_keys = keys[pl.ds(first, span), :]
    near_values = values[pl.ds(first, span), :]
    key_place = lax.broadcasted_iota(jnp.int32, (rows, span), 1)
    query_place = lax.broadcasted_iota(jnp.int32, (rows, span), 0) + reach
    start = starts_ref[...] - (first - halo_rows)
    allowed = (key_place <= query_place) & (key_place >= start)
    for g in range(GROUP):
        cols = slice(g * HEAD_WIDTH, (g + 1) * HEAD_WIDTH)
        scores = lax.dot_general(
            queries_ref[:, cols], near_keys, (((1,), (1,)), ((), ())), preferred_element_type=jnp.float32
        ) * (HEAD_WIDTH ** (-0.5))
        masked = jnp.where(allowed, scores, -1e30)
        row_max = jnp.max(masked, axis=1, keepdims=True)
        weights = jnp.exp(masked - row_max)
        totals = jnp.sum(weights, axis=1, keepdims=True)
        summed = jnp.dot(weights.astype(jnp.bfloat16), near_values, preferred_element_type=jnp.float32)
        out_ref[:, cols] = (summed / totals).astype(jnp.bfloat16)


def attention(packed, halo, halo_at, starts, reach):
    rows = packed.shape[0]
    halo_rows = halo.shape[0]
    return pl.pallas_call(
        functools.partial(attention_kernel, halo_rows, reach),
        grid=(rows // QUERY_TILE,),
        in_specs=[
            pl.BlockSpec((QUERY_TILE, 1), lambda t: (t, 0)),
            pl.BlockSpec((QUERY_TILE, Q_COLS), lambda t: (t, 0)),
            pl.BlockSpec((rows, KV_COLS), lambda t: (0, Q_COLS // KV_COLS)),
            pl.BlockSpec((halo_rows, KV_COLS), lambda t: (0, halo_at)),
        ],
        out_specs=pl.BlockSpec((QUERY_TILE, Q_COLS), lambda t: (t, 0)),
        out_shape=jax.ShapeDtypeStruct((rows, Q_COLS), jnp.bfloat16),
        scratch_shapes=[
            pltpu.VMEM((halo_rows + rows, HEAD_WIDTH), jnp.bfloat16),
            pltpu.VMEM((halo_rows + rows, HEAD_WIDTH), jnp.bfloat16),
        ],
        compiler_params=pltpu.CompilerParams(vmem_limit_bytes=VMEM_LIMIT),
        cost_estimate=BRIEF,
        name="attention",
    )(starts, packed, packed, halo)


def cut_kernel(gain_ref, gate_up_ref, down_ref, both_ref, gate_ref, up_ref, *down_refs):
    rows, cols = gate_ref.shape[1], down_refs[0].shape[2]
    for which, second_ref in enumerate((gate_ref, up_ref)):
        scaled = (gate_up_ref[which].astype(jnp.float32) * gain_ref[...]).astype(jnp.bfloat16)
        both_ref[0, which] = scaled[:rows]
        second_ref[0] = scaled[rows:]
    for part, out_ref in enumerate(down_refs):
        out_ref[0] = down_ref[:, part * cols : (part + 1) * cols]


def cut_weights(w_gate_up, w_down, gain, outer_count):
    _, features, width = w_gate_up.shape
    cols = width // outer_count
    rows = features // PARTS
    if cols % HEAD_WIDTH:
        wide = (w_gate_up.astype(jnp.float32) * gain[None]).astype(jnp.bfloat16)
        wide = jnp.transpose(wide.reshape(2, PARTS, rows, outer_count, cols), (1, 3, 0, 2, 4))
        tall = jnp.transpose(w_down.reshape(outer_count, cols, PARTS, rows), (2, 0, 1, 3))
        return [wide[0], wide[1, :, 0], wide[1, :, 1], *tall]
    return pl.pallas_call(
        cut_kernel,
        grid=(outer_count,),
        in_specs=[
            pl.BlockSpec((features, 1), lambda p: (0, 0)),
            pl.BlockSpec((2, features, cols), lambda p: (0, 0, p)),
            pl.BlockSpec((cols, features), lambda p: (p, 0)),
        ],
        out_specs=[pl.BlockSpec((1, 2, rows, cols), lambda p: (p, 0, 0, 0))]
        + [pl.BlockSpec((1, rows, cols), lambda p: (p, 0, 0))] * 2
        + [pl.BlockSpec((1, cols, rows), lambda p: (p, 0, 0))] * PARTS,
        out_shape=[jax.ShapeDtypeStruct((outer_count, 2, rows, cols), jnp.bfloat16)]
        + [jax.ShapeDtypeStruct((outer_count, rows, cols), jnp.bfloat16)] * 2
        + [jax.ShapeDtypeStruct((outer_count, cols, rows), jnp.bfloat16)] * PARTS,
        compiler_params=pltpu.CompilerParams(vmem_limit_bytes=VMEM_LIMIT),
        cost_estimate=BRIEF,
        name="cut_weights",
    )(gain, w_gate_up, w_down)


def projection_kernel(block_count, place_ref, *refs):
    blocks, weights_ref = refs[:block_count], refs[block_count]
    kept_ref, sent_ref = refs[block_count + 1 : block_count + 3]
    inner, head = place_ref[0], place_ref[1]
    half, depth = kept_ref.shape[0], blocks[0].shape[1]
    for e in range(sent_ref.shape[0] + 1):
        rows = pl.ds(pl.multiple_of((head ^ e) * half, half), half)
        total = jnp.zeros(kept_ref.shape, jnp.float32)
        for a, block in enumerate(blocks):
            at = pl.ds(pl.multiple_of((inner ^ a) * depth, depth), depth) if block_count > 1 else slice(None)
            total = total + jnp.dot(block[rows, :], weights_ref[at, :], preferred_element_type=jnp.float32)
        if e == 0:
            kept_ref[...] = total.astype(jnp.bfloat16)
        else:
            sent_ref[e - 1] = total.astype(jnp.bfloat16)
    if block_count > 1:
        context_ref = refs[block_count + 3]
        tokens = context_ref.shape[0]
        own = pl.ds(pl.multiple_of(inner * tokens, tokens), tokens)
        for a, block in enumerate(blocks):
            context_ref[:, pl.ds(pl.multiple_of((inner ^ a) * depth, depth), depth)] = block[own, :]


def projection(blocks, weights, place, head_count, inner_count):
    rows, depth = blocks[0].shape
    half, width = rows // head_count, weights.shape[1]
    outs = [(half, width), (head_count - 1, half, width)]
    if len(blocks) > 1:
        outs.append((rows // inner_count, len(blocks) * depth))
    return pl.pallas_call(
        functools.partial(projection_kernel, len(blocks)),
        in_specs=[SMEM] + [VMEM] * (len(blocks) + 1),
        out_specs=[VMEM] * len(outs),
        out_shape=[jax.ShapeDtypeStruct(shape, jnp.bfloat16) for shape in outs],
        compiler_params=pltpu.CompilerParams(vmem_limit_bytes=VMEM_LIMIT),
        cost_estimate=BRIEF,
        name="projection",
    )(place, *blocks, weights)


def gate_up_kernel(head_count, *refs):
    tokens = refs[:head_count]
    both, gate, up = refs[head_count : head_count + 3]
    *earlier, out_ref, held, near, token_sems, weight_sems = refs[head_count + 3 :]
    rows, depth = tokens[0].shape
    copies = [
        [pltpu.make_async_copy(both.at[:, which], near.at[which, :, 0], weight_sems.at[which, 0]),
         pltpu.make_async_copy(second, near.at[which, :, 1], weight_sems.at[which, 1])]
        for which, second in enumerate((gate, up))
    ]
    for e, token_ref in enumerate(tokens):
        copies[0].append(pltpu.make_async_copy(token_ref, held.at[pl.ds(e * rows, rows)], token_sems.at[e]))
    for group in copies:
        for copy in group:
            copy.start()
    for which, group in enumerate(copies):
        for copy in group:
            copy.wait()
        block = near[which].reshape(depth, -1)
        for tile in row_tiles(held.shape[0]):
            product = jnp.dot(held[tile, :], block, preferred_element_type=jnp.float32)
            if earlier:
                product = earlier[0][which, tile, :].astype(jnp.float32) + product
            out_ref[which, tile, :] = product.astype(jnp.bfloat16)


def gate_up(tokens, streams, earlier=()):
    rows, depth = tokens[0].shape
    sources, stream_rows, cols = streams[1].shape
    all_rows = rows * len(tokens)
    return pl.pallas_call(
        functools.partial(gate_up_kernel, len(tokens)),
        in_specs=[ANY] * (len(tokens) + len(streams)) + [VMEM] * len(earlier),
        out_specs=VMEM,
        out_shape=jax.ShapeDtypeStruct((2, all_rows, cols), jnp.bfloat16),
        scratch_shapes=[
            pltpu.VMEM((all_rows, depth), jnp.bfloat16),
            pltpu.VMEM((2, sources, PARTS, stream_rows, cols), jnp.bfloat16),
            pltpu.SemaphoreType.DMA((len(tokens),)),
            pltpu.SemaphoreType.DMA((2, PARTS)),
        ],
        compiler_params=pltpu.CompilerParams(vmem_limit_bytes=VMEM_LIMIT),
        cost_estimate=BRIEF,
        name="gate_up",
    )(*tokens, *streams, *earlier)


def activation_kernel(here_ref, there_ref, out_ref):
    gate = here_ref[0].astype(jnp.float32) + there_ref[0].astype(jnp.float32)
    up = here_ref[1].astype(jnp.float32) + there_ref[1].astype(jnp.float32)
    out_ref[...] = (gate / (1.0 + jnp.exp(-gate)) * up).astype(jnp.bfloat16)


def activation(here, there, part, parts):
    _, rows, cols = here.shape
    rows = rows // parts
    step = min(rows, ROW_TILE)
    first = part * rows // step
    return pl.pallas_call(
        activation_kernel,
        grid=(rows // step,),
        in_specs=[pl.BlockSpec((2, step, cols), lambda t: (0, first + t, 0))] * 2,
        out_specs=pl.BlockSpec((step, cols), lambda t: (t, 0)),
        out_shape=jax.ShapeDtypeStruct((rows, cols), jnp.bfloat16),
        compiler_params=pltpu.CompilerParams(vmem_limit_bytes=VMEM_LIMIT),
        cost_estimate=BRIEF,
        name="activation",
    )(here, there)


def down_kernel(activated_ref, weights_ref, out_ref):
    sources, _, cols = weights_ref.shape
    if cols % HEAD_WIDTH:
        blocks = [weights_ref[s] for s in range(sources)]
    else:
        blocks = [jnp.concatenate([weights_ref[s] for s in range(sources)], axis=1)]
    for s, block in enumerate(blocks):
        product = jnp.dot(activated_ref[...], block, preferred_element_type=jnp.float32)
        out_ref[:, s * block.shape[1] : (s + 1) * block.shape[1]] = product.astype(jnp.bfloat16)


def down_product(activated, weights):
    sources, _, cols = weights.shape
    return pl.pallas_call(
        down_kernel,
        in_specs=[VMEM, VMEM],
        out_specs=VMEM,
        out_shape=jax.ShapeDtypeStruct((activated.shape[0], sources * cols), jnp.bfloat16),
        compiler_params=pltpu.CompilerParams(vmem_limit_bytes=VMEM_LIMIT),
        cost_estimate=BRIEF,
        name="down",
    )(activated, weights)


def per_device(query, key, value, doc_lengths, resid, norm_gain, w_out, w_gate_up, w_down):
    inner_count = lax.axis_size("inner")
    outer_count = lax.axis_size("outer")
    head_count = lax.axis_size("head")
    outer, inner, head = lax.axis_index("outer"), lax.axis_index("inner"), lax.axis_index("head")
    rows = query.shape[0]
    plane_rows = rows * inner_count * head_count
    reach = plane_rows * outer_count // WINDOW_PER_DOC
    feature_rows = w_gate_up.shape[1]
    hidden_cols = w_gate_up.shape[2] // outer_count
    bounds = jnp.cumsum(doc_lengths)
    hops = reach // plane_rows
    token_rows = plane_rows // inner_count
    half = plane_rows // head_count
    packing = (rows, head_count, KEY_VALUE_HEADS // head_count, -1)

    weights_out = lax.all_gather(w_out, "outer", axis=1, tiled=True)
    if packing[2] == inner_count and hops == 1:
        earlier = [lax.ppermute(part, "outer", [(s, s + 1) for s in range(outer_count - 1)]) for part in (key, value)]
        groups = jnp.concatenate([part.reshape(packing) for part in (query, key, value, *earlier)], axis=3)
        groups = jnp.transpose(groups, (2, 1, 0, 3)).reshape(inner_count * head_count, rows, -1)
        packed = lax.all_to_all(groups, ("inner", "head"), split_axis=0, concat_axis=0, tiled=True)
        packed = packed.reshape(plane_rows, -1)
        starts = document_starts(bounds, outer * plane_rows, plane_rows)
        own_context = attention(packed, packed, Q_COLS // KV_COLS + 1, starts, reach)
        blocks = blocks_over_inner(own_context)
    else:
        groups = jnp.concatenate([part.reshape(packing) for part in (query, key, value)], axis=3)
        groups = jnp.transpose(groups[:, :, 0], (1, 0, 2))
        packed = lax.all_to_all(groups, "head", split_axis=0, concat_axis=0, tiled=True).reshape(token_rows, -1)
        plane_kv = lax.all_gather(packed[:, Q_COLS:], "inner", axis=0, tiled=True)
        every_kv = jnp.concatenate([earlier_planes(plane_kv, hops), plane_kv], axis=0)
        halo = lax.dynamic_slice_in_dim(every_kv, inner * token_rows, reach, 0)
        starts = document_starts(bounds, outer * plane_rows + inner * token_rows, token_rows)
        own_context = attention(packed, halo, 0, starts, reach)
        blocks = [lax.all_gather(own_context, "inner", axis=0, tiled=True)]

    spread = functools.partial(lax.all_to_all, axis_name="outer", split_axis=0, concat_axis=0, tiled=True)
    over_y = functools.partial(swap, axis="inner", distance=2)
    fence = lambda *arrays: lax.optimization_barrier(arrays)
    own_gain = lax.dynamic_slice_in_dim(norm_gain, outer * feature_rows, feature_rows, 0)
    cut = cut_weights(w_gate_up, w_down, own_gain[:, None], outer_count)

    place = jnp.stack([inner, head]).astype(jnp.int32)
    weights_out, *blocks = fence(weights_out, *blocks)
    first = spread(after(cut[0], weights_out))
    kept, sent, *whole = projection(blocks, weights_out, place, head_count, inner_count)
    context = whole[0] if whole else own_context
    projected = kept.astype(jnp.float32)
    for e in range(1, head_count):
        projected = projected + swap(sent[e - 1], "head", e).astype(jnp.float32)
    own_resid = lax.dynamic_slice_in_dim(resid, head * half, half, 0)
    hidden_part = (own_resid.astype(jnp.float32) + projected).astype(jnp.bfloat16)

    upper = inner // 2
    own_rows = half // 2
    mine = lax.dynamic_slice_in_dim(hidden_part, upper * own_rows, own_rows, 0)
    others = lax.dynamic_slice_in_dim(hidden_part, (1 - upper) * own_rows, own_rows, 0)
    state = [mine.astype(jnp.float32), over_y(others).astype(jnp.float32)]
    squares = sum([jnp.sum(block * block, axis=1) for block in state])
    squares = squares + swap(squares, "inner", 1)
    inverse = lax.rsqrt(squares / D + 1e-05)[:, None]
    part_rows = feature_rows // PARTS
    normed = jnp.concatenate([block * inverse for block in state], axis=1).astype(jnp.bfloat16)
    normed, first = fence(normed, first)
    state = [block.reshape(own_rows, outer_count, PARTS, part_rows) for block in state]
    state = [[block[:, :, part].reshape(own_rows, -1) for part in range(PARTS)] for block in state]

    tokens = lax.all_gather(normed, "outer", axis=0, tiled=True)
    second, first_y, tokens, state = fence(spread(after(cut[1], normed)), over_y(first), tokens, state)
    tokens = jnp.split(tokens, 2, axis=1)
    tokens = [[swap(block, "head", e) if e else block for e in range(head_count)] for block in tokens]
    third, second_y, tokens[0] = fence(spread(after(cut[2], second)), over_y(second), tokens[0])
    own_sums = gate_up(tokens[0], [first, second, third])
    fourth, third_y, own_sums = fence(spread(after(cut[3], third)), over_y(third), own_sums)
    sums = gate_up(tokens[1], [first_y, second_y, third_y], [own_sums])
    other_sums = swap(sums, "inner", 1)
    activated = [activation(sums, other_sums, e, head_count) for e in range(1, head_count)]
    sent = [down_product(rows_of, fourth) for rows_of in activated]
    activated = [activation(after(sums, sent[-1]), other_sums, 0, head_count), *activated]

    def over_heads(weights, moved=None):
        if moved is None:
            sent = [down_product(rows_of, weights) for rows_of in activated[1:]]
            moved = [swap(rows_of, "head", e) for e, rows_of in enumerate(sent, 1)]
        total = down_product(activated[0], weights).astype(jnp.float32)
        for rows_of in moved:
            total = total + rows_of.astype(jnp.float32)
        return total.reshape(outer_count, own_rows, -1)

    moved = [[swap(piece, "head", e) for piece in jnp.split(rows_of, 2)] for e, rows_of in enumerate(sent, 1)]
    fifth, fourth_y, moved[0][0] = fence(spread(after(cut[4], fourth)), over_y(fourth), moved[0][0])
    fifth_y = over_y(fifth)
    paired = {(0, 0): over_heads(fourth, [jnp.concatenate(pieces) for pieces in moved])}
    paired[1, 0] = over_heads(fourth_y)
    paired[0, 1] = over_heads(fifth)
    paired[1, 1] = over_heads(after(fifth_y, paired[0, 0]))

    pieces = [[None] * PARTS, [None] * PARTS]
    for part in range(PARTS):
        for a in range(2):
            total = state[a][part] + lax.dynamic_index_in_dim(paired[a, part], outer, 0, False)
            for d in range(1, outer_count):
                sent = lax.dynamic_index_in_dim(paired[a, part], outer ^ d, 0, False).astype(jnp.bfloat16)
                total = total + swap(sent, "outer", d).astype(jnp.float32)
            total = total.astype(jnp.bfloat16)
            pieces[a][part] = (over_y(total) if a else total).reshape(own_rows, outer_count, 1, part_rows)
    halves = [jnp.concatenate(parts, axis=2).reshape(own_rows, -1) for parts in pieces]
    layer_out = jnp.zeros((half, halves[0].shape[1]), jnp.bfloat16)
    layer_out = lax.dynamic_update_slice(layer_out, halves[0], (upper * own_rows, 0))
    layer_out = lax.dynamic_update_slice(layer_out, halves[1], ((1 - upper) * own_rows, 0))
    return (context, layer_out)


def solution(mesh):
    placed = (
        P(("outer", "inner", "head"), None),
        P(("outer", "inner", "head"), None),
        P(("outer", "inner", "head"), None),
        P(),
        P("outer", "inner"),
        P("inner"),
        P("head", ("inner", "outer")),
        P(None, ("inner", "outer"), "head"),
        P("head", ("inner", "outer")),
    )
    return jax.shard_map(
        per_device,
        mesh=mesh,
        in_specs=placed,
        out_specs=(P(("outer", "inner"), "head"), P(("outer", "head"), "inner")),
        check_vma=False,
    )
```
